256 devices in a mesh: role: 8 (over z), seq: 32 (over x, y, core).
Axes of the slice: x: 4, y: 4, z: 8, core: 2. Of those that a mesh axis runs over, the one named last changes fastest.
Arguments:
- prefill_queries: bfloat16 [8, 4096, 8192], P('role', 'seq'), may hold values from -140 to 140
- prefill_kv: bfloat16 [8, 4096, 2048], P('role', 'seq'), may hold values from -13 to 13
- prompt_lengths: int32 [4, 4], replicated, may hold values from 1 to 2048, as said below
- decode_group: int32 [4, 4], replicated, may hold values from 0 to 3, as said below
- decode_queries: bfloat16 [8, 4, 4, 8192], P('role', None, None, 'seq'), may hold values from -140 to 140
- decode_kv: bfloat16 [8, 4, 4, 2048], P('role'), may hold values from -13 to 13
- out_weight: bfloat16 [8192, 8192], P('seq'), may hold values from -0.125 to 0.125
Outputs:
- prefill_out: bfloat16 [8, 4096, 8192], P('role', 'seq')
- decode_out: bfloat16 [4, 4, 4, 8192], replicated
The draws below stay inside these ranges and needn't reach their ends.
Inputs may be any that keep to these rules, and one draw needn't show every extreme that they name: `prompt_lengths`: in each row the block counts ceil(length / 128) sum to 32 and are at most 16; each row has a request of exactly 16 blocks whose length is 2048. `decode_group`: each row is a permutation of 0 to 3.
All inputs are finite; a program needn't handle non-finite values.
Results may differ from the reference program's by a relative error of at most 0.006.
Values may be sent and summed in bfloat16 or wider, within the bound.
A program may use at most 128 MiB of HBM per device.

```python
import jax
import jax.numpy as jnp
from jax import lax

D = 8192
H = 64
KVH = 8
HD = 128
BLOCK = 128
STEPS = 4
GROUPS = 8
PGROUPS = 4
REQS = 4
SPAN = 4096
MOSTB = 16
CAPR = 2048


def shared_pairs(key, shape):
    first_key = jax.random.fold_in(jax.random.fold_in(key, 101), 0)
    pairs = jnp.clip(jax.random.normal(first_key, shape + (2, HD), jnp.float32), -4.0, 4.0)
    pairs = pairs * jnp.array([1.0, 3.0], jnp.float32).reshape(2, 1)
    return pairs


def draw_prompt_lengths(key, part):
    key = jax.random.fold_in(key, 5)

    def one_row(row_key):
        split_keys = jax.random.split(row_key, 3)
        remaining = SPAN // BLOCK - MOSTB
        cuts = jnp.sort(jax.random.permutation(split_keys[0], remaining - 1)[:REQS - 2] + 1).astype(jnp.int32)
        edges = jnp.concatenate([jnp.zeros((1,), jnp.int32), cuts, jnp.full((1,), remaining, jnp.int32)])
        counts = jnp.concatenate([jnp.full((1,), MOSTB, jnp.int32), edges[1:] - edges[:-1]])
        tails = jax.random.randint(split_keys[1], (REQS,), 1, BLOCK + 1).astype(jnp.int32)
        tails = jnp.where(jnp.arange(REQS) == 0, BLOCK, tails)
        lengths = (counts - 1) * BLOCK + tails
        return lengths[jax.random.permutation(split_keys[2], REQS)]
    return jax.vmap(one_row)(jax.random.split(key, PGROUPS)).astype(jnp.int32)


def draw_decode_group(key, part):
    key = jax.random.fold_in(key, 23)
    return jax.vmap(lambda row_key: jax.random.permutation(row_key, PGROUPS))(jax.random.split(key, PGROUPS)).astype(jnp.int32)


def draw_prefill_kv(key, part):
    pairs = shared_pairs(key, (GROUPS, SPAN, KVH))
    return pairs.reshape(GROUPS, SPAN, KVH * 2 * HD).astype(jnp.bfloat16)


def draw_prefill_queries(key, part):
    key = jax.random.fold_in(key, 3)
    queries = 2.0 * jnp.clip(jax.random.normal(key, (GROUPS, SPAN, KVH, H // KVH, HD), jnp.float32), -4.0, 4.0)
    return queries.reshape(GROUPS, SPAN, H * HD).astype(jnp.bfloat16)


def draw_decode_kv(key, part):
    pairs = shared_pairs(key, (GROUPS, STEPS, PGROUPS, KVH))
    return pairs.reshape(GROUPS, STEPS, PGROUPS, KVH * 2 * HD).astype(jnp.bfloat16)


def draw_decode_queries(key, part):
    key = jax.random.fold_in(key, 17)
    queries = 2.0 * jnp.clip(jax.random.normal(key, (GROUPS, STEPS, PGROUPS, KVH, H // KVH, HD), jnp.float32), -4.0, 4.0)
    return queries.reshape(GROUPS, STEPS, PGROUPS, H * HD).astype(jnp.bfloat16)


def block_scale(stream_key, extent, pieces, smallest, high):
    def one(dim, shards_of):
        heights = jax.random.uniform(jax.random.fold_in(jax.random.fold_in(stream_key, 6), dim), (shards_of,), jnp.float32, smallest / len(pieces), high / len(pieces))
        return jnp.repeat(jnp.exp(heights), extent[dim] // shards_of).reshape((-1,) + (1,) * (len(extent) - dim - 1))

    level = one(*pieces[0])
    for cut in pieces[1:]:
        level = level * one(*cut)
    return level


def noise(own_key, dims, deviation, bound, shards=(), kind=jnp.bfloat16):
    drawn = jax.random.normal(own_key, dims, jnp.float32) * deviation
    if len(shards) > 0:
        drawn = block_scale(own_key, dims, shards, -0.22, 0.18) * drawn
    return jnp.clip(drawn, min=-bound, max=bound).astype(kind)


def setup_inputs(seed: int = 0) -> dict:
    key_list = jax.random.split(jax.random.key(seed), 8)
    return {
        "prefill_queries": draw_prefill_queries(jax.random.fold_in(key_list[7], 71), 0),
        "prefill_kv": draw_prefill_kv(jax.random.fold_in(key_list[7], 71), 0),
        "prompt_lengths": draw_prompt_lengths(jax.random.fold_in(key_list[7], 71), 0),
        "decode_group": draw_decode_group(jax.random.fold_in(key_list[7], 71), 0),
        "decode_queries": draw_decode_queries(jax.random.fold_in(key_list[7], 71), 0),
        "decode_kv": draw_decode_kv(jax.random.fold_in(key_list[7], 71), 0),
        "out_weight": noise(key_list[6], (H * HD, D), (H * HD // 4) ** -0.5, 0.125, ((0, 32),)),
    }


def request_layout(lengths, span_rows):
    blocks = (lengths + BLOCK - 1) // BLOCK
    starts = ((jnp.cumsum(blocks) - blocks) * BLOCK).astype(jnp.int32)
    position = jnp.arange(span_rows, dtype=jnp.int32)
    member = starts[None, :] <= position[:, None]
    segment = (jnp.sum(member.astype(jnp.int32), axis=1) - 1).astype(jnp.int32)
    owning = segment[:, None] == jnp.arange(lengths.shape[0], dtype=jnp.int32)[None, :]
    opening = jnp.sum(jnp.where(owning, starts[None, :], 0), axis=1).astype(jnp.int32)
    ceiling = jnp.sum(jnp.where(owning, lengths[None, :], 0), axis=1).astype(jnp.int32)
    return segment, position - opening < ceiling, starts


def prefill_group(queries, cached, lengths):
    segment, live_rows, starts = request_layout(lengths, SPAN)
    position = jnp.arange(SPAN, dtype=jnp.int32)
    allowed = (segment[:, None] == segment[None, :]) & (position[None, :] <= position[:, None]) & live_rows[None, :]
    grouped = H // KVH
    query_heads = queries.reshape(SPAN, H, HD)
    cache_heads = cached.reshape(SPAN, KVH, 2, HD)

    def one_head(head_index):
        query_rows = query_heads[:, head_index]
        key_value = cache_heads[:, head_index // grouped]
        scores = jnp.dot(query_rows, key_value[:, 0].T, preferred_element_type=jnp.float32) * HD ** -0.5
        scores = jnp.where(allowed, scores, -jnp.inf)
        weights = jnp.exp(scores - jnp.max(scores, axis=1, keepdims=True))
        weights = (weights / jnp.sum(weights, axis=1, keepdims=True)).astype(jnp.bfloat16)
        mixed_rows = jnp.dot(weights, key_value[:, 1], preferred_element_type=jnp.float32)
        return jnp.where(live_rows[:, None], mixed_rows, 0.0).astype(jnp.bfloat16)

    heads = lax.map(one_head, jnp.arange(H, dtype=jnp.int32))
    return jnp.transpose(heads, (1, 0, 2)).reshape(SPAN, H * HD)


def decode_pair(pair, prefill_kv, prompt_lengths, decode_group, decode_queries, decode_kv, out_weight):
    target = (pair // PGROUPS).astype(jnp.int32)
    source = (pair % PGROUPS).astype(jnp.int32)
    lengths = prompt_lengths[source]
    matched = decode_group[source] == target
    position_in = jnp.sum(jnp.where(matched, jnp.arange(REQS, dtype=jnp.int32), 0)).astype(jnp.int32)
    length_in = jnp.sum(jnp.where(matched, lengths, 0)).astype(jnp.int32)
    blocks = (lengths + BLOCK - 1) // BLOCK
    starts = ((jnp.cumsum(blocks) - blocks) * BLOCK).astype(jnp.int32)
    opening = jnp.sum(jnp.where(matched, starts, 0)).astype(jnp.int32)
    padded = jnp.concatenate([prefill_kv[source], jnp.zeros((CAPR, KVH * 2 * HD), jnp.bfloat16)], axis=0)
    cache_rows = lax.dynamic_slice_in_dim(padded, opening, CAPR, 0)
    cache_rows = cache_rows.reshape(CAPR, KVH, 2, HD).astype(jnp.float32)
    live_keys = jnp.arange(CAPR, dtype=jnp.int32) < length_in
    query_rows = decode_queries[PGROUPS + target][:, source].reshape(STEPS, KVH, H // KVH, HD).astype(jnp.float32)
    arrivals = decode_kv[PGROUPS + target][:, source].reshape(STEPS, KVH, 2, HD).astype(jnp.float32)
    score_scale = HD ** -0.5
    cached_scores = jnp.einsum("skgd,ckd->kgsc", query_rows, cache_rows[:, :, 0]) * score_scale
    cached_scores = jnp.where(live_keys[None, None, None, :], cached_scores, -jnp.inf)
    causal = jnp.arange(STEPS)[None, :] <= jnp.arange(STEPS)[:, None]
    fresh_scores = jnp.einsum("skgd,tkd->kgst", query_rows, arrivals[:, :, 0]) * score_scale
    fresh_scores = jnp.where(causal, fresh_scores, -jnp.inf)
    scores = jnp.concatenate([cached_scores, fresh_scores], axis=3)
    weights = jnp.exp(scores - jnp.max(scores, axis=3, keepdims=True))
    weights = (weights / jnp.sum(weights, axis=3, keepdims=True)).astype(jnp.bfloat16)
    weights = lax.optimization_barrier(weights).astype(jnp.float32)
    mixed_heads = jnp.einsum("kgsc,ckd->skgd", weights[..., :CAPR], cache_rows[:, :, 1])
    mixed_heads = mixed_heads + jnp.einsum("kgst,tkd->skgd", weights[..., CAPR:], arrivals[:, :, 1])
    attended = mixed_heads.reshape(STEPS, H * HD).astype(jnp.bfloat16)
    return jnp.dot(attended, out_weight, preferred_element_type=jnp.float32)


def reference(prefill_queries, prefill_kv, prompt_lengths, decode_group, decode_queries, decode_kv, out_weight):
    outputs = [prefill_group(prefill_queries[group], prefill_kv[group], prompt_lengths[group]) for group in range(PGROUPS)]
    prefill_out = jnp.concatenate([jnp.stack(outputs), jnp.zeros((GROUPS - PGROUPS, SPAN, H * HD), jnp.bfloat16)], axis=0)
    results = lax.map(lambda pair: decode_pair(pair, prefill_kv, prompt_lengths, decode_group, decode_queries, decode_kv, out_weight), jnp.arange(PGROUPS * PGROUPS, dtype=jnp.int32))
    arranged = results.reshape(PGROUPS, PGROUPS, STEPS, D)
    decode_out = jnp.transpose(arranged, (2, 0, 1, 3)).astype(jnp.bfloat16)
    return prefill_out, decode_out
```

```python
import functools

import jax
import jax.numpy as jnp
from jax import lax
from jax.experimental import pallas as pl
from jax.experimental.pallas import tpu as pltpu
from jax.sharding import PartitionSpec as P

MESH = pl.DeviceIdType.MESH
H = 64
KVH = 8
HD = 128
BLOCK = 128
PG = 4
NEG = -1e30
SCALE = HD**-0.5
LOG2E = 1.4426950408889634
SLOTS = 9
HALF = KVH // 2
GROUP = H // KVH
ROWS = 512
KT = 512
WINDOW = 2048


def fused_kernel(
    lengths, serves, q_hbm, kv_hbm, dq, fresh, w_hbm, out_hbm, dec_hbm,
    qbuf, kvbuf, sbuf, sbuf1, peak0, peak1, obuf, zbuf, wbuf, qz, qd, ds, dr, cs, dz, rs_s, rs_r, fz, fo,
    slot_sem, q_sem, own_sem, out_sem, fill_sem, send_sem, din, dout, dlocal
):
    role = lax.axis_index("role")
    seq = lax.axis_index("seq")
    core = seq % 2
    chip = seq // 2
    y = chip % 4
    x = chip // 4
    home = seq // 16
    prefilling = role < PG
    factor = SCALE * LOG2E

    def plane(other):
        return (role, other)

    def line(other):
        return (other, seq)

    def remote(src, dst, send, recv, device):
        return pltpu.make_async_remote_copy(
            src_ref=src, dst_ref=dst, send_sem=send, recv_sem=recv, device_id=device, device_id_type=MESH)

    def await_bytes(ref, sem):
        pltpu.make_async_copy(ref, ref, sem).wait()

    def q_columns(half, h):
        return q_hbm.at[:, pl.ds(pl.multiple_of((half * 32 + h) * HD, HD), HD)]

    def kv_columns(half, j):
        return kv_hbm.at[:, pl.ds(pl.multiple_of(half * HALF * 256 + j * 256, 256), 256)]

    def chunk(slot, j):
        return kvbuf.at[j, pl.ds(pl.multiple_of((8 - slot) * 256, 256), 256), :]

    def own_rows(j):
        return kvbuf.at[j, pl.ds(pl.multiple_of(2048 + core * 128, 128), 128), :]

    barrier = pltpu.get_barrier_semaphore()

    def greet(d, carry):
        pl.semaphore_signal(barrier, inc=1, device_id=plane((seq + d) % 32), device_id_type=MESH)
        return carry

    lax.fori_loop(1, 32, greet, 0)

    @pl.when(prefilling)
    def _():
        for g in range(PG):
            pl.semaphore_signal(barrier, inc=1, device_id=line(PG + g), device_id_type=MESH)
        for j in range(HALF):
            pltpu.make_async_copy(kv_columns(core, j), own_rows(j), own_sem.at[j]).start()

        def keep_q(h, carry):
            pltpu.make_async_copy(q_columns(core, h), qbuf.at[core, h], q_sem.at[1]).start()
            return carry

        lax.fori_loop(0, 32, keep_q, 0)
        pl.semaphore_wait(barrier, 35)

    @pl.when(role >= PG)
    def _():
        for d in range(1, 2 * PG):
            pl.semaphore_signal(barrier, inc=1, device_id=line((role + d) % (2 * PG)), device_id_type=MESH)
        pltpu.make_async_copy(w_hbm, wbuf, dlocal.at[0]).start()
        zbuf[...] = jnp.zeros_like(zbuf)
        for i in range(8):
            pltpu.make_async_copy(zbuf, out_hbm.at[:, i * 1024:(i + 1) * 1024], fill_sem.at[i]).start()
        pl.semaphore_wait(barrier, 38)

    def dec_columns(s):
        return dec_hbm.at[:, pl.ds(pl.multiple_of(s * 256, 256), 256)]

    sibling = plane(seq + 1 - 2 * core)

    def finish_own():
        await_first = prefilling

        @pl.when(await_first)
        def _():
            await_bytes(fz.at[0:4], din.at[5])

        @pl.when(jnp.logical_not(await_first))
        def _():
            await_bytes(fz.at[0:3], din.at[5])

        to = lax.broadcasted_iota(jnp.int32, (64, 64), 0)
        at = lax.broadcasted_iota(jnp.int32, (64, 64), 1)
        order = (at == ((to // 4) % 4) * 16 + (to % 4) * 4 + to // 16).astype(jnp.bfloat16)
        slab = jnp.dot(order, fz[0:4].reshape(64, 256), preferred_element_type=jnp.float32)
        fo[...] = slab.astype(jnp.bfloat16)
        pltpu.make_async_copy(fo, dec_columns(seq), dlocal.at[1]).start()

        def spread(d, carry):
            other = ((chip + d) % 16) * 2 + core
            remote(fo, dec_columns(seq), dout.at[6], din.at[6], plane(other)).start()
            return carry

        lax.fori_loop(1, 16, spread, 0)

    def finish_pair():
        pltpu.make_async_copy(fo, dec_columns(seq), dlocal.at[1]).wait()
        await_bytes(dec_hbm.at[:, 0:3840], din.at[6])

        def mirror(c, carry):
            remote(dec_columns(2 * c + core), dec_columns(2 * c + core), dout.at[7], din.at[7], sibling).start()
            return carry

        lax.fori_loop(0, 16, mirror, 0)

    def finish_wait():
        await_bytes(dec_hbm.at[:, 0:3840], dout.at[6])
        await_bytes(dec_hbm.at[:, 0:4096], dout.at[7])
        await_bytes(dec_hbm.at[:, 0:4096], din.at[7])

    @pl.when(prefilling)
    def _():
        right, left = (y + 1) % 4, (y + 3) % 4

        def device(xx, yy):
            return plane((xx * 4 + yy) * 2 + core)

        for j in range(HALF):
            remote(kv_columns(1 - core, j), own_rows(j), send_sem.at[10], slot_sem.at[0, j], sibling).start()

        for slot in range(1, SLOTS):
            @pl.when(chip < slot)
            def _(slot=slot):
                for j in range(HALF):
                    kvbuf[j, (8 - slot) * 256:(9 - slot) * 256, :] = jnp.zeros((256, 256), jnp.bfloat16)

        def wait_slot(slot, j):
            @pl.when(chip >= slot)
            def _():
                await_bytes(chunk(slot, j), slot_sem.at[slot, j])

        def send(kind, src, dst, j, xx, yy):
            remote(chunk(src, j), chunk(dst, j), send_sem.at[kind], slot_sem.at[dst, j], device(xx, yy)).start()

        def own(j):
            pltpu.make_async_copy(kv_columns(core, j), own_rows(j), own_sem.at[j]).wait()
            await_bytes(own_rows(j), slot_sem.at[0, j])

            @pl.when(x < 3)
            def _():
                send(0, 0, 4, j, (x + 1) % 4, y)

            @pl.when(x < 2)
            def _():
                send(1, 0, 8, j, (x + 2) % 4, y)

        def own_along_y(j):
            @pl.when(y < 3)
            def _():
                send(2, 0, 1, j, x, right)

            @pl.when(y == 0)
            def _():
                send(3, 0, 3, j, x, left)

        right_dst = jnp.where(y < 3, 5, 1)
        left_dst = jnp.where(y > 0, 3, 7)
        right_fwd = jnp.where(y < 3, 1, 5)
        left_fwd = jnp.where(y > 0, 7, 3)

        def inject(j):
            wait_slot(4, j)

            @pl.when(x >= 1)
            def _():
                send(4, 4, right_dst, j, x, right)
                send(5, 4, left_dst, j, x, left)

            wait_slot(8, j)

            @pl.when(jnp.logical_and(x >= 2, y == 3))
            def _():
                send(6, 8, 5, j, x, right)

            @pl.when(jnp.logical_and(x >= 2, y > 0))
            def _():
                send(7, 8, 7, j, x, left)

        def forward(j):
            wait_slot(right_fwd, j)

            @pl.when(chip >= right_fwd)
            def _():
                send(8, right_fwd, 2, j, x, right)

            wait_slot(left_fwd, j)

            @pl.when(chip >= left_fwd)
            def _():
                send(9, left_fwd, 6, j, x, left)

        def rest(j):
            wait_slot(6 - right_fwd, j)
            wait_slot(10 - left_fwd, j)
            wait_slot(2, j)
            wait_slot(6, j)

        counts = [lengths[role, i] for i in range(4)]
        served = [serves[role, i] for i in range(4)]
        blocks = [(n + 127) // 128 for n in counts]
        starts = [0, blocks[0], blocks[0] + blocks[1], blocks[0] + blocks[1] + blocks[2]]

        def pick(block, values):
            chosen = values[0]
            for i in range(1, 4):
                chosen = jnp.where(block >= starts[i], values[i], chosen)
            return chosen

        firsts, lives = [], []
        for e in range(2):
            block = 2 * chip + e
            first = pick(block, starts)
            firsts.append((first - (2 * chip - 15 + e)) * 128)
            lives.append(pick(block, counts) - (block - first) * 128)

        at_home = home == core

        def spread_queries():
            await_bytes(qz, din.at[0])

            @pl.when(at_home)
            def _():
                qd[seq % 16] = qz[...]

            def one(d, carry):
                other = ((chip + d) % 16) * 2 + home

                @pl.when(other != seq)
                def _():
                    remote(qz, qd.at[seq % 16], dout.at[1], din.at[1], plane(other)).start()

                return carry

            lax.fori_loop(0, 16, one, 0)

        def await_many(buffer, sem):
            @pl.when(at_home)
            def _():
                await_bytes(buffer.at[0:15], sem)

            @pl.when(jnp.logical_not(at_home))
            def _():
                await_bytes(buffer, sem)

        lanes = lax.broadcasted_iota(jnp.int32, (32, HD), 1)

        def partial_terms():
            await_many(qd, din.at[1])
            for e in range(2):
                group = pick(2 * chip + e, served)
                live = lives[e]

                for j in range(HALF):
                    q = jnp.zeros((4, 8, HD), jnp.float32)
                    for g in range(PG):
                        q = jnp.where(group == g, qd[4 * j:4 * j + 4, g], q)
                    q = q.reshape(32, HD).astype(jnp.bfloat16)
                    keys = kvbuf[j, 2048 + 128 * e:2176 + 128 * e, 0:HD]
                    values = kvbuf[j, 2048 + 128 * e:2176 + 128 * e, HD:2 * HD]
                    s = lax.dot_general(q, keys, (((1,), (1,)), ((), ())), preferred_element_type=jnp.float32)
                    s = jnp.where(lanes < live, s, NEG)
                    m = jnp.max(s, axis=1, keepdims=True)
                    w = jnp.exp2((s - m) * factor)
                    total = jnp.sum(w, axis=1, keepdims=True)
                    o = jnp.dot(w.astype(jnp.bfloat16), values, preferred_element_type=jnp.float32)
                    ds[4 * j:4 * j + 4, e, 0] = o.reshape(4, 8, HD)
                    ds[4 * j:4 * j + 4, e, 1] = jnp.where(lanes < 64, m, total).reshape(4, 8, HD)

            @pl.when(at_home)
            def _():
                dr[chip] = ds[seq % 16]

            def out(d, carry):
                other = 16 * core + (chip + d) % 16

                @pl.when(other != seq)
                def _():
                    remote(ds.at[(chip + d) % 16], dr.at[chip], dout.at[2], din.at[2], plane(other)).start()

                return carry

            lax.fori_loop(0, 16, out, 0)

        which = lax.broadcasted_iota(jnp.int32, (PG, 8, HD), 0)

        def combine_terms():
            await_many(dr, din.at[2])

            terms = []
            top = jnp.full((PG, 8, HD), NEG, jnp.float32)
            for b in range(32):
                flag = which == pick(jnp.int32(b), served)
                m = jnp.broadcast_to(dr[b // 2, b % 2, 1][:, 0:1], (8, HD))[None]
                top = jnp.maximum(top, jnp.where(flag, m, NEG))
                terms.append((flag, m))
            total = jnp.zeros((PG, 8, HD), jnp.float32)
            mixed = jnp.zeros((PG, 8, HD), jnp.float32)
            for b in range(32):
                flag, m = terms[b]
                part = jnp.broadcast_to(dr[b // 2, b % 2, 1][:, 64:65], (8, HD))[None]
                add = jnp.where(flag, jnp.exp2((jnp.minimum(m, top) - top) * factor), 0.0)
                total = total + add * part
                mixed = mixed + add * dr[b // 2, b % 2, 0][None]
            lane3 = lax.broadcasted_iota(jnp.int32, (PG, 8, HD), 2)
            cs[:, 0] = mixed
            cs[:, 1] = jnp.where(lane3 < 64, top, total)
            for g in range(PG):
                remote(cs.at[g], dz.at[role], dout.at[3], din.at[3], line(PG + g)).start()

        for j in range(HALF):
            own(j)
            if j < 2:
                own_along_y(j)

        spread_queries()

        def start_q(h, carry):
            remote(q_columns(1 - core, h), qbuf.at[core, h], send_sem.at[11], q_sem.at[0], sibling).start()
            return carry

        lax.fori_loop(0, 32, start_q, 0)
        partial_terms()
        inject(0)
        own_along_y(2)
        forward(0)
        combine_terms()
        inject(1)
        own_along_y(3)
        rest(0)

        await_bytes(qbuf.at[0], q_sem.at[0])
        await_bytes(qbuf.at[0], q_sem.at[1])

        lane = lax.broadcasted_iota(jnp.int32, (1, KT), 1)
        tri = lax.broadcasted_iota(jnp.int32, (ROWS, 128), 0) % 128 >= lax.broadcasted_iota(jnp.int32, (ROWS, 128), 1)
        row_in = lax.broadcasted_iota(jnp.int32, (ROWS, 128), 0) % 128
        ones = jnp.ones((KT, HD), jnp.bfloat16)
        last = WINDOW // KT - 1

        def place(n):
            j, u = n // 4, n % 4
            return j, u // 2, j * GROUP + (u % 2) * 4

        def key_rows(j, e, kt):
            return j, pl.ds(pl.multiple_of(128 + e * 128 + kt * KT, 128), KT)

        def weave(current, following):
            if following is not None:
                n, scores, peaks = following
                j, e, base = place(n)
                threshold = jnp.where(e == 0, firsts[0], firsts[1])
                q = qbuf[e, pl.ds(base, 4)].reshape(ROWS, HD)
                peak = None
            if current is not None:
                cn, cscores, cpeaks = current
                cj, ce, cbase = place(cn)
                total = None
            for kt in range(WINDOW // KT):
                if following is not None:
                    rows = key_rows(j, e, kt)
                    s = lax.dot_general(
                        q, kvbuf[rows[0], rows[1], 0:HD], (((1,), (1,)), ((), ())), preferred_element_type=jnp.float32)
                if current is not None:
                    weights = [
                        jnp.exp2((cscores[:, kt * KT + i * 128:kt * KT + (i + 1) * 128] - cpeaks[...]) * factor)
                        for i in range(KT // 128)
                    ]
                    rows = key_rows(cj, ce, kt)
                    product = jnp.dot(
                        jnp.concatenate(weights, axis=1).astype(jnp.bfloat16),
                        jnp.concatenate([kvbuf[rows[0], rows[1], HD:2 * HD], ones], axis=1),
                        preferred_element_type=jnp.float32)
                    total = product if total is None else total + product
                if following is not None:
                    s = s + jnp.where(lane + kt * KT >= threshold, 0.0, NEG)
                    pieces = [s[:, i * 128:(i + 1) * 128] for i in range(KT // 128)]
                    if kt == last:
                        pieces[-1] = jnp.where(tri, pieces[-1], NEG)
                    for i, piece in enumerate(pieces):
                        scores[:, kt * KT + i * 128:kt * KT + (i + 1) * 128] = piece
                    while len(pieces) > 1:
                        pieces = [jnp.maximum(a, b) for a, b in zip(pieces[::2], pieces[1::2])]
                    peak = pieces[0] if peak is None else jnp.maximum(peak, pieces[0])
            if following is not None:
                peaks[...] = jnp.broadcast_to(jnp.max(peak, axis=1, keepdims=True), (ROWS, 128))
            if current is not None:
                live = jnp.where(ce == 0, lives[0], lives[1])
                mixed = total[:, :HD] / total[:, HD:]
                mixed = jnp.where(row_in < live, mixed, 0.0).astype(jnp.bfloat16)
                obuf[ce, pl.ds(cbase, 4)] = mixed.reshape(4, BLOCK, HD)
                for i in range(4):
                    columns = out_hbm.at[:, pl.ds(pl.multiple_of((core * 32 + cbase + i) * HD, HD), HD)]

                    @pl.when(ce == core)
                    def _(i=i, columns=columns):
                        pltpu.make_async_copy(obuf.at[ce, cbase + i], columns, out_sem.at[0]).start()

                    @pl.when(ce != core)
                    def _(i=i, columns=columns):
                        remote(obuf.at[ce, cbase + i], columns, send_sem.at[12], out_sem.at[1], sibling).start()

        weave(None, (jnp.int32(0), sbuf, peak0))

        def pair(i, carry):
            j = i // 2
            weave((2 * i, sbuf, peak0), (2 * i + 1, sbuf1, peak1))

            @pl.when(jnp.logical_and(i % 2 == 0, j < HALF - 1))
            def _():
                forward(j + 1)

            @pl.when(jnp.logical_and(i % 2 == 1, j < HALF - 2))
            def _():
                inject(j + 2)

            @pl.when(jnp.logical_and(i % 2 == 1, j < HALF - 1))
            def _():
                rest(j + 1)

            @pl.when(i == 6)
            def _():
                finish_own()

            weave((2 * i + 1, sbuf1, peak1), (2 * i + 2, sbuf, peak0))
            return carry

        lax.fori_loop(0, 7, pair, 0)
        weave((jnp.int32(14), sbuf, peak0), (jnp.int32(15), sbuf1, peak1))
        finish_pair()
        weave((jnp.int32(15), sbuf1, peak1), None)

        span = kvbuf.at[:, 0:256, :]

        def sent(kind, condition):
            @pl.when(condition)
            def _():
                await_bytes(span, send_sem.at[kind])

        sent(0, x < 3)
        sent(1, x < 2)
        sent(2, y < 3)
        sent(3, y == 0)
        sent(4, x >= 1)
        sent(5, x >= 1)
        sent(6, jnp.logical_and(x >= 2, y == 3))
        sent(7, jnp.logical_and(x >= 2, y > 0))
        sent(8, chip >= right_fwd)
        sent(9, chip >= left_fwd)
        await_bytes(kvbuf.at[:, 0:128, :], send_sem.at[10])
        await_bytes(qbuf.at[0], send_sem.at[11])
        await_bytes(obuf.at[0], send_sem.at[12])
        await_bytes(obuf.at[0], out_sem.at[0])
        await_many(qd, dout.at[1])
        await_many(dr, dout.at[2])
        await_bytes(cs, dout.at[3])
        await_bytes(obuf.at[0], out_sem.at[1])
        finish_wait()

    @pl.when(role >= PG)
    def _():
        group = role - PG
        for p in range(PG):
            remote(dq.at[p], qz.at[group], dout.at[0], din.at[0], line(p)).start()
        pltpu.make_async_copy(w_hbm, wbuf, dlocal.at[0]).wait()
        await_bytes(dz, din.at[3])
        step = lax.broadcasted_iota(jnp.int32, (8, HD), 0) % 4
        tiles = []
        for p in range(PG):
            pair = dz[p, 1]
            m = jnp.broadcast_to(pair[:, 0:1], (8, HD))
            part = jnp.broadcast_to(pair[:, 64:65], (8, HD))
            q = dq[p]
            scores = []
            for t in range(4):
                s = jnp.sum(q * fresh[p, 0, t:t + 1, :], axis=1, keepdims=True)
                scores.append(jnp.where(step >= t, jnp.broadcast_to(s, (8, HD)), NEG))
            top = m
            for s in scores:
                top = jnp.maximum(top, s)
            old = jnp.exp2((m - top) * factor)
            total = part * old
            mixed = dz[p, 0] * old
            for t in range(4):
                w = jnp.exp2((scores[t] - top) * factor)
                total = total + w
                mixed = mixed + w * fresh[p, 1, t:t + 1, :]
            tiles.append(mixed / total)
        rows = jnp.concatenate(tiles, axis=0).astype(jnp.bfloat16)
        to = lax.broadcasted_iota(jnp.int32, (16, 32), 0)
        at = lax.broadcasted_iota(jnp.int32, (16, 32), 1)
        halves = []
        for h in range(2):
            chosen = (at == (to // 4) * 8 + h * 4 + to % 4).astype(jnp.bfloat16)
            halves.append(jnp.dot(chosen, rows, preferred_element_type=jnp.float32).astype(jnp.bfloat16))
        attended = jnp.concatenate(halves, axis=1)

        def project(i, carry):
            others = [(seq + 4 * i + d) % 32 for d in range(4)]
            for other in others:
                columns = pl.ds(pl.multiple_of(other * 256, 256), 256)
                rs_s[other] = jnp.dot(attended, wbuf[:, columns], preferred_element_type=jnp.float32)
            for other in others:
                @pl.when(other != seq)
                def _(other=other):
                    remote(rs_s.at[other], rs_r.at[seq], dout.at[4], din.at[4], plane(other)).start()

            return carry

        lax.fori_loop(0, 8, project, 0)
        rs_r[seq] = rs_s[seq]
        await_bytes(rs_r.at[0:31], din.at[4])

        def add(i, total):
            four = [rs_r[4 * i + d] for d in range(4)]
            return total + ((four[0] + four[1]) + (four[2] + four[3]))

        summed = lax.fori_loop(0, 8, add, jnp.zeros((16, 256), jnp.float32))
        fz[group] = summed.astype(jnp.bfloat16)
        for d in range(1, 2 * PG):
            remote(fz.at[group], fz.at[group], dout.at[5], din.at[5], line((role + d) % (2 * PG))).start()
        finish_own()
        finish_pair()
        await_bytes(qz, dout.at[0])
        await_bytes(rs_s.at[0:31], dout.at[4])
        await_bytes(fz.at[0:7], dout.at[5])
        for i in range(8):
            pltpu.make_async_copy(zbuf, out_hbm.at[:, i * 1024:(i + 1) * 1024], fill_sem.at[i]).wait()
        finish_wait()


def fused(prompt_lengths, decode_group, queries, kv, dq, fresh, out_weight):
    smem = pl.BlockSpec(memory_space=pltpu.SMEM)
    vmem = pl.BlockSpec(memory_space=pltpu.VMEM)
    hbm = pl.BlockSpec(memory_space=pl.ANY)
    return pl.pallas_call(
        fused_kernel,
        out_shape=[
            jax.ShapeDtypeStruct((BLOCK, H * HD), jnp.bfloat16),
            jax.ShapeDtypeStruct((64, H * HD), jnp.bfloat16),
        ],
        in_specs=[smem, smem, hbm, hbm, vmem, vmem, hbm],
        out_specs=[hbm, hbm],
        scratch_shapes=[
            pltpu.VMEM((2, 32, BLOCK, HD), jnp.bfloat16),
            pltpu.VMEM((HALF, SLOTS * 256, 256), jnp.bfloat16),
            pltpu.VMEM((ROWS, WINDOW), jnp.float32),
            pltpu.VMEM((ROWS, WINDOW), jnp.float32),
            pltpu.VMEM((ROWS, 128), jnp.float32),
            pltpu.VMEM((ROWS, 128), jnp.float32),
            pltpu.VMEM((2, 32, BLOCK, HD), jnp.bfloat16),
            pltpu.VMEM((BLOCK, 1024), jnp.bfloat16),
            pltpu.VMEM((256, 8192), jnp.bfloat16),
            pltpu.VMEM((PG, 8, HD), jnp.float32),
            pltpu.VMEM((16, PG, 8, HD), jnp.float32),
            pltpu.VMEM((16, 2, 2, 8, HD), jnp.float32),
            pltpu.VMEM((16, 2, 2, 8, HD), jnp.float32),
            pltpu.VMEM((PG, 2, 8, HD), jnp.float32),
            pltpu.VMEM((PG, 2, 8, HD), jnp.float32),
            pltpu.VMEM((32, 16, 256), jnp.float32),
            pltpu.VMEM((32, 16, 256), jnp.float32),
            pltpu.VMEM((8, 16, 256), jnp.bfloat16),
            pltpu.VMEM((64, 256), jnp.bfloat16),
            pltpu.SemaphoreType.DMA((SLOTS, HALF)),
            pltpu.SemaphoreType.DMA((2,)),
            pltpu.SemaphoreType.DMA((HALF,)),
            pltpu.SemaphoreType.DMA((2,)),
            pltpu.SemaphoreType.DMA((8,)),
            pltpu.SemaphoreType.DMA((13,)),
            pltpu.SemaphoreType.DMA((8,)),
            pltpu.SemaphoreType.DMA((8,)),
            pltpu.SemaphoreType.DMA((2,)),
        ],
        compiler_params=pltpu.CompilerParams(
            collective_id=0, has_side_effects=True, vmem_limit_bytes=62 * 1024 * 1024
        ),
        cost_estimate=pl.CostEstimate(flops=17_000_000_000, bytes_accessed=16_000_000, transcendentals=17_000_000),
    )(prompt_lengths, decode_group, queries, kv, dq, fresh, out_weight)


def on_device(prefill_queries, prefill_kv, prompt_lengths, decode_group, decode_queries, decode_kv, out_weight):
    kv_head = lax.axis_index("seq") // (lax.axis_size("seq") // KVH)
    dq = decode_queries[0].reshape(4, PG, 2, HD).transpose(1, 2, 0, 3).reshape(PG, 8, HD).astype(jnp.float32)
    fresh = lax.dynamic_slice_in_dim(decode_kv[0], kv_head * 2 * HD, 2 * HD, 2)
    fresh = fresh.reshape(4, PG, 2, HD).transpose(1, 2, 0, 3).astype(jnp.float32)
    prefill_out, decode_out = fused(
        prompt_lengths, decode_group, prefill_queries[0], prefill_kv[0], dq, fresh, out_weight
    )
    return prefill_out[None], decode_out.reshape(4, PG, PG, -1)


def solution(mesh):
    in_specs = (
        P("role", "seq", None),
        P("role", "seq", None),
        P(),
        P(),
        P("role", None, None, "seq"),
        P("role", None, None, None),
        P("seq", None),
    )
    out_specs = (P("role", "seq", None), P())
    return jax.shard_map(on_device, mesh=mesh, in_specs=in_specs, out_specs=out_specs, check_vma=False)
```

```python
import functools

import jax
import jax.numpy as jnp
from jax import lax
from jax.experimental import pallas as pl
from jax.experimental.pallas import tpu as pltpu
from jax.sharding import PartitionSpec as P

MESH = pl.DeviceIdType.MESH
H = 64
KVH = 8
HD = 128
BLOCK = 128
PG = 4
NEG = -1e30
SCALE = HD**-0.5
LOG2E = 1.4426950408889634
SLOTS = 9
HALF = KVH // 2
GROUP = H // KVH
ROWS = 512
KT = 512
WINDOW = 2048


def fused_kernel(
    lengths, serves, q_hbm, kv_hbm, dq, fresh, w_hbm, out_hbm, dec_hbm,
    qbuf, kvbuf, sbuf, sbuf1, peak0, peak1, obuf, zbuf, wbuf, qz, qb, qd, ds, dr, cs, dz, rs_s, rs_r, fz, fo,
    slot_sem, q_sem, own_sem, out_sem, fill_sem, send_sem, din, dout, dlocal
):
    role = lax.axis_index("role")
    seq = lax.axis_index("seq")
    core = seq % 2
    chip = seq // 2
    y = chip % 4
    x = chip // 4
    home = seq // 16
    prefilling = role < PG
    factor = SCALE * LOG2E

    def plane(other):
        return (role, other)

    def line(other):
        return (other, seq)

    def remote(src, dst, send, recv, device):
        return pltpu.make_async_remote_copy(
            src_ref=src, dst_ref=dst, send_sem=send, recv_sem=recv, device_id=device, device_id_type=MESH)

    def await_bytes(ref, sem):
        pltpu.make_async_copy(ref, ref, sem).wait()

    def q_columns(half, h):
        return q_hbm.at[:, pl.ds(pl.multiple_of((half * 32 + h) * HD, HD), HD)]

    def kv_columns(half, j):
        return kv_hbm.at[:, pl.ds(pl.multiple_of(half * HALF * 256 + j * 256, 256), 256)]

    def chunk(slot, j):
        return kvbuf.at[j, pl.ds(pl.multiple_of((8 - slot) * 256, 256), 256), :]

    def own_rows(j):
        return kvbuf.at[j, pl.ds(pl.multiple_of(2048 + core * 128, 128), 128), :]

    barrier = pltpu.get_barrier_semaphore()

    def greet(d, carry):
        pl.semaphore_signal(barrier, inc=1, device_id=plane((seq + d) % 32), device_id_type=MESH)
        return carry

    lax.fori_loop(1, 32, greet, 0)

    @pl.when(prefilling)
    def _():
        for g in range(PG):
            pl.semaphore_signal(barrier, inc=1, device_id=line(PG + g), device_id_type=MESH)
        for j in range(HALF):
            pltpu.make_async_copy(kv_columns(core, j), own_rows(j), own_sem.at[j]).start()

        def keep_q(h, carry):
            pltpu.make_async_copy(q_columns(core, h), qbuf.at[core, h], q_sem.at[1]).start()
            return carry

        lax.fori_loop(0, 32, keep_q, 0)
        pl.semaphore_wait(barrier, 35)

    @pl.when(role >= PG)
    def _():
        for d in range(1, 2 * PG):
            pl.semaphore_signal(barrier, inc=1, device_id=line((role + d) % (2 * PG)), device_id_type=MESH)
        pltpu.make_async_copy(w_hbm, wbuf, dlocal.at[0]).start()
        zbuf[...] = jnp.zeros_like(zbuf)
        for i in range(8):
            pltpu.make_async_copy(zbuf, out_hbm.at[:, i * 1024:(i + 1) * 1024], fill_sem.at[i]).start()
        pl.semaphore_wait(barrier, 38)

    mine = dec_hbm.at[chip, core]

    sibling = plane(seq + 1 - 2 * core)

    def finish_own():
        await_first = prefilling

        @pl.when(await_first)
        def _():
            await_bytes(fz.at[0:4], din.at[5])

        @pl.when(jnp.logical_not(await_first))
        def _():
            await_bytes(fz.at[0:3], din.at[5])

        to = lax.broadcasted_iota(jnp.int32, (64, 64), 0)
        at = lax.broadcasted_iota(jnp.int32, (64, 64), 1)
        order = (at == ((to // 4) % 4) * 16 + (to % 4) * 4 + to // 16).astype(jnp.bfloat16)
        slab = jnp.dot(order, fz[0:4].reshape(64, 256), preferred_element_type=jnp.float32)
        fo[...] = slab.astype(jnp.bfloat16)
        pltpu.make_async_copy(fo, mine, dlocal.at[1]).start()

        def spread(d, carry):
            other = ((chip + d) % 16) * 2 + core
            remote(fo, mine, dout.at[6], din.at[6], plane(other)).start()
            return carry

        lax.fori_loop(1, 16, spread, 0)

    def finish_pair():
        pltpu.make_async_copy(fo, mine, dlocal.at[1]).wait()
        await_bytes(dec_hbm.at[0:15, 0], din.at[6])
        remote(dec_hbm.at[:, core], dec_hbm.at[:, core], dout.at[7], din.at[7], sibling).start()

    def finish_wait():
        await_bytes(dec_hbm.at[0:15, 0], dout.at[6])
        await_bytes(dec_hbm.at[:, 0], dout.at[7])
        await_bytes(dec_hbm.at[:, 0], din.at[7])

    @pl.when(prefilling)
    def _():
        right, left = (y + 1) % 4, (y + 3) % 4

        def device(xx, yy):
            return plane((xx * 4 + yy) * 2 + core)

        for j in range(HALF):
            remote(kv_columns(1 - core, j), own_rows(j), send_sem.at[10], slot_sem.at[0, j], sibling).start()

        def wait_slot(slot, j):
            @pl.when(chip >= slot)
            def _():
                await_bytes(chunk(slot, j), slot_sem.at[slot, j])

        def send(kind, src, dst, j, xx, yy):
            remote(chunk(src, j), chunk(dst, j), send_sem.at[kind], slot_sem.at[dst, j], device(xx, yy)).start()

        def own_wait(j):
            pltpu.make_async_copy(kv_columns(core, j), own_rows(j), own_sem.at[j]).wait()
            await_bytes(own_rows(j), slot_sem.at[0, j])

        def own(j):
            @pl.when(x < 3)
            def _():
                send(0, 0, 4, j, (x + 1) % 4, y)

            @pl.when(x < 2)
            def _():
                send(1, 0, 8, j, (x + 2) % 4, y)

        def own_along_y(j):
            @pl.when(y < 3)
            def _():
                send(2, 0, 1, j, x, right)

            @pl.when(y == 0)
            def _():
                send(3, 0, 3, j, x, left)

        right_dst = jnp.where(y < 3, 5, 1)
        left_dst = jnp.where(y > 0, 3, 7)
        right_fwd = jnp.where(y < 3, 1, 5)
        left_fwd = jnp.where(y > 0, 7, 3)

        def inject(j):
            wait_slot(4, j)

            @pl.when(x >= 1)
            def _():
                send(4, 4, right_dst, j, x, right)
                send(5, 4, left_dst, j, x, left)

            wait_slot(8, j)

            @pl.when(jnp.logical_and(x >= 2, y == 3))
            def _():
                send(6, 8, 5, j, x, right)

            @pl.when(jnp.logical_and(x >= 2, y > 0))
            def _():
                send(7, 8, 7, j, x, left)

        def forward(j):
            wait_slot(right_fwd, j)

            @pl.when(chip >= right_fwd)
            def _():
                send(8, right_fwd, 2, j, x, right)

            wait_slot(left_fwd, j)

            @pl.when(chip >= left_fwd)
            def _():
                send(9, left_fwd, 6, j, x, left)

        def rest(j):
            wait_slot(6 - right_fwd, j)
            wait_slot(10 - left_fwd, j)
            wait_slot(2, j)
            wait_slot(6, j)

        counts = [lengths[role, i] for i in range(4)]
        served = [serves[role, i] for i in range(4)]
        blocks = [(n + 127) // 128 for n in counts]
        starts = [0, blocks[0], blocks[0] + blocks[1], blocks[0] + blocks[1] + blocks[2]]

        def pick(block, values):
            chosen = values[0]
            for i in range(1, 4):
                chosen = jnp.where(block >= starts[i], values[i], chosen)
            return chosen

        firsts, lives = [], []
        for e in range(2):
            block = 2 * chip + e
            first = pick(block, starts)
            firsts.append((first - (2 * chip - 15 + e)) * 128)
            lives.append(pick(block, counts) - (block - first) * 128)

        at_home = home == core

        def spread_queries():
            await_bytes(qz, din.at[0])
            qb[...] = qz[...].reshape(32, HD).astype(jnp.bfloat16)

            @pl.when(at_home)
            def _():
                qd[seq % 16] = qb[...]

            def one(d, carry):
                other = ((chip + d) % 16) * 2 + home

                @pl.when(other != seq)
                def _():
                    remote(qb, qd.at[seq % 16], dout.at[1], din.at[1], plane(other)).start()

                return carry

            lax.fori_loop(0, 16, one, 0)

        def await_many(buffer, sem):
            @pl.when(at_home)
            def _():
                await_bytes(buffer.at[0:15], sem)

            @pl.when(jnp.logical_not(at_home))
            def _():
                await_bytes(buffer, sem)

        lanes = lax.broadcasted_iota(jnp.int32, (32, HD), 1)

        def partial_terms():
            await_many(qd, din.at[1])
            stats = []
            for e in range(2):
                group = pick(2 * chip + e, served)
                live = lives[e]

                for j in range(HALF):
                    q = jnp.zeros((4, 8, HD), jnp.float32)
                    wide = qd[4 * j:4 * j + 4].astype(jnp.float32).reshape(4, PG, 8, HD)
                    for g in range(PG):
                        q = jnp.where(group == g, wide[:, g], q)
                    q = q.reshape(32, HD).astype(jnp.bfloat16)
                    keys = kvbuf[j, 2048 + 128 * e:2176 + 128 * e, 0:HD]
                    values = kvbuf[j, 2048 + 128 * e:2176 + 128 * e, HD:2 * HD]
                    s = lax.dot_general(q, keys, (((1,), (1,)), ((), ())), preferred_element_type=jnp.float32)
                    s = jnp.where(lanes < live, s, NEG)
                    m = jnp.max(s, axis=1, keepdims=True)
                    w = jnp.exp2((s - m) * factor)
                    total = jnp.sum(w, axis=1, keepdims=True)
                    o = jnp.dot(w.astype(jnp.bfloat16), values, preferred_element_type=jnp.float32)
                    ds[4 * j:4 * j + 4, e] = o.reshape(4, 8, HD)
                    stat = jnp.where(lanes < 64, m, total)
                    if e == 0:
                        stats.append(stat)
                    else:
                        stat = jnp.where(lanes % 64 < 32, stats[j], stat)
                        ds[4 * j:4 * j + 4, 2] = stat.reshape(4, 8, HD)

            @pl.when(at_home)
            def _():
                dr[chip] = ds[seq % 16]

            def out(d, carry):
                other = 16 * core + (chip + d) % 16

                @pl.when(other != seq)
                def _():
                    remote(ds.at[(chip + d) % 16], dr.at[chip], dout.at[2], din.at[2], plane(other)).start()

                return carry

            lax.fori_loop(0, 16, out, 0)

        which = lax.broadcasted_iota(jnp.int32, (PG, 8, HD), 0)

        def combine_terms():
            await_many(dr, din.at[2])

            terms = []
            top = jnp.full((PG, 8, HD), NEG, jnp.float32)
            for b in range(32):
                flag = which == pick(jnp.int32(b), served)
                m = jnp.broadcast_to(dr[b // 2, 2][:, 32 * (b % 2):32 * (b % 2) + 1], (8, HD))[None]
                top = jnp.maximum(top, jnp.where(flag, m, NEG))
                terms.append((flag, m))
            total = jnp.zeros((PG, 8, HD), jnp.float32)
            mixed = jnp.zeros((PG, 8, HD), jnp.float32)
            for b in range(32):
                flag, m = terms[b]
                part = jnp.broadcast_to(dr[b // 2, 2][:, 64 + 32 * (b % 2):65 + 32 * (b % 2)], (8, HD))[None]
                add = jnp.where(flag, jnp.exp2((jnp.minimum(m, top) - top) * factor), 0.0)
                total = total + add * part
                mixed = mixed + add * dr[b // 2, b % 2][None]
            lane3 = lax.broadcasted_iota(jnp.int32, (PG, 8, HD), 2)
            cs[:, 0] = mixed
            cs[:, 1] = jnp.where(lane3 < 64, top, total)
            for g in range(PG):
                remote(cs.at[g], dz.at[role], dout.at[3], din.at[3], line(PG + g)).start()

        own_wait(0)
        own(0)

        for slot in range(1, SLOTS):
            @pl.when(chip < slot)
            def _(slot=slot):
                for j in range(HALF):
                    kvbuf[j, (8 - slot) * 256:(9 - slot) * 256, :] = jnp.zeros((256, 256), jnp.bfloat16)

        spread_queries()
        own_along_y(0)

        def start_q(h, carry):
            remote(q_columns(1 - core, h), qbuf.at[core, h], send_sem.at[11], q_sem.at[0], sibling).start()
            return carry

        lax.fori_loop(0, 32, start_q, 0)
        for j in range(1, HALF):
            own_wait(j)
        partial_terms()
        own(1)
        inject(0)
        own_along_y(1)
        combine_terms()
        forward(0)
        own(2)
        inject(1)
        own_along_y(2)
        rest(0)

        await_bytes(qbuf.at[0], q_sem.at[0])
        await_bytes(qbuf.at[0], q_sem.at[1])

        lane = lax.broadcasted_iota(jnp.int32, (1, KT), 1)
        tri = lax.broadcasted_iota(jnp.int32, (ROWS, 128), 0) % 128 >= lax.broadcasted_iota(jnp.int32, (ROWS, 128), 1)
        row_in = lax.broadcasted_iota(jnp.int32, (ROWS, 128), 0) % 128
        ones = jnp.ones((KT, HD), jnp.bfloat16)
        last = WINDOW // KT - 1

        def place(n):
            j, u = n // 4, n % 4
            return j, u // 2, j * GROUP + (u % 2) * 4

        def key_rows(j, e, kt):
            return j, pl.ds(pl.multiple_of(128 + e * 128 + kt * KT, 128), KT)

        def weave(current, following):
            if following is not None:
                n, scores, peaks = following
                j, e, base = place(n)
                threshold = jnp.where(e == 0, firsts[0], firsts[1])
                q = qbuf[e, pl.ds(base, 4)].reshape(ROWS, HD)
                peak = None
            if current is not None:
                cn, cscores, cpeaks = current
                cj, ce, cbase = place(cn)
                total = None
            for kt in range(WINDOW // KT):
                if following is not None:
                    rows = key_rows(j, e, kt)
                    s = lax.dot_general(
                        q, kvbuf[rows[0], rows[1], 0:HD], (((1,), (1,)), ((), ())), preferred_element_type=jnp.float32)
                if current is not None:
                    weights = [
                        jnp.exp2((cscores[:, kt * KT + i * 128:kt * KT + (i + 1) * 128] - cpeaks[...]) * factor)
                        for i in range(KT // 128)
                    ]
                    rows = key_rows(cj, ce, kt)
                    product = jnp.dot(
                        jnp.concatenate(weights, axis=1).astype(jnp.bfloat16),
                        jnp.concatenate([kvbuf[rows[0], rows[1], HD:2 * HD], ones], axis=1),
                        preferred_element_type=jnp.float32)
                    total = product if total is None else total + product
                if following is not None:
                    s = s + jnp.where(lane + kt * KT >= threshold, 0.0, NEG)
                    pieces = [s[:, i * 128:(i + 1) * 128] for i in range(KT // 128)]
                    if kt == last:
                        pieces[-1] = jnp.where(tri, pieces[-1], NEG)
                    for i, piece in enumerate(pieces):
                        scores[:, kt * KT + i * 128:kt * KT + (i + 1) * 128] = piece
                    while len(pieces) > 1:
                        pieces = [jnp.maximum(a, b) for a, b in zip(pieces[::2], pieces[1::2])]
                    peak = pieces[0] if peak is None else jnp.maximum(peak, pieces[0])
            if following is not None:
                peaks[...] = jnp.broadcast_to(jnp.max(peak, axis=1, keepdims=True), (ROWS, 128))
            if current is not None:
                live = jnp.where(ce == 0, lives[0], lives[1])
                mixed = total[:, :HD] / total[:, HD:]
                mixed = jnp.where(row_in < live, mixed, 0.0).astype(jnp.bfloat16)
                obuf[ce, pl.ds(cbase, 4)] = mixed.reshape(4, BLOCK, HD)
                for i in range(4):
                    columns = out_hbm.at[:, pl.ds(pl.multiple_of((core * 32 + cbase + i) * HD, HD), HD)]

                    @pl.when(ce == core)
                    def _(i=i, columns=columns):
                        pltpu.make_async_copy(obuf.at[ce, cbase + i], columns, out_sem.at[0]).start()

                    @pl.when(ce != core)
                    def _(i=i, columns=columns):
                        remote(obuf.at[ce, cbase + i], columns, send_sem.at[12], out_sem.at[1], sibling).start()

        weave(None, (jnp.int32(0), sbuf, peak0))

        def pair(i, carry):
            j = i // 2
            weave((2 * i, sbuf, peak0), (2 * i + 1, sbuf1, peak1))

            @pl.when(i == 0)
            def _():
                own(3)

            @pl.when(jnp.logical_and(i % 2 == 0, j < HALF - 1))
            def _():
                forward(j + 1)

            @pl.when(i == 1)
            def _():
                own_along_y(3)

            @pl.when(jnp.logical_and(i % 2 == 1, j < HALF - 2))
            def _():
                inject(j + 2)

            @pl.when(jnp.logical_and(i % 2 == 1, j < HALF - 1))
            def _():
                rest(j + 1)

            @pl.when(i == 6)
            def _():
                finish_own()

            weave((2 * i + 1, sbuf1, peak1), (2 * i + 2, sbuf, peak0))
            return carry

        lax.fori_loop(0, 7, pair, 0)
        weave((jnp.int32(14), sbuf, peak0), (jnp.int32(15), sbuf1, peak1))
        finish_pair()
        weave((jnp.int32(15), sbuf1, peak1), None)

        span = kvbuf.at[:, 0:256, :]

        def sent(kind, condition):
            @pl.when(condition)
            def _():
                await_bytes(span, send_sem.at[kind])

        sent(0, x < 3)
        sent(1, x < 2)
        sent(2, y < 3)
        sent(3, y == 0)
        sent(4, x >= 1)
        sent(5, x >= 1)
        sent(6, jnp.logical_and(x >= 2, y == 3))
        sent(7, jnp.logical_and(x >= 2, y > 0))
        sent(8, chip >= right_fwd)
        sent(9, chip >= left_fwd)
        await_bytes(kvbuf.at[:, 0:128, :], send_sem.at[10])
        await_bytes(qbuf.at[0], send_sem.at[11])
        await_bytes(obuf.at[0], send_sem.at[12])
        await_bytes(obuf.at[0], out_sem.at[0])
        await_many(qd, dout.at[1])
        await_many(dr, dout.at[2])
        await_bytes(cs, dout.at[3])
        await_bytes(obuf.at[0], out_sem.at[1])
        finish_wait()

    @pl.when(role >= PG)
    def _():
        group = role - PG
        for p in range(PG):
            remote(dq.at[p], qz.at[group], dout.at[0], din.at[0], line(p)).start()
        pltpu.make_async_copy(w_hbm, wbuf, dlocal.at[0]).wait()
        await_bytes(dz, din.at[3])
        step = lax.broadcasted_iota(jnp.int32, (8, HD), 0) % 4
        tiles = []
        for p in range(PG):
            pair = dz[p, 1]
            m = jnp.broadcast_to(pair[:, 0:1], (8, HD))
            part = jnp.broadcast_to(pair[:, 64:65], (8, HD))
            q = dq[p]
            scores = []
            for t in range(4):
                s = jnp.sum(q * fresh[p, 0, t:t + 1, :], axis=1, keepdims=True)
                scores.append(jnp.where(step >= t, jnp.broadcast_to(s, (8, HD)), NEG))
            top = m
            for s in scores:
                top = jnp.maximum(top, s)
            old = jnp.exp2((m - top) * factor)
            total = part * old
            mixed = dz[p, 0] * old
            for t in range(4):
                w = jnp.exp2((scores[t] - top) * factor)
                total = total + w
                mixed = mixed + w * fresh[p, 1, t:t + 1, :]
            tiles.append(mixed / total)
        rows = jnp.concatenate(tiles, axis=0).astype(jnp.bfloat16)
        to = lax.broadcasted_iota(jnp.int32, (16, 32), 0)
        at = lax.broadcasted_iota(jnp.int32, (16, 32), 1)
        halves = []
        for h in range(2):
            chosen = (at == (to // 4) * 8 + h * 4 + to % 4).astype(jnp.bfloat16)
            halves.append(jnp.dot(chosen, rows, preferred_element_type=jnp.float32).astype(jnp.bfloat16))
        attended = jnp.concatenate(halves, axis=1)

        def project(i, carry):
            others = [(seq + 4 * i + d) % 32 for d in range(4)]
            for other in others:
                columns = pl.ds(pl.multiple_of(other * 256, 256), 256)
                rs_s[other] = jnp.dot(
                    attended, wbuf[:, columns], preferred_element_type=jnp.float32).astype(jnp.bfloat16)
            for other in others:
                @pl.when(other != seq)
                def _(other=other):
                    remote(rs_s.at[other], rs_r.at[seq], dout.at[4], din.at[4], plane(other)).start()

            return carry

        lax.fori_loop(0, 8, project, 0)
        rs_r[seq] = rs_s[seq]
        await_bytes(rs_r.at[0:31], din.at[4])

        def add(i, total):
            four = [rs_r[4 * i + d].astype(jnp.float32) for d in range(4)]
            return total + ((four[0] + four[1]) + (four[2] + four[3]))

        summed = lax.fori_loop(0, 8, add, jnp.zeros((16, 256), jnp.float32))
        fz[group] = summed.astype(jnp.bfloat16)
        for d in range(1, 2 * PG):
            remote(fz.at[group], fz.at[group], dout.at[5], din.at[5], line((role + d) % (2 * PG))).start()
        finish_own()
        finish_pair()
        await_bytes(qz, dout.at[0])
        await_bytes(rs_s.at[0:31], dout.at[4])
        await_bytes(fz.at[0:7], dout.at[5])
        for i in range(8):
            pltpu.make_async_copy(zbuf, out_hbm.at[:, i * 1024:(i + 1) * 1024], fill_sem.at[i]).wait()
        finish_wait()


def fused(prompt_lengths, decode_group, queries, kv, dq, fresh, out_weight):
    smem = pl.BlockSpec(memory_space=pltpu.SMEM)
    vmem = pl.BlockSpec(memory_space=pltpu.VMEM)
    hbm = pl.BlockSpec(memory_space=pl.ANY)
    return pl.pallas_call(
        fused_kernel,
        out_shape=[
            jax.ShapeDtypeStruct((BLOCK, H * HD), jnp.bfloat16),
            jax.ShapeDtypeStruct((16, 2, 64, 256), jnp.bfloat16),
        ],
        in_specs=[smem, smem, hbm, hbm, vmem, vmem, hbm],
        out_specs=[hbm, hbm],
        scratch_shapes=[
            pltpu.VMEM((2, 32, BLOCK, HD), jnp.bfloat16),
            pltpu.VMEM((HALF, SLOTS * 256, 256), jnp.bfloat16),
            pltpu.VMEM((ROWS, WINDOW), jnp.float32),
            pltpu.VMEM((ROWS, WINDOW), jnp.float32),
            pltpu.VMEM((ROWS, 128), jnp.float32),
            pltpu.VMEM((ROWS, 128), jnp.float32),
            pltpu.VMEM((2, 32, BLOCK, HD), jnp.bfloat16),
            pltpu.VMEM((BLOCK, 1024), jnp.bfloat16),
            pltpu.VMEM((256, 8192), jnp.bfloat16),
            pltpu.VMEM((PG, 8, HD), jnp.float32),
            pltpu.VMEM((32, HD), jnp.bfloat16),
            pltpu.VMEM((16, 32, HD), jnp.bfloat16),
            pltpu.VMEM((16, 3, 8, HD), jnp.float32),
            pltpu.VMEM((16, 3, 8, HD), jnp.float32),
            pltpu.VMEM((PG, 2, 8, HD), jnp.float32),
            pltpu.VMEM((PG, 2, 8, HD), jnp.float32),
            pltpu.VMEM((32, 16, 256), jnp.bfloat16),
            pltpu.VMEM((32, 16, 256), jnp.bfloat16),
            pltpu.VMEM((8, 16, 256), jnp.bfloat16),
            pltpu.VMEM((64, 256), jnp.bfloat16),
            pltpu.SemaphoreType.DMA((SLOTS, HALF)),
            pltpu.SemaphoreType.DMA((2,)),
            pltpu.SemaphoreType.DMA((HALF,)),
            pltpu.SemaphoreType.DMA((2,)),
            pltpu.SemaphoreType.DMA((8,)),
            pltpu.SemaphoreType.DMA((13,)),
            pltpu.SemaphoreType.DMA((8,)),
            pltpu.SemaphoreType.DMA((8,)),
            pltpu.SemaphoreType.DMA((2,)),
        ],
        compiler_params=pltpu.CompilerParams(
            collective_id=0, has_side_effects=True, vmem_limit_bytes=62 * 1024 * 1024
        ),
        cost_estimate=pl.CostEstimate(flops=17_000_000_000, bytes_accessed=16_000_000, transcendentals=17_000_000),
    )(prompt_lengths, decode_group, queries, kv, dq, fresh, out_weight)


def on_device(prefill_queries, prefill_kv, prompt_lengths, decode_group, decode_queries, decode_kv, out_weight):
    kv_head = lax.axis_index("seq") // (lax.axis_size("seq") // KVH)
    dq = decode_queries[0].reshape(4, PG, 2, HD).transpose(1, 2, 0, 3).reshape(PG, 8, HD).astype(jnp.float32)
    fresh = lax.dynamic_slice_in_dim(decode_kv[0], kv_head * 2 * HD, 2 * HD, 2)
    fresh = fresh.reshape(4, PG, 2, HD).transpose(1, 2, 0, 3).astype(jnp.float32)
    prefill_out, decode_out = fused(
        prompt_lengths, decode_group, prefill_queries[0], prefill_kv[0], dq, fresh, out_weight
    )
    decode_out = decode_out.reshape(32, 4, PG, PG, 256).transpose(1, 2, 3, 0, 4).reshape(4, PG, PG, -1)
    return prefill_out[None], decode_out


def solution(mesh):
    in_specs = (
        P("role", "seq", None),
        P("role", "seq", None),
        P(),
        P(),
        P("role", None, None, "seq"),
        P("role", None, None, None),
        P("seq", None),
    )
    out_specs = (P("role", "seq", None), P())
    return jax.shard_map(on_device, mesh=mesh, in_specs=in_specs, out_specs=out_specs, check_vma=False)
```

```python
import functools

import jax
import jax.numpy as jnp
from jax import lax
from jax.experimental import pallas as pl
from jax.experimental.pallas import tpu as pltpu
from jax.sharding import PartitionSpec as P

MESH = pl.DeviceIdType.MESH
H = 64
KVH = 8
HD = 128
BLOCK = 128
PG = 4
NEG = -1e30
SCALE = HD**-0.5
LOG2E = 1.4426950408889634
SLOTS = 9
HALF = KVH // 2
GROUP = H // KVH
ROWS = 512
KT = 512
WINDOW = 2048


def fused_kernel(
    lengths, serves, q_hbm, kv_hbm, dq, fresh, w_hbm, out_hbm, dec_hbm,
    qbuf, kvbuf, rawbuf, stage, sbuf, sbuf1, peak0, peak1, eye, maskbuf, obuf, zbuf, wbuf, qz, qb, qd, ds, dr, cs, dz, rs_s, rs_r, fz, fo,
    slot_sem, q_sem, own_sem, out_sem, fill_sem, send_sem, din, dout, dlocal
):
    role = lax.axis_index("role")
    seq = lax.axis_index("seq")
    core = seq % 2
    chip = seq // 2
    y = chip % 4
    x = chip // 4
    home = seq // 16
    prefilling = role < PG
    factor = SCALE * LOG2E

    def plane(other):
        return (role, other)

    def line(other):
        return (other, seq)

    def remote(src, dst, send, recv, device):
        return pltpu.make_async_remote_copy(
            src_ref=src, dst_ref=dst, send_sem=send, recv_sem=recv, device_id=device, device_id_type=MESH)

    def await_bytes(ref, sem):
        pltpu.make_async_copy(ref, ref, sem).wait()

    def q_columns(half, h):
        return q_hbm.at[:, pl.ds(pl.multiple_of((half * 32 + h) * HD, HD), HD)]

    def chunk(slot, j):
        return kvbuf.at[j, pl.ds(16 - 2 * slot, 2)]

    barrier = pltpu.get_barrier_semaphore()

    def greet(d, carry):
        pl.semaphore_signal(barrier, inc=1, device_id=plane((seq + d) % 32), device_id_type=MESH)
        return carry

    lax.fori_loop(1, 32, greet, 0)

    @pl.when(prefilling)
    def _():
        for g in range(PG):
            pl.semaphore_signal(barrier, inc=1, device_id=line(PG + g), device_id_type=MESH)
        raw_copy = pltpu.make_async_copy(kv_hbm, rawbuf, own_sem.at[0])
        raw_copy.start()

        def keep_q(h, carry):
            pltpu.make_async_copy(q_columns(core, h), qbuf.at[core, h], q_sem.at[1]).start()
            return carry

        lax.fori_loop(0, 32, keep_q, 0)
        raw_copy.wait()

        def halves(side, j):
            start = pl.multiple_of(side * HALF * 256 + j * 256, 256)
            return rawbuf[:, pl.ds(start, HD)].T, rawbuf[:, pl.ds(pl.multiple_of(start + HD, HD), HD)]

        for j in range(HALF):
            stage[j, 0], stage[j, 1] = halves(1 - core, j)
        for j in range(HALF):
            kvbuf[j, 16 + core, 0], kvbuf[j, 16 + core, 1] = halves(core, j)
        pl.semaphore_wait(barrier, 35)

    @pl.when(role >= PG)
    def _():
        for d in range(1, 2 * PG):
            pl.semaphore_signal(barrier, inc=1, device_id=line((role + d) % (2 * PG)), device_id_type=MESH)
        pltpu.make_async_copy(w_hbm, wbuf, dlocal.at[0]).start()
        zbuf[...] = jnp.zeros_like(zbuf)
        for i in range(8):
            pltpu.make_async_copy(zbuf, out_hbm.at[:, i * 1024:(i + 1) * 1024], fill_sem.at[i]).start()
        pl.semaphore_wait(barrier, 38)

    mine = dec_hbm.at[chip, core]

    sibling = plane(seq + 1 - 2 * core)

    def finish_own():
        await_first = prefilling

        @pl.when(await_first)
        def _():
            await_bytes(fz.at[0:4], din.at[5])

        @pl.when(jnp.logical_not(await_first))
        def _():
            await_bytes(fz.at[0:3], din.at[5])

        to = lax.broadcasted_iota(jnp.int32, (64, 64), 0)
        at = lax.broadcasted_iota(jnp.int32, (64, 64), 1)
        order = (at == ((to // 4) % 4) * 16 + (to % 4) * 4 + to // 16).astype(jnp.bfloat16)
        slab = jnp.dot(order, fz[0:4].reshape(64, 256), preferred_element_type=jnp.float32)
        fo[...] = slab.astype(jnp.bfloat16)
        pltpu.make_async_copy(fo, mine, dlocal.at[1]).start()

        def spread(d, carry):
            other = ((chip + d) % 16) * 2 + core
            remote(fo, mine, dout.at[6], din.at[6], plane(other)).start()
            return carry

        lax.fori_loop(1, 16, spread, 0)

    def finish_pair():
        pltpu.make_async_copy(fo, mine, dlocal.at[1]).wait()
        await_bytes(dec_hbm.at[0:15, 0], din.at[6])
        remote(dec_hbm.at[:, core], dec_hbm.at[:, core], dout.at[7], din.at[7], sibling).start()

    def finish_wait():
        await_bytes(dec_hbm.at[0:15, 0], dout.at[6])
        await_bytes(dec_hbm.at[:, 0], dout.at[7])
        await_bytes(dec_hbm.at[:, 0], din.at[7])

    @pl.when(prefilling)
    def _():
        right, left = (y + 1) % 4, (y + 3) % 4

        def device(xx, yy):
            return plane((xx * 4 + yy) * 2 + core)

        for j in range(HALF):
            remote(stage.at[j], kvbuf.at[j, 16 + core], send_sem.at[10], slot_sem.at[0, j], sibling).start()

        def wait_slot(slot, j):
            @pl.when(chip >= slot)
            def _():
                await_bytes(chunk(slot, j), slot_sem.at[slot, j])

        def send(kind, src, dst, j, xx, yy):
            remote(chunk(src, j), chunk(dst, j), send_sem.at[kind], slot_sem.at[dst, j], device(xx, yy)).start()

        def own_wait(j):
            await_bytes(kvbuf.at[j, 16 + core], slot_sem.at[0, j])

        def own(j):
            @pl.when(x < 3)
            def _():
                send(0, 0, 4, j, (x + 1) % 4, y)

            @pl.when(x < 2)
            def _():
                send(1, 0, 8, j, (x + 2) % 4, y)

        def own_along_y(j):
            @pl.when(y < 3)
            def _():
                send(2, 0, 1, j, x, right)

            @pl.when(y == 0)
            def _():
                send(3, 0, 3, j, x, left)

        right_dst = jnp.where(y < 3, 5, 1)
        left_dst = jnp.where(y > 0, 3, 7)
        right_fwd = jnp.where(y < 3, 1, 5)
        left_fwd = jnp.where(y > 0, 7, 3)

        def inject(j):
            wait_slot(4, j)

            @pl.when(x >= 1)
            def _():
                send(4, 4, right_dst, j, x, right)
                send(5, 4, left_dst, j, x, left)

            wait_slot(8, j)

            @pl.when(jnp.logical_and(x >= 2, y == 3))
            def _():
                send(6, 8, 5, j, x, right)

            @pl.when(jnp.logical_and(x >= 2, y > 0))
            def _():
                send(7, 8, 7, j, x, left)

        def forward(j):
            wait_slot(right_fwd, j)

            @pl.when(chip >= right_fwd)
            def _():
                send(8, right_fwd, 2, j, x, right)

            wait_slot(left_fwd, j)

            @pl.when(chip >= left_fwd)
            def _():
                send(9, left_fwd, 6, j, x, left)

        def rest(j):
            wait_slot(6 - right_fwd, j)
            wait_slot(10 - left_fwd, j)
            wait_slot(2, j)
            wait_slot(6, j)

        counts = [lengths[role, i] for i in range(4)]
        served = [serves[role, i] for i in range(4)]
        blocks = [(n + 127) // 128 for n in counts]
        starts = [0, blocks[0], blocks[0] + blocks[1], blocks[0] + blocks[1] + blocks[2]]

        def pick(block, values):
            chosen = values[0]
            for i in range(1, 4):
                chosen = jnp.where(block >= starts[i], values[i], chosen)
            return chosen

        firsts, lives = [], []
        for e in range(2):
            block = 2 * chip + e
            first = pick(block, starts)
            firsts.append(first - (2 * chip - 15 + e))
            lives.append(pick(block, counts) - (block - first) * 128)

        at_home = home == core

        def spread_queries():
            await_bytes(qz, din.at[0])
            qb[...] = qz[...].reshape(32, HD).astype(jnp.bfloat16)

            @pl.when(at_home)
            def _():
                qd[seq % 16] = qb[...]

            def one(d, carry):
                other = ((chip + d) % 16) * 2 + home

                @pl.when(other != seq)
                def _():
                    remote(qb, qd.at[seq % 16], dout.at[1], din.at[1], plane(other)).start()

                return carry

            lax.fori_loop(0, 16, one, 0)

        def await_many(buffer, sem):
            @pl.when(at_home)
            def _():
                await_bytes(buffer.at[0:15], sem)

            @pl.when(jnp.logical_not(at_home))
            def _():
                await_bytes(buffer, sem)

        lanes = lax.broadcasted_iota(jnp.int32, (32, HD), 1)

        def partial_terms():
            await_many(qd, din.at[1])
            stats = []
            for e in range(2):
                group = pick(2 * chip + e, served)
                live = lives[e]

                for j in range(HALF):
                    q = jnp.zeros((4, 8, HD), jnp.float32)
                    wide = qd[4 * j:4 * j + 4].astype(jnp.float32).reshape(4, PG, 8, HD)
                    for g in range(PG):
                        q = jnp.where(group == g, wide[:, g], q)
                    q = q.reshape(32, HD).astype(jnp.bfloat16)
                    values = kvbuf[j, 16 + e, 1]
                    s = jnp.dot(q, kvbuf[j, 16 + e, 0], preferred_element_type=jnp.float32)
                    s = jnp.where(lanes < live, s, NEG)
                    m = jnp.max(s, axis=1, keepdims=True)
                    w = jnp.exp2((s - m) * factor)
                    total = jnp.sum(w, axis=1, keepdims=True)
                    o = jnp.dot(w.astype(jnp.bfloat16), values, preferred_element_type=jnp.float32)
                    ds[4 * j:4 * j + 4, e] = o.reshape(4, 8, HD)
                    stat = jnp.where(lanes < 64, m, total)
                    if e == 0:
                        stats.append(stat)
                    else:
                        stat = jnp.where(lanes % 64 < 32, stats[j], stat)
                        ds[4 * j:4 * j + 4, 2] = stat.reshape(4, 8, HD)

            @pl.when(at_home)
            def _():
                dr[chip] = ds[seq % 16]

            def out(d, carry):
                other = 16 * core + (chip + d) % 16

                @pl.when(other != seq)
                def _():
                    remote(ds.at[(chip + d) % 16], dr.at[chip], dout.at[2], din.at[2], plane(other)).start()

                return carry

            lax.fori_loop(0, 16, out, 0)

        which = lax.broadcasted_iota(jnp.int32, (PG, 8, HD), 0)

        def combine_terms():
            await_many(dr, din.at[2])

            terms = []
            top = jnp.full((PG, 8, HD), NEG, jnp.float32)
            for b in range(32):
                flag = which == pick(jnp.int32(b), served)
                m = jnp.broadcast_to(dr[b // 2, 2][:, 32 * (b % 2):32 * (b % 2) + 1], (8, HD))[None]
                top = jnp.maximum(top, jnp.where(flag, m, NEG))
                terms.append((flag, m))
            total = jnp.zeros((PG, 8, HD), jnp.float32)
            mixed = jnp.zeros((PG, 8, HD), jnp.float32)
            for b in range(32):
                flag, m = terms[b]
                part = jnp.broadcast_to(dr[b // 2, 2][:, 64 + 32 * (b % 2):65 + 32 * (b % 2)], (8, HD))[None]
                add = jnp.where(flag, jnp.exp2((jnp.minimum(m, top) - top) * factor), 0.0)
                total = total + add * part
                mixed = mixed + add * dr[b // 2, b % 2][None]
            lane3 = lax.broadcasted_iota(jnp.int32, (PG, 8, HD), 2)
            cs[:, 0] = mixed
            cs[:, 1] = jnp.where(lane3 < 64, top, total)
            for g in range(PG):
                remote(cs.at[g], dz.at[role], dout.at[3], din.at[3], line(PG + g)).start()

        own_wait(0)
        own(0)

        own_along_y(0)

        for slot in range(1, SLOTS):
            @pl.when(chip < slot)
            def _(slot=slot):
                for j in range(HALF):
                    kvbuf[j, 16 - 2 * slot:18 - 2 * slot] = jnp.zeros((2, 2, 128, 128), jnp.bfloat16)

        at = lax.broadcasted_iota(jnp.int32, (128, 128), 0)
        to = lax.broadcasted_iota(jnp.int32, (128, 128), 1)
        for i in range(ROWS // 128):
            eye[i * 128:(i + 1) * 128, :] = (at == to).astype(jnp.bfloat16)
        for e in range(2):
            for w in range(15):
                level = jnp.where(firsts[e] <= w, 0.0, NEG)
                maskbuf[e, :, w * 128:(w + 1) * 128] = jnp.full((128, 128), level, jnp.float32).astype(jnp.bfloat16)
            maskbuf[e, :, 1920:2048] = jnp.where(to <= at, 0.0, NEG).astype(jnp.bfloat16)

        spread_queries()

        def start_q(h, carry):
            remote(q_columns(1 - core, h), qbuf.at[core, h], send_sem.at[11], q_sem.at[0], sibling).start()
            return carry

        lax.fori_loop(0, 32, start_q, 0)
        inject(0)
        for j in range(1, HALF):
            own_wait(j)
        own(1)
        partial_terms()
        forward(0)
        own_along_y(1)
        own(2)
        inject(1)
        own_along_y(2)
        rest(0)

        await_bytes(qbuf.at[0], q_sem.at[0])
        await_bytes(qbuf.at[0], q_sem.at[1])

        row_in = lax.broadcasted_iota(jnp.int32, (ROWS, 128), 0) & 127
        ones = jnp.ones((KT, HD), jnp.bfloat16)

        def place(n):
            j, u = n // 4, n % 4
            return j, u // 2, j * GROUP + (u % 2) * 4

        def weave(current, following):
            if following is not None:
                n, scores, peaks = following
                j, e, base = place(n)
                q = jnp.concatenate([qbuf[e, pl.ds(base, 4)].reshape(ROWS, HD), eye[...]], axis=1)
                peak = None
            if current is not None:
                cn, cscores, cpeaks = current
                cj, ce, cbase = place(cn)
                total = None
            for kt in range(WINDOW // KT):
                if following is not None:
                    blocks_t = [kvbuf[j, 1 + e + 4 * kt + i, 0] for i in range(4)]
                    masked_keys = jnp.concatenate(
                        [jnp.concatenate(blocks_t, axis=1), maskbuf[e, :, kt * KT:(kt + 1) * KT]], axis=0)
                    s = jnp.dot(q, masked_keys, preferred_element_type=jnp.float32)
                if current is not None:
                    weights = [
                        jnp.exp2((cscores[:, kt * KT + i * 128:kt * KT + (i + 1) * 128] - cpeaks[...]) * factor)
                        for i in range(KT // 128)
                    ]
                    values = kvbuf[cj, pl.ds(1 + ce + 4 * kt, 4), 1].reshape(KT, HD)
                    product = jnp.dot(
                        jnp.concatenate(weights, axis=1).astype(jnp.bfloat16),
                        jnp.concatenate([values, ones], axis=1),
                        preferred_element_type=jnp.float32)
                    total = product if total is None else total + product
                if following is not None:
                    pieces = [s[:, i * 128:(i + 1) * 128] for i in range(KT // 128)]
                    for i, piece in enumerate(pieces):
                        scores[:, kt * KT + i * 128:kt * KT + (i + 1) * 128] = piece
                    while len(pieces) > 1:
                        pieces = [jnp.maximum(a, b) for a, b in zip(pieces[::2], pieces[1::2])]
                    peak = pieces[0] if peak is None else jnp.maximum(peak, pieces[0])
            if following is not None:
                peaks[...] = jnp.broadcast_to(jnp.max(peak, axis=1, keepdims=True), (ROWS, 128))
            if current is not None:
                live = jnp.where(ce == 0, lives[0], lives[1])
                mixed = total[:, :HD] / total[:, HD:]
                mixed = jnp.where(row_in < live, mixed, 0.0).astype(jnp.bfloat16)
                obuf[ce, pl.ds(cbase, 4)] = mixed.reshape(4, BLOCK, HD)
                for i in range(4):
                    columns = out_hbm.at[:, pl.ds(pl.multiple_of((core * 32 + cbase + i) * HD, HD), HD)]

                    @pl.when(ce == core)
                    def _(i=i, columns=columns):
                        pltpu.make_async_copy(obuf.at[ce, cbase + i], columns, out_sem.at[0]).start()

                    @pl.when(ce != core)
                    def _(i=i, columns=columns):
                        remote(obuf.at[ce, cbase + i], columns, send_sem.at[12], out_sem.at[1], sibling).start()

        weave(None, (jnp.int32(0), sbuf, peak0))

        def pair(i, carry):
            j = i // 2
            weave((2 * i, sbuf, peak0), (2 * i + 1, sbuf1, peak1))

            @pl.when(i == 0)
            def _():
                combine_terms()
                own(3)

            @pl.when(jnp.logical_and(i % 2 == 0, j < HALF - 1))
            def _():
                forward(j + 1)

            @pl.when(i == 1)
            def _():
                own_along_y(3)

            @pl.when(jnp.logical_and(i % 2 == 1, j < HALF - 2))
            def _():
                inject(j + 2)

            @pl.when(jnp.logical_and(i % 2 == 1, j < HALF - 1))
            def _():
                rest(j + 1)

            @pl.when(i == 6)
            def _():
                finish_own()

            weave((2 * i + 1, sbuf1, peak1), (2 * i + 2, sbuf, peak0))
            return carry

        lax.fori_loop(0, 7, pair, 0)
        weave((jnp.int32(14), sbuf, peak0), (jnp.int32(15), sbuf1, peak1))
        finish_pair()
        weave((jnp.int32(15), sbuf1, peak1), None)

        span = kvbuf.at[:, 0:2]

        def sent(kind, condition):
            @pl.when(condition)
            def _():
                await_bytes(span, send_sem.at[kind])

        sent(0, x < 3)
        sent(1, x < 2)
        sent(2, y < 3)
        sent(3, y == 0)
        sent(4, x >= 1)
        sent(5, x >= 1)
        sent(6, jnp.logical_and(x >= 2, y == 3))
        sent(7, jnp.logical_and(x >= 2, y > 0))
        sent(8, chip >= right_fwd)
        sent(9, chip >= left_fwd)
        await_bytes(stage, send_sem.at[10])
        await_bytes(qbuf.at[0], send_sem.at[11])
        await_bytes(obuf.at[0], send_sem.at[12])
        await_bytes(obuf.at[0], out_sem.at[0])
        await_many(qd, dout.at[1])
        await_many(dr, dout.at[2])
        await_bytes(cs, dout.at[3])
        await_bytes(obuf.at[0], out_sem.at[1])
        finish_wait()

    @pl.when(role >= PG)
    def _():
        group = role - PG
        for p in range(PG):
            remote(dq.at[p], qz.at[group], dout.at[0], din.at[0], line(p)).start()
        pltpu.make_async_copy(w_hbm, wbuf, dlocal.at[0]).wait()
        await_bytes(dz, din.at[3])
        step = lax.broadcasted_iota(jnp.int32, (8, HD), 0) % 4
        tiles = []
        for p in range(PG):
            pair = dz[p, 1]
            m = jnp.broadcast_to(pair[:, 0:1], (8, HD))
            part = jnp.broadcast_to(pair[:, 64:65], (8, HD))
            q = dq[p]
            scores = []
            for t in range(4):
                s = jnp.sum(q * fresh[p, 0, t:t + 1, :], axis=1, keepdims=True)
                scores.append(jnp.where(step >= t, jnp.broadcast_to(s, (8, HD)), NEG))
            top = m
            for s in scores:
                top = jnp.maximum(top, s)
            old = jnp.exp2((m - top) * factor)
            total = part * old
            mixed = dz[p, 0] * old
            for t in range(4):
                w = jnp.exp2((scores[t] - top) * factor)
                total = total + w
                mixed = mixed + w * fresh[p, 1, t:t + 1, :]
            tiles.append(mixed / total)
        rows = jnp.concatenate(tiles, axis=0).astype(jnp.bfloat16)
        to = lax.broadcasted_iota(jnp.int32, (16, 32), 0)
        at = lax.broadcasted_iota(jnp.int32, (16, 32), 1)
        halves = []
        for h in range(2):
            chosen = (at == (to // 4) * 8 + h * 4 + to % 4).astype(jnp.bfloat16)
            halves.append(jnp.dot(chosen, rows, preferred_element_type=jnp.float32).astype(jnp.bfloat16))
        attended = jnp.concatenate(halves, axis=1)

        def project(i, carry):
            others = [(seq + 4 * i + d) % 32 for d in range(4)]
            for other in others:
                columns = pl.ds(pl.multiple_of(other * 256, 256), 256)
                rs_s[other] = jnp.dot(
                    attended, wbuf[:, columns], preferred_element_type=jnp.float32).astype(jnp.bfloat16)
            for other in others:
                @pl.when(other != seq)
                def _(other=other):
                    remote(rs_s.at[other], rs_r.at[seq], dout.at[4], din.at[4], plane(other)).start()

            return carry

        lax.fori_loop(0, 8, project, 0)
        rs_r[seq] = rs_s[seq]
        await_bytes(rs_r.at[0:31], din.at[4])

        def add(i, total):
            four = [rs_r[4 * i + d].astype(jnp.float32) for d in range(4)]
            return total + ((four[0] + four[1]) + (four[2] + four[3]))

        summed = lax.fori_loop(0, 8, add, jnp.zeros((16, 256), jnp.float32))
        fz[group] = summed.astype(jnp.bfloat16)
        for d in range(1, 2 * PG):
            remote(fz.at[group], fz.at[group], dout.at[5], din.at[5], line((role + d) % (2 * PG))).start()
        finish_own()
        finish_pair()
        await_bytes(qz, dout.at[0])
        await_bytes(rs_s.at[0:31], dout.at[4])
        await_bytes(fz.at[0:7], dout.at[5])
        for i in range(8):
            pltpu.make_async_copy(zbuf, out_hbm.at[:, i * 1024:(i + 1) * 1024], fill_sem.at[i]).wait()
        finish_wait()


def fused(prompt_lengths, decode_group, queries, kv, dq, fresh, out_weight):
    smem = pl.BlockSpec(memory_space=pltpu.SMEM)
    vmem = pl.BlockSpec(memory_space=pltpu.VMEM)
    hbm = pl.BlockSpec(memory_space=pl.ANY)
    return pl.pallas_call(
        fused_kernel,
        out_shape=[
            jax.ShapeDtypeStruct((BLOCK, H * HD), jnp.bfloat16),
            jax.ShapeDtypeStruct((16, 2, 64, 256), jnp.bfloat16),
        ],
        in_specs=[smem, smem, hbm, hbm, vmem, vmem, hbm],
        out_specs=[hbm, hbm],
        scratch_shapes=[
            pltpu.VMEM((2, 32, BLOCK, HD), jnp.bfloat16),
            pltpu.VMEM((HALF, 2 * SLOTS, 2, BLOCK, HD), jnp.bfloat16),
            pltpu.VMEM((BLOCK, 2 * KVH * HD), jnp.bfloat16),
            pltpu.VMEM((HALF, 2, BLOCK, HD), jnp.bfloat16),
            pltpu.VMEM((ROWS, WINDOW), jnp.float32),
            pltpu.VMEM((ROWS, WINDOW), jnp.float32),
            pltpu.VMEM((ROWS, 128), jnp.float32),
            pltpu.VMEM((ROWS, 128), jnp.float32),
            pltpu.VMEM((ROWS, 128), jnp.bfloat16),
            pltpu.VMEM((2, 128, WINDOW), jnp.bfloat16),
            pltpu.VMEM((2, 32, BLOCK, HD), jnp.bfloat16),
            pltpu.VMEM((BLOCK, 1024), jnp.bfloat16),
            pltpu.VMEM((256, 8192), jnp.bfloat16),
            pltpu.VMEM((PG, 8, HD), jnp.float32),
            pltpu.VMEM((32, HD), jnp.bfloat16),
            pltpu.VMEM((16, 32, HD), jnp.bfloat16),
            pltpu.VMEM((16, 3, 8, HD), jnp.float32),
            pltpu.VMEM((16, 3, 8, HD), jnp.float32),
            pltpu.VMEM((PG, 2, 8, HD), jnp.float32),
            pltpu.VMEM((PG, 2, 8, HD), jnp.float32),
            pltpu.VMEM((32, 16, 256), jnp.bfloat16),
            pltpu.VMEM((32, 16, 256), jnp.bfloat16),
            pltpu.VMEM((8, 16, 256), jnp.bfloat16),
            pltpu.VMEM((64, 256), jnp.bfloat16),
            pltpu.SemaphoreType.DMA((SLOTS, HALF)),
            pltpu.SemaphoreType.DMA((2,)),
            pltpu.SemaphoreType.DMA((HALF,)),
            pltpu.SemaphoreType.DMA((2,)),
            pltpu.SemaphoreType.DMA((8,)),
            pltpu.SemaphoreType.DMA((13,)),
            pltpu.SemaphoreType.DMA((8,)),
            pltpu.SemaphoreType.DMA((8,)),
            pltpu.SemaphoreType.DMA((2,)),
        ],
        compiler_params=pltpu.CompilerParams(
            collective_id=0, has_side_effects=True, vmem_limit_bytes=62 * 1024 * 1024
        ),
        cost_estimate=pl.CostEstimate(flops=17_000_000_000, bytes_accessed=16_000_000, transcendentals=17_000_000),
    )(prompt_lengths, decode_group, queries, kv, dq, fresh, out_weight)


def on_device(prefill_queries, prefill_kv, prompt_lengths, decode_group, decode_queries, decode_kv, out_weight):
    kv_head = lax.axis_index("seq") // (lax.axis_size("seq") // KVH)
    dq = decode_queries[0].reshape(4, PG, 2, HD).transpose(1, 2, 0, 3).reshape(PG, 8, HD).astype(jnp.float32)
    fresh = lax.dynamic_slice_in_dim(decode_kv[0], kv_head * 2 * HD, 2 * HD, 2)
    fresh = fresh.reshape(4, PG, 2, HD).transpose(1, 2, 0, 3).astype(jnp.float32)
    prefill_out, decode_out = fused(
        prompt_lengths, decode_group, prefill_queries[0], prefill_kv[0], dq, fresh, out_weight
    )
    decode_out = decode_out.reshape(32, 4, PG, PG, 256).transpose(1, 2, 3, 0, 4).reshape(4, PG, PG, -1)
    return prefill_out[None], decode_out


def solution(mesh):
    in_specs = (
        P("role", "seq", None),
        P("role", "seq", None),
        P(),
        P(),
        P("role", None, None, "seq"),
        P("role", None, None, None),
        P("seq", None),
    )
    out_specs = (P("role", "seq", None), P())
    return jax.shard_map(on_device, mesh=mesh, in_specs=in_specs, out_specs=out_specs, check_vma=False)
```

```python
import functools

import jax
import jax.numpy as jnp
from jax import lax
from jax.experimental import pallas as pl
from jax.experimental.pallas import tpu as pltpu
from jax.sharding import PartitionSpec as P

MESH = pl.DeviceIdType.MESH
H = 64
KVH = 8
HD = 128
BLOCK = 128
PG = 4
NEG = -1e30
SCALE = HD**-0.5
LOG2E = 1.4426950408889634
SLOTS = 9
HALF = KVH // 2
GROUP = H // KVH
ROWS = 512
KT = 512
WINDOW = 2048


def fused_kernel(
    lengths, serves, q_hbm, kv_hbm, dq, fresh, w_hbm, out_hbm, dec_hbm,
    qbuf, kvbuf, sbuf, sbuf1, peak0, peak1, eye, maskbuf, obuf, zbuf, wbuf, qz, qb, qd, ds, dr, cs, dz, rs_s, rs_r, fz, fo,
    slot_sem, q_sem, own_sem, out_sem, fill_sem, send_sem, din, dout, dlocal
):
    role = lax.axis_index("role")
    seq = lax.axis_index("seq")
    core = seq % 2
    chip = seq // 2
    y = chip % 4
    x = chip // 4
    home = seq // 16
    prefilling = role < PG
    factor = SCALE * LOG2E

    def plane(other):
        return (role, other)

    def line(other):
        return (other, seq)

    def remote(src, dst, send, recv, device):
        return pltpu.make_async_remote_copy(
            src_ref=src, dst_ref=dst, send_sem=send, recv_sem=recv, device_id=device, device_id_type=MESH)

    def await_bytes(ref, sem):
        pltpu.make_async_copy(ref, ref, sem).wait()

    def q_columns(half, h):
        return q_hbm.at[:, pl.ds(pl.multiple_of((half * 32 + h) * HD, HD), HD)]

    def kv_columns(half, j):
        return kv_hbm.at[:, pl.ds(pl.multiple_of(half * HALF * 256 + j * 256, 256), 256)]

    def chunk(slot, j):
        return kvbuf.at[j, pl.ds(pl.multiple_of((8 - slot) * 256, 256), 256), :]

    def own_rows(j):
        return kvbuf.at[j, pl.ds(pl.multiple_of(2048 + core * 128, 128), 128), :]

    barrier = pltpu.get_barrier_semaphore()

    def greet(d, carry):
        pl.semaphore_signal(barrier, inc=1, device_id=plane((seq + d) % 32), device_id_type=MESH)
        return carry

    lax.fori_loop(1, 32, greet, 0)

    @pl.when(prefilling)
    def _():
        for g in range(PG):
            pl.semaphore_signal(barrier, inc=1, device_id=line(PG + g), device_id_type=MESH)
        for j in range(HALF):
            pltpu.make_async_copy(kv_columns(core, j), own_rows(j), own_sem.at[j]).start()

        def keep_q(h, carry):
            pltpu.make_async_copy(q_columns(core, h), qbuf.at[core, h], q_sem.at[1]).start()
            return carry

        lax.fori_loop(0, 32, keep_q, 0)
        pl.semaphore_wait(barrier, 35)

    @pl.when(role >= PG)
    def _():
        for d in range(1, 2 * PG):
            pl.semaphore_signal(barrier, inc=1, device_id=line((role + d) % (2 * PG)), device_id_type=MESH)
        pltpu.make_async_copy(w_hbm, wbuf, dlocal.at[0]).start()
        zbuf[...] = jnp.zeros_like(zbuf)
        for i in range(8):
            pltpu.make_async_copy(zbuf, out_hbm.at[:, i * 1024:(i + 1) * 1024], fill_sem.at[i]).start()
        pl.semaphore_wait(barrier, 38)

    mine = dec_hbm.at[chip, core]

    sibling = plane(seq + 1 - 2 * core)

    def finish_own():
        await_first = prefilling

        @pl.when(await_first)
        def _():
            await_bytes(fz.at[0:4], din.at[5])

        @pl.when(jnp.logical_not(await_first))
        def _():
            await_bytes(fz.at[0:3], din.at[5])

        to = lax.broadcasted_iota(jnp.int32, (64, 64), 0)
        at = lax.broadcasted_iota(jnp.int32, (64, 64), 1)
        order = (at == ((to // 4) % 4) * 16 + (to % 4) * 4 + to // 16).astype(jnp.bfloat16)
        slab = jnp.dot(order, fz[0:4].reshape(64, 256), preferred_element_type=jnp.float32)
        fo[...] = slab.astype(jnp.bfloat16)
        pltpu.make_async_copy(fo, mine, dlocal.at[1]).start()

        def spread(d, carry):
            other = ((chip + d) % 16) * 2 + core
            remote(fo, mine, dout.at[6], din.at[6], plane(other)).start()
            return carry

        lax.fori_loop(1, 16, spread, 0)

    def finish_pair():
        pltpu.make_async_copy(fo, mine, dlocal.at[1]).wait()
        await_bytes(dec_hbm.at[0:15, 0], din.at[6])
        remote(dec_hbm.at[:, core], dec_hbm.at[:, core], dout.at[7], din.at[7], sibling).start()

    def finish_wait():
        await_bytes(dec_hbm.at[0:15, 0], dout.at[6])
        await_bytes(dec_hbm.at[:, 0], dout.at[7])
        await_bytes(dec_hbm.at[:, 0], din.at[7])

    @pl.when(prefilling)
    def _():
        right, left = (y + 1) % 4, (y + 3) % 4

        def device(xx, yy):
            return plane((xx * 4 + yy) * 2 + core)

        for j in range(HALF):
            remote(kv_columns(1 - core, j), own_rows(j), send_sem.at[10], slot_sem.at[0, j], sibling).start()

        def wait_slot(slot, j):
            @pl.when(chip >= slot)
            def _():
                await_bytes(chunk(slot, j), slot_sem.at[slot, j])

        def send(kind, src, dst, j, xx, yy):
            remote(chunk(src, j), chunk(dst, j), send_sem.at[kind], slot_sem.at[dst, j], device(xx, yy)).start()

        def own_wait(j):
            pltpu.make_async_copy(kv_columns(core, j), own_rows(j), own_sem.at[j]).wait()
            await_bytes(own_rows(j), slot_sem.at[0, j])

        def own(j):
            @pl.when(x < 3)
            def _():
                send(0, 0, 4, j, (x + 1) % 4, y)

            @pl.when(x < 2)
            def _():
                send(1, 0, 8, j, (x + 2) % 4, y)

        def own_along_y(j):
            @pl.when(y < 3)
            def _():
                send(2, 0, 1, j, x, right)

            @pl.when(y == 0)
            def _():
                send(3, 0, 3, j, x, left)

        right_dst = jnp.where(y < 3, 5, 1)
        left_dst = jnp.where(y > 0, 3, 7)
        right_fwd = jnp.where(y < 3, 1, 5)
        left_fwd = jnp.where(y > 0, 7, 3)

        def inject(j):
            wait_slot(4, j)

            @pl.when(x >= 1)
            def _():
                send(4, 4, right_dst, j, x, right)
                send(5, 4, left_dst, j, x, left)

            wait_slot(8, j)

            @pl.when(jnp.logical_and(x >= 2, y == 3))
            def _():
                send(6, 8, 5, j, x, right)

            @pl.when(jnp.logical_and(x >= 2, y > 0))
            def _():
                send(7, 8, 7, j, x, left)

        def forward(j):
            wait_slot(right_fwd, j)

            @pl.when(chip >= right_fwd)
            def _():
                send(8, right_fwd, 2, j, x, right)

            wait_slot(left_fwd, j)

            @pl.when(chip >= left_fwd)
            def _():
                send(9, left_fwd, 6, j, x, left)

        def rest(j):
            wait_slot(6 - right_fwd, j)
            wait_slot(10 - left_fwd, j)
            wait_slot(2, j)
            wait_slot(6, j)

        counts = [lengths[role, i] for i in range(4)]
        served = [serves[role, i] for i in range(4)]
        blocks = [(n + 127) // 128 for n in counts]
        starts = [0, blocks[0], blocks[0] + blocks[1], blocks[0] + blocks[1] + blocks[2]]

        def pick(block, values):
            chosen = values[0]
            for i in range(1, 4):
                chosen = jnp.where(block >= starts[i], values[i], chosen)
            return chosen

        firsts, lives = [], []
        for e in range(2):
            block = 2 * chip + e
            first = pick(block, starts)
            firsts.append(first - (2 * chip - 15 + e))
            lives.append(pick(block, counts) - (block - first) * 128)

        at_home = home == core

        def spread_queries():
            await_bytes(qz, din.at[0])
            qb[...] = qz[...].reshape(32, HD).astype(jnp.bfloat16)

            @pl.when(at_home)
            def _():
                qd[seq % 16] = qb[...]

            def one(d, carry):
                other = ((chip + d) % 16) * 2 + home

                @pl.when(other != seq)
                def _():
                    remote(qb, qd.at[seq % 16], dout.at[1], din.at[1], plane(other)).start()

                return carry

            lax.fori_loop(0, 16, one, 0)

        def await_many(buffer, sem):
            @pl.when(at_home)
            def _():
                await_bytes(buffer.at[0:15], sem)

            @pl.when(jnp.logical_not(at_home))
            def _():
                await_bytes(buffer, sem)

        lanes = lax.broadcasted_iota(jnp.int32, (32, HD), 1)

        def partial_terms():
            await_many(qd, din.at[1])
            stats = []
            for e in range(2):
                group = pick(2 * chip + e, served)
                live = lives[e]

                for j in range(HALF):
                    q = jnp.zeros((4, 8, HD), jnp.float32)
                    wide = qd[4 * j:4 * j + 4].astype(jnp.float32).reshape(4, PG, 8, HD)
                    for g in range(PG):
                        q = jnp.where(group == g, wide[:, g], q)
                    q = q.reshape(32, HD).astype(jnp.bfloat16)
                    keys = kvbuf[j, 2048 + 128 * e:2176 + 128 * e, 0:HD]
                    values = kvbuf[j, 2048 + 128 * e:2176 + 128 * e, HD:2 * HD]
                    s = lax.dot_general(q, keys, (((1,), (1,)), ((), ())), preferred_element_type=jnp.float32)
                    s = jnp.where(lanes < live, s, NEG)
                    m = jnp.max(s, axis=1, keepdims=True)
                    w = jnp.exp2((s - m) * factor)
                    total = jnp.sum(w, axis=1, keepdims=True)
                    o = jnp.dot(w.astype(jnp.bfloat16), values, preferred_element_type=jnp.float32)
                    ds[4 * j:4 * j + 4, e] = o.reshape(4, 8, HD)
                    stat = jnp.where(lanes < 64, m, total)
                    if e == 0:
                        stats.append(stat)
                    else:
                        stat = jnp.where(lanes % 64 < 32, stats[j], stat)
                        ds[4 * j:4 * j + 4, 2] = stat.reshape(4, 8, HD)

            @pl.when(at_home)
            def _():
                dr[chip] = ds[seq % 16]

            def out(d, carry):
                other = 16 * core + (chip + d) % 16

                @pl.when(other != seq)
                def _():
                    remote(ds.at[(chip + d) % 16], dr.at[chip], dout.at[2], din.at[2], plane(other)).start()

                return carry

            lax.fori_loop(0, 16, out, 0)

        which = lax.broadcasted_iota(jnp.int32, (PG, 8, HD), 0)

        def combine_terms():
            await_many(dr, din.at[2])

            terms = []
            top = jnp.full((PG, 8, HD), NEG, jnp.float32)
            for b in range(32):
                flag = which == pick(jnp.int32(b), served)
                m = jnp.broadcast_to(dr[b // 2, 2][:, 32 * (b % 2):32 * (b % 2) + 1], (8, HD))[None]
                top = jnp.maximum(top, jnp.where(flag, m, NEG))
                terms.append((flag, m))
            total = jnp.zeros((PG, 8, HD), jnp.float32)
            mixed = jnp.zeros((PG, 8, HD), jnp.float32)
            for b in range(32):
                flag, m = terms[b]
                part = jnp.broadcast_to(dr[b // 2, 2][:, 64 + 32 * (b % 2):65 + 32 * (b % 2)], (8, HD))[None]
                add = jnp.where(flag, jnp.exp2((jnp.minimum(m, top) - top) * factor), 0.0)
                total = total + add * part
                mixed = mixed + add * dr[b // 2, b % 2][None]
            lane3 = lax.broadcasted_iota(jnp.int32, (PG, 8, HD), 2)
            cs[:, 0] = mixed
            cs[:, 1] = jnp.where(lane3 < 64, top, total)
            for g in range(PG):
                remote(cs.at[g], dz.at[role], dout.at[3], din.at[3], line(PG + g)).start()

        own_wait(0)
        own(0)

        own_along_y(0)

        for slot in range(1, SLOTS):
            @pl.when(chip < slot)
            def _(slot=slot):
                for j in range(HALF):
                    kvbuf[j, (8 - slot) * 256:(9 - slot) * 256, :] = jnp.zeros((256, 256), jnp.bfloat16)

        at = lax.broadcasted_iota(jnp.int32, (128, 128), 0)
        to = lax.broadcasted_iota(jnp.int32, (128, 128), 1)
        for i in range(ROWS // 128):
            eye[i * 128:(i + 1) * 128, :] = (at == to).astype(jnp.bfloat16)
        for e in range(2):
            for w in range(15):
                level = jnp.where(firsts[e] <= w, 0.0, NEG)
                maskbuf[e, w * 128:(w + 1) * 128, :] = jnp.full((128, 128), level, jnp.float32).astype(jnp.bfloat16)
            maskbuf[e, 1920:2048, :] = jnp.where(at <= to, 0.0, NEG).astype(jnp.bfloat16)

        spread_queries()

        def start_q(h, carry):
            remote(q_columns(1 - core, h), qbuf.at[core, h], send_sem.at[11], q_sem.at[0], sibling).start()
            return carry

        lax.fori_loop(0, 32, start_q, 0)
        inject(0)
        for j in range(1, HALF):
            own_wait(j)
        own(1)
        own_along_y(1)
        partial_terms()
        forward(0)
        inject(1)
        own(2)
        own_along_y(2)
        combine_terms()
        rest(0)

        await_bytes(qbuf.at[0], q_sem.at[0])
        await_bytes(qbuf.at[0], q_sem.at[1])

        row_in = lax.broadcasted_iota(jnp.int32, (ROWS, 128), 0) & 127
        ones = jnp.ones((KT, HD), jnp.bfloat16)

        def place(n):
            j, u = n // 4, n % 4
            return j, u // 2, j * GROUP + (u % 2) * 4

        def key_rows(j, e, kt):
            return j, pl.ds(pl.multiple_of(128 + e * 128 + kt * KT, 128), KT)

        def weave(current, following):
            if following is not None:
                n, scores, peaks = following
                j, e, base = place(n)
                q = jnp.concatenate([qbuf[e, pl.ds(base, 4)].reshape(ROWS, HD), eye[...]], axis=1)
                peak = None
            if current is not None:
                cn, cscores, cpeaks = current
                cj, ce, cbase = place(cn)
                total = None
            for kt in range(WINDOW // KT):
                if following is not None:
                    rows = key_rows(j, e, kt)
                    masked_keys = jnp.concatenate(
                        [kvbuf[rows[0], rows[1], 0:HD], maskbuf[e, kt * KT:(kt + 1) * KT, :]], axis=1)
                    s = lax.dot_general(
                        q, masked_keys, (((1,), (1,)), ((), ())), preferred_element_type=jnp.float32)
                if current is not None:
                    weights = [
                        jnp.exp2((cscores[:, kt * KT + i * 128:kt * KT + (i + 1) * 128] - cpeaks[...]) * factor)
                        for i in range(KT // 128)
                    ]
                    rows = key_rows(cj, ce, kt)
                    product = jnp.dot(
                        jnp.concatenate(weights, axis=1).astype(jnp.bfloat16),
                        jnp.concatenate([kvbuf[rows[0], rows[1], HD:2 * HD], ones], axis=1),
                        preferred_element_type=jnp.float32)
                    total = product if total is None else total + product
                if following is not None:
                    pieces = [s[:, i * 128:(i + 1) * 128] for i in range(KT // 128)]
                    for i, piece in enumerate(pieces):
                        scores[:, kt * KT + i * 128:kt * KT + (i + 1) * 128] = piece
                    while len(pieces) > 1:
                        pieces = [jnp.maximum(a, b) for a, b in zip(pieces[::2], pieces[1::2])]
                    peak = pieces[0] if peak is None else jnp.maximum(peak, pieces[0])
            if following is not None:
                peaks[...] = jnp.broadcast_to(jnp.max(peak, axis=1, keepdims=True), (ROWS, 128))
            if current is not None:
                live = jnp.where(ce == 0, lives[0], lives[1])
                mixed = total[:, :HD] / total[:, HD:]
                mixed = jnp.where(row_in < live, mixed, 0.0).astype(jnp.bfloat16)
                obuf[ce, pl.ds(cbase, 4)] = mixed.reshape(4, BLOCK, HD)
                for i in range(4):
                    columns = out_hbm.at[:, pl.ds(pl.multiple_of((core * 32 + cbase + i) * HD, HD), HD)]

                    @pl.when(ce == core)
                    def _(i=i, columns=columns):
                        pltpu.make_async_copy(obuf.at[ce, cbase + i], columns, out_sem.at[0]).start()

                    @pl.when(ce != core)
                    def _(i=i, columns=columns):
                        remote(obuf.at[ce, cbase + i], columns, send_sem.at[12], out_sem.at[1], sibling).start()

        weave(None, (jnp.int32(0), sbuf, peak0))

        def pair(i, carry):
            j = i // 2
            weave((2 * i, sbuf, peak0), (2 * i + 1, sbuf1, peak1))

            @pl.when(i == 0)
            def _():
                inject(2)
                own(3)
                own_along_y(3)

            @pl.when(i == 1)
            def _():
                inject(3)
                rest(1)

            @pl.when(i == 3)
            def _():
                rest(2)

            @pl.when(i == 5)
            def _():
                rest(3)

            @pl.when(i == 6)
            def _():
                finish_own()

            weave((2 * i + 1, sbuf1, peak1), (2 * i + 2, sbuf, peak0))

            @pl.when(i < HALF - 1)
            def _():
                forward(i + 1)

            return carry

        lax.fori_loop(0, 7, pair, 0)
        weave((jnp.int32(14), sbuf, peak0), (jnp.int32(15), sbuf1, peak1))
        finish_pair()
        weave((jnp.int32(15), sbuf1, peak1), None)

        span = kvbuf.at[:, 0:256, :]

        def sent(kind, condition):
            @pl.when(condition)
            def _():
                await_bytes(span, send_sem.at[kind])

        sent(0, x < 3)
        sent(1, x < 2)
        sent(2, y < 3)
        sent(3, y == 0)
        sent(4, x >= 1)
        sent(5, x >= 1)
        sent(6, jnp.logical_and(x >= 2, y == 3))
        sent(7, jnp.logical_and(x >= 2, y > 0))
        sent(8, chip >= right_fwd)
        sent(9, chip >= left_fwd)
        await_bytes(kvbuf.at[:, 0:128, :], send_sem.at[10])
        await_bytes(qbuf.at[0], send_sem.at[11])
        await_bytes(obuf.at[0], send_sem.at[12])
        await_bytes(obuf.at[0], out_sem.at[0])
        await_many(qd, dout.at[1])
        await_many(dr, dout.at[2])
        await_bytes(cs, dout.at[3])
        await_bytes(obuf.at[0], out_sem.at[1])
        finish_wait()

    @pl.when(role >= PG)
    def _():
        group = role - PG
        for p in range(PG):
            remote(dq.at[p], qz.at[group], dout.at[0], din.at[0], line(p)).start()
        pltpu.make_async_copy(w_hbm, wbuf, dlocal.at[0]).wait()
        await_bytes(dz, din.at[3])
        step = lax.broadcasted_iota(jnp.int32, (8, HD), 0) % 4
        tiles = []
        for p in range(PG):
            pair = dz[p, 1]
            m = jnp.broadcast_to(pair[:, 0:1], (8, HD))
            part = jnp.broadcast_to(pair[:, 64:65], (8, HD))
            q = dq[p]
            scores = []
            for t in range(4):
                s = jnp.sum(q * fresh[p, 0, t:t + 1, :], axis=1, keepdims=True)
                scores.append(jnp.where(step >= t, jnp.broadcast_to(s, (8, HD)), NEG))
            top = m
            for s in scores:
                top = jnp.maximum(top, s)
            old = jnp.exp2((m - top) * factor)
            total = part * old
            mixed = dz[p, 0] * old
            for t in range(4):
                w = jnp.exp2((scores[t] - top) * factor)
                total = total + w
                mixed = mixed + w * fresh[p, 1, t:t + 1, :]
            tiles.append(mixed / total)
        rows = jnp.concatenate(tiles, axis=0).astype(jnp.bfloat16)
        to = lax.broadcasted_iota(jnp.int32, (16, 32), 0)
        at = lax.broadcasted_iota(jnp.int32, (16, 32), 1)
        halves = []
        for h in range(2):
            chosen = (at == (to // 4) * 8 + h * 4 + to % 4).astype(jnp.bfloat16)
            halves.append(jnp.dot(chosen, rows, preferred_element_type=jnp.float32).astype(jnp.bfloat16))
        attended = jnp.concatenate(halves, axis=1)

        def project(i, carry):
            others = [(seq + 4 * i + d) % 32 for d in range(4)]
            for other in others:
                columns = pl.ds(pl.multiple_of(other * 256, 256), 256)
                rs_s[other] = jnp.dot(
                    attended, wbuf[:, columns], preferred_element_type=jnp.float32).astype(jnp.bfloat16)
            for other in others:
                @pl.when(other != seq)
                def _(other=other):
                    remote(rs_s.at[other], rs_r.at[seq], dout.at[4], din.at[4], plane(other)).start()

            return carry

        lax.fori_loop(0, 8, project, 0)
        rs_r[seq] = rs_s[seq]
        await_bytes(rs_r.at[0:31], din.at[4])

        def add(i, total):
            four = [rs_r[4 * i + d].astype(jnp.float32) for d in range(4)]
            return total + ((four[0] + four[1]) + (four[2] + four[3]))

        summed = lax.fori_loop(0, 8, add, jnp.zeros((16, 256), jnp.float32))
        fz[group] = summed.astype(jnp.bfloat16)
        for d in range(1, 2 * PG):
            remote(fz.at[group], fz.at[group], dout.at[5], din.at[5], line((role + d) % (2 * PG))).start()
        finish_own()
        finish_pair()
        await_bytes(qz, dout.at[0])
        await_bytes(rs_s.at[0:31], dout.at[4])
        await_bytes(fz.at[0:7], dout.at[5])
        for i in range(8):
            pltpu.make_async_copy(zbuf, out_hbm.at[:, i * 1024:(i + 1) * 1024], fill_sem.at[i]).wait()
        finish_wait()


def fused(prompt_lengths, decode_group, queries, kv, dq, fresh, out_weight):
    smem = pl.BlockSpec(memory_space=pltpu.SMEM)
    vmem = pl.BlockSpec(memory_space=pltpu.VMEM)
    hbm = pl.BlockSpec(memory_space=pl.ANY)
    return pl.pallas_call(
        fused_kernel,
        out_shape=[
            jax.ShapeDtypeStruct((BLOCK, H * HD), jnp.bfloat16),
            jax.ShapeDtypeStruct((16, 2, 64, 256), jnp.bfloat16),
        ],
        in_specs=[smem, smem, hbm, hbm, vmem, vmem, hbm],
        out_specs=[hbm, hbm],
        scratch_shapes=[
            pltpu.VMEM((2, 32, BLOCK, HD), jnp.bfloat16),
            pltpu.VMEM((HALF, SLOTS * 256, 256), jnp.bfloat16),
            pltpu.VMEM((ROWS, WINDOW), jnp.float32),
            pltpu.VMEM((ROWS, WINDOW), jnp.float32),
            pltpu.VMEM((ROWS, 128), jnp.float32),
            pltpu.VMEM((ROWS, 128), jnp.float32),
            pltpu.VMEM((ROWS, 128), jnp.bfloat16),
            pltpu.VMEM((2, WINDOW, 128), jnp.bfloat16),
            pltpu.VMEM((2, 32, BLOCK, HD), jnp.bfloat16),
            pltpu.VMEM((BLOCK, 1024), jnp.bfloat16),
            pltpu.VMEM((256, 8192), jnp.bfloat16),
            pltpu.VMEM((PG, 8, HD), jnp.float32),
            pltpu.VMEM((32, HD), jnp.bfloat16),
            pltpu.VMEM((16, 32, HD), jnp.bfloat16),
            pltpu.VMEM((16, 3, 8, HD), jnp.float32),
            pltpu.VMEM((16, 3, 8, HD), jnp.float32),
            pltpu.VMEM((PG, 2, 8, HD), jnp.float32),
            pltpu.VMEM((PG, 2, 8, HD), jnp.float32),
            pltpu.VMEM((32, 16, 256), jnp.bfloat16),
            pltpu.VMEM((32, 16, 256), jnp.bfloat16),
            pltpu.VMEM((8, 16, 256), jnp.bfloat16),
            pltpu.VMEM((64, 256), jnp.bfloat16),
            pltpu.SemaphoreType.DMA((SLOTS, HALF)),
            pltpu.SemaphoreType.DMA((2,)),
            pltpu.SemaphoreType.DMA((HALF,)),
            pltpu.SemaphoreType.DMA((2,)),
            pltpu.SemaphoreType.DMA((8,)),
            pltpu.SemaphoreType.DMA((13,)),
            pltpu.SemaphoreType.DMA((8,)),
            pltpu.SemaphoreType.DMA((8,)),
            pltpu.SemaphoreType.DMA((2,)),
        ],
        compiler_params=pltpu.CompilerParams(
            collective_id=0, has_side_effects=True, vmem_limit_bytes=62 * 1024 * 1024
        ),
        cost_estimate=pl.CostEstimate(flops=17_000_000_000, bytes_accessed=16_000_000, transcendentals=17_000_000),
    )(prompt_lengths, decode_group, queries, kv, dq, fresh, out_weight)


def on_device(prefill_queries, prefill_kv, prompt_lengths, decode_group, decode_queries, decode_kv, out_weight):
    kv_head = lax.axis_index("seq") // (lax.axis_size("seq") // KVH)
    dq = decode_queries[0].reshape(4, PG, 2, HD).transpose(1, 2, 0, 3).reshape(PG, 8, HD).astype(jnp.float32)
    fresh = lax.dynamic_slice_in_dim(decode_kv[0], kv_head * 2 * HD, 2 * HD, 2)
    fresh = fresh.reshape(4, PG, 2, HD).transpose(1, 2, 0, 3).astype(jnp.float32)
    prefill_out, decode_out = fused(
        prompt_lengths, decode_group, prefill_queries[0], prefill_kv[0], dq, fresh, out_weight
    )
    decode_out = decode_out.reshape(32, 4, PG, PG, 256).transpose(1, 2, 3, 0, 4).reshape(4, PG, PG, -1)
    return prefill_out[None], decode_out


def solution(mesh):
    in_specs = (
        P("role", "seq", None),
        P("role", "seq", None),
        P(),
        P(),
        P("role", None, None, "seq"),
        P("role", None, None, None),
        P("seq", None),
    )
    out_specs = (P("role", "seq", None), P())
    return jax.shard_map(on_device, mesh=mesh, in_specs=in_specs, out_specs=out_specs, check_vma=False)
```

```python
import functools

import jax
import jax.numpy as jnp
from jax import lax
from jax.experimental import pallas as pl
from jax.experimental.pallas import tpu as pltpu
from jax.sharding import PartitionSpec as P

MESH = pl.DeviceIdType.MESH
H = 64
KVH = 8
HD = 128
BLOCK = 128
PG = 4
NEG = -1e30
SCALE = HD**-0.5
LOG2E = 1.4426950408889634
SLOTS = 9
HALF = KVH // 2
GROUP = H // KVH
ROWS = 512
KT = 1024
WINDOW = 2048


def fused_kernel(
    lengths, serves, q_hbm, kv_hbm, raw_q, raw_kv, w_hbm, out_hbm, dec_hbm,
    qbuf, kvbuf, sbuf, sbuf1, peak0, peak1, eye, maskbuf, obuf, zbuf, wbuf, dq, qz, qb, qd, ds, dr, cs, dz, rs_s, rs_r, fz, fo,
    slot_sem, q_sem, own_sem, out_sem, fill_sem, send_sem, din, dout, dlocal
):
    role = lax.axis_index("role")
    seq = lax.axis_index("seq")
    core = seq % 2
    chip = seq // 2
    y = chip % 4
    x = chip // 4
    home = seq // 16
    prefilling = role < PG
    factor = SCALE * LOG2E

    def plane(other):
        return (role, other)

    def line(other):
        return (other, seq)

    def remote(src, dst, send, recv, device):
        return pltpu.make_async_remote_copy(
            src_ref=src, dst_ref=dst, send_sem=send, recv_sem=recv, device_id=device, device_id_type=MESH)

    def await_bytes(ref, sem):
        pltpu.make_async_copy(ref, ref, sem).wait()

    def q_columns(half, h):
        return q_hbm.at[:, pl.ds(pl.multiple_of((half * 32 + h) * HD, HD), HD)]

    def kv_columns(half, j):
        return kv_hbm.at[:, pl.ds(pl.multiple_of(half * HALF * 256 + j * 256, 256), 256)]

    def chunk(slot, j):
        return kvbuf.at[j, pl.ds(pl.multiple_of((8 - slot) * 256, 256), 256), :]

    def own_rows(j):
        return kvbuf.at[j, pl.ds(pl.multiple_of(2048 + core * 128, 128), 128), :]

    barrier = pltpu.get_barrier_semaphore()

    def greet(d, carry):
        pl.semaphore_signal(barrier, inc=1, device_id=plane((seq + d) % 32), device_id_type=MESH)
        return carry

    lax.fori_loop(1, 32, greet, 0)

    @pl.when(prefilling)
    def _():
        for g in range(PG):
            pl.semaphore_signal(barrier, inc=1, device_id=line(PG + g), device_id_type=MESH)
        for j in range(HALF):
            pltpu.make_async_copy(kv_columns(core, j), own_rows(j), own_sem.at[j]).start()

        def keep_q(h, carry):
            pltpu.make_async_copy(q_columns(core, h), qbuf.at[core, h], q_sem.at[1]).start()
            return carry

        lax.fori_loop(0, 32, keep_q, 0)
        pl.semaphore_wait(barrier, 35)

    @pl.when(role >= PG)
    def _():
        for d in range(1, 2 * PG):
            pl.semaphore_signal(barrier, inc=1, device_id=line((role + d) % (2 * PG)), device_id_type=MESH)
        pltpu.make_async_copy(w_hbm, wbuf, dlocal.at[0]).start()
        zbuf[...] = jnp.zeros_like(zbuf)
        for i in range(8):
            pltpu.make_async_copy(zbuf, out_hbm.at[:, i * 1024:(i + 1) * 1024], fill_sem.at[i]).start()
        pl.semaphore_wait(barrier, 38)

    mine = dec_hbm.at[chip, core]

    sibling = plane(seq + 1 - 2 * core)

    def finish_own():
        await_first = prefilling

        @pl.when(await_first)
        def _():
            await_bytes(fz.at[0:4], din.at[5])

        @pl.when(jnp.logical_not(await_first))
        def _():
            await_bytes(fz.at[0:3], din.at[5])

        to = lax.broadcasted_iota(jnp.int32, (64, 64), 0)
        at = lax.broadcasted_iota(jnp.int32, (64, 64), 1)
        order = (at == ((to // 4) % 4) * 16 + (to % 4) * 4 + to // 16).astype(jnp.bfloat16)
        slab = jnp.dot(order, fz[0:4].reshape(64, 256), preferred_element_type=jnp.float32)
        for i in range(16):
            fo[i // 4, i % 4] = slab[4 * i:4 * i + 4].astype(jnp.bfloat16)
        pltpu.make_async_copy(fo, mine, dlocal.at[1]).start()

        def spread(d, carry):
            other = ((chip + d) % 16) * 2 + core
            remote(fo, mine, dout.at[6], din.at[6], plane(other)).start()
            return carry

        lax.fori_loop(1, 16, spread, 0)

    def finish_pair():
        pltpu.make_async_copy(fo, mine, dlocal.at[1]).wait()
        await_bytes(dec_hbm.at[0:15, 0], din.at[6])
        remote(dec_hbm.at[:, core], dec_hbm.at[:, core], dout.at[7], din.at[7], sibling).start()

    def finish_wait():
        await_bytes(dec_hbm.at[0:15, 0], dout.at[6])
        await_bytes(dec_hbm.at[:, 0], dout.at[7])
        await_bytes(dec_hbm.at[:, 0], din.at[7])

    @pl.when(prefilling)
    def _():
        right, left = (y + 1) % 4, (y + 3) % 4

        def device(xx, yy):
            return plane((xx * 4 + yy) * 2 + core)

        for j in range(HALF):
            remote(kv_columns(1 - core, j), own_rows(j), send_sem.at[10], slot_sem.at[0, j], sibling).start()

        def wait_slot(slot, j):
            @pl.when(chip >= slot)
            def _():
                await_bytes(chunk(slot, j), slot_sem.at[slot, j])

        def send(kind, src, dst, j, xx, yy):
            remote(chunk(src, j), chunk(dst, j), send_sem.at[kind], slot_sem.at[dst, j], device(xx, yy)).start()

        def own_wait(j):
            pltpu.make_async_copy(kv_columns(core, j), own_rows(j), own_sem.at[j]).wait()
            await_bytes(own_rows(j), slot_sem.at[0, j])

        def own(j):
            @pl.when(x < 3)
            def _():
                send(0, 0, 4, j, (x + 1) % 4, y)

            @pl.when(x < 2)
            def _():
                send(1, 0, 8, j, (x + 2) % 4, y)

        def own_along_y(j):
            @pl.when(y < 3)
            def _():
                send(2, 0, 1, j, x, right)

            @pl.when(y == 0)
            def _():
                send(3, 0, 3, j, x, left)

        right_dst = jnp.where(y < 3, 5, 1)
        left_dst = jnp.where(y > 0, 3, 7)
        right_fwd = jnp.where(y < 3, 1, 5)
        left_fwd = jnp.where(y > 0, 7, 3)

        def inject(j):
            wait_slot(4, j)

            @pl.when(x >= 1)
            def _():
                send(4, 4, right_dst, j, x, right)
                send(5, 4, left_dst, j, x, left)

            wait_slot(8, j)

            @pl.when(jnp.logical_and(x >= 2, y == 3))
            def _():
                send(6, 8, 5, j, x, right)

            @pl.when(jnp.logical_and(x >= 2, y > 0))
            def _():
                send(7, 8, 7, j, x, left)

        def forward(j):
            wait_slot(right_fwd, j)

            @pl.when(chip >= right_fwd)
            def _():
                send(8, right_fwd, 2, j, x, right)

            wait_slot(left_fwd, j)

            @pl.when(chip >= left_fwd)
            def _():
                send(9, left_fwd, 6, j, x, left)

        def rest(j):
            wait_slot(6 - right_fwd, j)
            wait_slot(10 - left_fwd, j)
            wait_slot(2, j)
            wait_slot(6, j)

        counts = [lengths[role, i] for i in range(4)]
        served = [serves[role, i] for i in range(4)]
        blocks = [(n + 127) // 128 for n in counts]
        starts = [0, blocks[0], blocks[0] + blocks[1], blocks[0] + blocks[1] + blocks[2]]

        def pick(block, values):
            chosen = values[0]
            for i in range(1, 4):
                chosen = jnp.where(block >= starts[i], values[i], chosen)
            return chosen

        firsts, lives = [], []
        for e in range(2):
            block = 2 * chip + e
            first = pick(block, starts)
            firsts.append(first - (2 * chip - 15 + e))
            lives.append(pick(block, counts) - (block - first) * 128)

        at_home = home == core

        def spread_queries():
            await_bytes(qz, din.at[0])
            qb[...] = qz[...].reshape(32, HD).astype(jnp.bfloat16)

            @pl.when(at_home)
            def _():
                qd[seq % 16] = qb[...]

            def one(d, carry):
                other = ((chip + d) % 16) * 2 + home

                @pl.when(other != seq)
                def _():
                    remote(qb, qd.at[seq % 16], dout.at[1], din.at[1], plane(other)).start()

                return carry

            lax.fori_loop(0, 16, one, 0)

        def await_many(buffer, sem):
            @pl.when(at_home)
            def _():
                await_bytes(buffer.at[0:15], sem)

            @pl.when(jnp.logical_not(at_home))
            def _():
                await_bytes(buffer, sem)

        lanes = lax.broadcasted_iota(jnp.int32, (32, HD), 1)

        def partial_terms():
            await_many(qd, din.at[1])
            stats = []
            for e in range(2):
                group = pick(2 * chip + e, served)
                live = lives[e]

                for j in range(HALF):
                    q = jnp.zeros((4, 8, HD), jnp.float32)
                    wide = qd[4 * j:4 * j + 4].astype(jnp.float32).reshape(4, PG, 8, HD)
                    for g in range(PG):
                        q = jnp.where(group == g, wide[:, g], q)
                    q = q.reshape(32, HD).astype(jnp.bfloat16)
                    keys = kvbuf[j, 2048 + 128 * e:2176 + 128 * e, 0:HD]
                    values = kvbuf[j, 2048 + 128 * e:2176 + 128 * e, HD:2 * HD]
                    s = lax.dot_general(q, keys, (((1,), (1,)), ((), ())), preferred_element_type=jnp.float32)
                    s = jnp.where(lanes < live, s, NEG)
                    m = jnp.max(s, axis=1, keepdims=True)
                    w = jnp.exp2((s - m) * factor)
                    total = jnp.sum(w, axis=1, keepdims=True)
                    o = jnp.dot(w.astype(jnp.bfloat16), values, preferred_element_type=jnp.float32)
                    ds[4 * j:4 * j + 4, e] = o.reshape(4, 8, HD)
                    stat = jnp.where(lanes < 64, m, total)
                    if e == 0:
                        stats.append(stat)
                    else:
                        stat = jnp.where(lanes % 64 < 32, stats[j], stat)
                        ds[4 * j:4 * j + 4, 2] = stat.reshape(4, 8, HD)

            @pl.when(at_home)
            def _():
                dr[chip] = ds[seq % 16]

            def out(d, carry):
                other = 16 * core + (chip + d) % 16

                @pl.when(other != seq)
                def _():
                    remote(ds.at[(chip + d) % 16], dr.at[chip], dout.at[2], din.at[2], plane(other)).start()

                return carry

            lax.fori_loop(0, 16, out, 0)

        which = lax.broadcasted_iota(jnp.int32, (PG, 8, HD), 0)

        def combine_terms():
            await_many(dr, din.at[2])

            terms = []
            top = jnp.full((PG, 8, HD), NEG, jnp.float32)
            for b in range(32):
                flag = which == pick(jnp.int32(b), served)
                m = jnp.broadcast_to(dr[b // 2, 2][:, 32 * (b % 2):32 * (b % 2) + 1], (8, HD))[None]
                top = jnp.maximum(top, jnp.where(flag, m, NEG))
                terms.append((flag, m))
            total = jnp.zeros((PG, 8, HD), jnp.float32)
            mixed = jnp.zeros((PG, 8, HD), jnp.float32)
            for b in range(32):
                flag, m = terms[b]
                part = jnp.broadcast_to(dr[b // 2, 2][:, 64 + 32 * (b % 2):65 + 32 * (b % 2)], (8, HD))[None]
                add = jnp.where(flag, jnp.exp2((jnp.minimum(m, top) - top) * factor), 0.0)
                total = total + add * part
                mixed = mixed + add * dr[b // 2, b % 2][None]
            lane3 = lax.broadcasted_iota(jnp.int32, (PG, 8, HD), 2)
            cs[:, 0] = mixed
            cs[:, 1] = jnp.where(lane3 < 64, top, total)
            for g in range(PG):
                remote(cs.at[g], dz.at[role], dout.at[3], din.at[3], line(PG + g)).start()

        own_wait(0)
        own(0)

        own_along_y(0)

        for slot in range(1, SLOTS):
            @pl.when(chip < slot)
            def _(slot=slot):
                for j in range(HALF):
                    kvbuf[j, (8 - slot) * 256:(9 - slot) * 256, :] = jnp.zeros((256, 256), jnp.bfloat16)

        at = lax.broadcasted_iota(jnp.int32, (128, 128), 0)
        to = lax.broadcasted_iota(jnp.int32, (128, 128), 1)
        for i in range(ROWS // 128):
            eye[i * 128:(i + 1) * 128, :] = (at == to).astype(jnp.bfloat16)
        for e in range(2):
            for w in range(15):
                level = jnp.where(firsts[e] <= w, 0.0, NEG)
                maskbuf[e, w * 128:(w + 1) * 128, :] = jnp.full((128, 128), level, jnp.float32).astype(jnp.bfloat16)
            maskbuf[e, 1920:2048, :] = jnp.where(at <= to, 0.0, NEG).astype(jnp.bfloat16)

        spread_queries()

        def start_q(h, carry):
            remote(q_columns(1 - core, h), qbuf.at[core, h], send_sem.at[11], q_sem.at[0], sibling).start()
            return carry

        lax.fori_loop(0, 32, start_q, 0)
        inject(0)
        for j in range(1, HALF):
            own_wait(j)
        own(1)
        own_along_y(1)
        partial_terms()
        forward(0)
        inject(1)
        own(2)
        own_along_y(2)
        combine_terms()
        rest(0)

        await_bytes(qbuf.at[0], q_sem.at[0])
        await_bytes(qbuf.at[0], q_sem.at[1])

        row_in = lax.broadcasted_iota(jnp.int32, (ROWS, 128), 0) & 127
        ones = jnp.ones((KT, HD), jnp.bfloat16)

        def place(n):
            j, u = n // 4, n % 4
            return j, u // 2, j * GROUP + (u % 2) * 4

        def key_rows(j, e, kt):
            return j, pl.ds(pl.multiple_of(128 + e * 128 + kt * KT, 128), KT)

        def weave(current, following):
            if following is not None:
                n, scores, peaks = following
                j, e, base = place(n)
                q = jnp.concatenate([qbuf[e, pl.ds(base, 4)].reshape(ROWS, HD), eye[...]], axis=1)
                peak = None
            if current is not None:
                cn, cscores, cpeaks = current
                cj, ce, cbase = place(cn)
                total = None
            for kt in range(WINDOW // KT):
                if following is not None:
                    rows = key_rows(j, e, kt)
                    masked_keys = jnp.concatenate(
                        [kvbuf[rows[0], rows[1], 0:HD], maskbuf[e, kt * KT:(kt + 1) * KT, :]], axis=1)
                    s = lax.dot_general(
                        q, masked_keys, (((1,), (1,)), ((), ())), preferred_element_type=jnp.float32)
                if current is not None:
                    weights = [
                        jnp.exp2((cscores[:, kt * KT + i * 128:kt * KT + (i + 1) * 128] - cpeaks[...]) * factor)
                        for i in range(KT // 128)
                    ]
                    rows = key_rows(cj, ce, kt)
                    product = jnp.dot(
                        jnp.concatenate(weights, axis=1).astype(jnp.bfloat16),
                        jnp.concatenate([kvbuf[rows[0], rows[1], HD:2 * HD], ones], axis=1),
                        preferred_element_type=jnp.float32)
                    total = product if total is None else total + product
                if following is not None:
                    pieces = [s[:, i * 128:(i + 1) * 128] for i in range(KT // 128)]
                    for i, piece in enumerate(pieces):
                        scores[:, kt * KT + i * 128:kt * KT + (i + 1) * 128] = piece
                    while len(pieces) > 1:
                        pieces = [jnp.maximum(a, b) for a, b in zip(pieces[::2], pieces[1::2])]
                    peak = pieces[0] if peak is None else jnp.maximum(peak, pieces[0])
            if following is not None:
                peaks[...] = jnp.broadcast_to(jnp.max(peak, axis=1, keepdims=True), (ROWS, 128))
            if current is not None:
                live = jnp.where(ce == 0, lives[0], lives[1])
                mixed = total[:, :HD] / total[:, HD:]
                mixed = jnp.where(row_in < live, mixed, 0.0).astype(jnp.bfloat16)
                obuf[ce, pl.ds(cbase, 4)] = mixed.reshape(4, BLOCK, HD)
                for i in range(4):
                    columns = out_hbm.at[:, pl.ds(pl.multiple_of((core * 32 + cbase + i) * HD, HD), HD)]

                    @pl.when(ce == core)
                    def _(i=i, columns=columns):
                        pltpu.make_async_copy(obuf.at[ce, cbase + i], columns, out_sem.at[0]).start()

                    @pl.when(ce != core)
                    def _(i=i, columns=columns):
                        remote(obuf.at[ce, cbase + i], columns, send_sem.at[12], out_sem.at[1], sibling).start()

        weave(None, (jnp.int32(0), sbuf, peak0))

        def pair(i, carry):
            j = i // 2
            weave((2 * i, sbuf, peak0), (2 * i + 1, sbuf1, peak1))

            @pl.when(i == 0)
            def _():
                inject(2)
                own(3)
                own_along_y(3)

            @pl.when(i == 1)
            def _():
                inject(3)
                rest(1)

            @pl.when(i == 3)
            def _():
                rest(2)

            @pl.when(i == 5)
            def _():
                rest(3)

            @pl.when(i == 6)
            def _():
                finish_own()

            weave((2 * i + 1, sbuf1, peak1), (2 * i + 2, sbuf, peak0))

            @pl.when(i < HALF - 1)
            def _():
                forward(i + 1)

            return carry

        lax.fori_loop(0, 7, pair, 0)
        weave((jnp.int32(14), sbuf, peak0), (jnp.int32(15), sbuf1, peak1))
        finish_pair()
        weave((jnp.int32(15), sbuf1, peak1), None)

        span = kvbuf.at[:, 0:256, :]

        def sent(kind, condition):
            @pl.when(condition)
            def _():
                await_bytes(span, send_sem.at[kind])

        sent(0, x < 3)
        sent(1, x < 2)
        sent(2, y < 3)
        sent(3, y == 0)
        sent(4, x >= 1)
        sent(5, x >= 1)
        sent(6, jnp.logical_and(x >= 2, y == 3))
        sent(7, jnp.logical_and(x >= 2, y > 0))
        sent(8, chip >= right_fwd)
        sent(9, chip >= left_fwd)
        await_bytes(kvbuf.at[:, 0:128, :], send_sem.at[10])
        await_bytes(qbuf.at[0], send_sem.at[11])
        await_bytes(obuf.at[0], send_sem.at[12])
        await_bytes(obuf.at[0], out_sem.at[0])
        await_many(qd, dout.at[1])
        await_many(dr, dout.at[2])
        await_bytes(cs, dout.at[3])
        await_bytes(obuf.at[0], out_sem.at[1])
        finish_wait()

    @pl.when(role >= PG)
    def _():
        group = role - PG
        to = lax.broadcasted_iota(jnp.int32, (32, 16), 0)
        at = lax.broadcasted_iota(jnp.int32, (32, 16), 1)
        ordered = jnp.zeros((32, HD), jnp.float32)
        for h in range(2):
            chosen = jnp.logical_and((to & 7) // 4 == h, at == (to & 3) * 4 + to // 8).astype(jnp.bfloat16)
            ordered = ordered + jnp.dot(
                chosen, raw_q[:, h * HD:(h + 1) * HD], preferred_element_type=jnp.float32)
        dq[...] = ordered.reshape(PG, 8, HD)
        for p in range(PG):
            remote(dq.at[p], qz.at[group], dout.at[0], din.at[0], line(p)).start()
        pltpu.make_async_copy(w_hbm, wbuf, dlocal.at[0]).wait()
        await_bytes(dz, din.at[3])
        step = lax.broadcasted_iota(jnp.int32, (8, HD), 0) & 3
        to = lax.broadcasted_iota(jnp.int32, (32, 16), 0)
        at = lax.broadcasted_iota(jnp.int32, (32, 16), 1)
        chosen = jnp.logical_and((to & 7) < 4, at == (to & 3) * 4 + to // 8).astype(jnp.bfloat16)
        new_rows = [
            jnp.dot(chosen, raw_kv[:, i * HD:(i + 1) * HD], preferred_element_type=jnp.float32).reshape(PG, 8, HD)
            for i in range(2)
        ]
        tiles = []
        for p in range(PG):
            pair = dz[p, 1]
            m = jnp.broadcast_to(pair[:, 0:1], (8, HD))
            part = jnp.broadcast_to(pair[:, 64:65], (8, HD))
            q = dq[p]
            scores = []
            for t in range(4):
                s = jnp.sum(q * new_rows[0][p, t:t + 1, :], axis=1, keepdims=True)
                scores.append(jnp.where(step >= t, jnp.broadcast_to(s, (8, HD)), NEG))
            top = m
            for s in scores:
                top = jnp.maximum(top, s)
            old = jnp.exp2((m - top) * factor)
            total = part * old
            mixed = dz[p, 0] * old
            for t in range(4):
                w = jnp.exp2((scores[t] - top) * factor)
                total = total + w
                mixed = mixed + w * new_rows[1][p, t:t + 1, :]
            tiles.append(mixed / total)
        rows = jnp.concatenate(tiles, axis=0).astype(jnp.bfloat16)
        to = lax.broadcasted_iota(jnp.int32, (16, 32), 0)
        at = lax.broadcasted_iota(jnp.int32, (16, 32), 1)
        halves = []
        for h in range(2):
            chosen = (at == (to // 4) * 8 + h * 4 + to % 4).astype(jnp.bfloat16)
            halves.append(jnp.dot(chosen, rows, preferred_element_type=jnp.float32).astype(jnp.bfloat16))
        attended = jnp.concatenate(halves, axis=1)

        def project(i, carry):
            others = [(seq + 4 * i + d) % 32 for d in range(4)]
            for other in others:
                columns = pl.ds(pl.multiple_of(other * 256, 256), 256)
                rs_s[other] = jnp.dot(
                    attended, wbuf[:, columns], preferred_element_type=jnp.float32).astype(jnp.bfloat16)
            for other in others:
                @pl.when(other != seq)
                def _(other=other):
                    remote(rs_s.at[other], rs_r.at[seq], dout.at[4], din.at[4], plane(other)).start()

            return carry

        lax.fori_loop(0, 8, project, 0)
        rs_r[seq] = rs_s[seq]
        await_bytes(rs_r.at[0:31], din.at[4])

        def add(i, total):
            four = [rs_r[4 * i + d].astype(jnp.float32) for d in range(4)]
            return total + ((four[0] + four[1]) + (four[2] + four[3]))

        summed = lax.fori_loop(0, 8, add, jnp.zeros((16, 256), jnp.float32))
        fz[group] = summed.astype(jnp.bfloat16)
        for d in range(1, 2 * PG):
            remote(fz.at[group], fz.at[group], dout.at[5], din.at[5], line((role + d) % (2 * PG))).start()
        finish_own()
        finish_pair()
        await_bytes(qz, dout.at[0])
        await_bytes(rs_s.at[0:31], dout.at[4])
        await_bytes(fz.at[0:7], dout.at[5])
        for i in range(8):
            pltpu.make_async_copy(zbuf, out_hbm.at[:, i * 1024:(i + 1) * 1024], fill_sem.at[i]).wait()
        finish_wait()


def fused(prompt_lengths, decode_group, queries, kv, dq, fresh, out_weight):
    smem = pl.BlockSpec(memory_space=pltpu.SMEM)
    vmem = pl.BlockSpec(memory_space=pltpu.VMEM)
    hbm = pl.BlockSpec(memory_space=pl.ANY)
    return pl.pallas_call(
        fused_kernel,
        out_shape=[
            jax.ShapeDtypeStruct((BLOCK, H * HD), jnp.bfloat16),
            jax.ShapeDtypeStruct((16, 2, 4, PG, PG, 256), jnp.bfloat16),
        ],
        in_specs=[smem, smem, hbm, hbm, vmem, vmem, hbm],
        out_specs=[hbm, hbm],
        scratch_shapes=[
            pltpu.VMEM((2, 32, BLOCK, HD), jnp.bfloat16),
            pltpu.VMEM((HALF, SLOTS * 256, 256), jnp.bfloat16),
            pltpu.VMEM((ROWS, WINDOW), jnp.float32),
            pltpu.VMEM((ROWS, WINDOW), jnp.float32),
            pltpu.VMEM((ROWS, 128), jnp.float32),
            pltpu.VMEM((ROWS, 128), jnp.float32),
            pltpu.VMEM((ROWS, 128), jnp.bfloat16),
            pltpu.VMEM((2, WINDOW, 128), jnp.bfloat16),
            pltpu.VMEM((2, 32, BLOCK, HD), jnp.bfloat16),
            pltpu.VMEM((BLOCK, 1024), jnp.bfloat16),
            pltpu.VMEM((256, 8192), jnp.bfloat16),
            pltpu.VMEM((PG, 8, HD), jnp.float32),
            pltpu.VMEM((PG, 8, HD), jnp.float32),
            pltpu.VMEM((32, HD), jnp.bfloat16),
            pltpu.VMEM((16, 32, HD), jnp.bfloat16),
            pltpu.VMEM((16, 3, 8, HD), jnp.float32),
            pltpu.VMEM((16, 3, 8, HD), jnp.float32),
            pltpu.VMEM((PG, 2, 8, HD), jnp.float32),
            pltpu.VMEM((PG, 2, 8, HD), jnp.float32),
            pltpu.VMEM((32, 16, 256), jnp.bfloat16),
            pltpu.VMEM((32, 16, 256), jnp.bfloat16),
            pltpu.VMEM((8, 16, 256), jnp.bfloat16),
            pltpu.VMEM((4, PG, PG, 256), jnp.bfloat16),
            pltpu.SemaphoreType.DMA((SLOTS, HALF)),
            pltpu.SemaphoreType.DMA((2,)),
            pltpu.SemaphoreType.DMA((HALF,)),
            pltpu.SemaphoreType.DMA((2,)),
            pltpu.SemaphoreType.DMA((8,)),
            pltpu.SemaphoreType.DMA((13,)),
            pltpu.SemaphoreType.DMA((8,)),
            pltpu.SemaphoreType.DMA((8,)),
            pltpu.SemaphoreType.DMA((2,)),
        ],
        compiler_params=pltpu.CompilerParams(
            collective_id=0, has_side_effects=True, vmem_limit_bytes=62 * 1024 * 1024
        ),
        cost_estimate=pl.CostEstimate(flops=17_000_000_000, bytes_accessed=16_000_000, transcendentals=17_000_000),
    )(prompt_lengths, decode_group, queries, kv, dq, fresh, out_weight)


def on_device(prefill_queries, prefill_kv, prompt_lengths, decode_group, decode_queries, decode_kv, out_weight):
    kv_head = lax.axis_index("seq") // (lax.axis_size("seq") // KVH)
    dq = decode_queries.reshape(4 * PG, 2 * HD)
    fresh = lax.dynamic_slice_in_dim(decode_kv[0], kv_head * 2 * HD, 2 * HD, 2)
    fresh = fresh.reshape(4 * PG, 2 * HD)
    prefill_out, decode_out = fused(
        prompt_lengths, decode_group, prefill_queries[0], prefill_kv[0], dq, fresh, out_weight
    )
    decode_out = decode_out.reshape(32, 4, PG, PG, 256).transpose(1, 2, 3, 0, 4).reshape(4, PG, PG, -1)
    return prefill_out[None], decode_out


def solution(mesh):
    in_specs = (
        P("role", "seq", None),
        P("role", "seq", None),
        P(),
        P(),
        P("role", None, None, "seq"),
        P("role", None, None, None),
        P("seq", None),
    )
    out_specs = (P("role", "seq", None), P())
    return jax.shard_map(on_device, mesh=mesh, in_specs=in_specs, out_specs=out_specs, check_vma=False)
```

```python
import functools

import jax
import jax.numpy as jnp
from jax import lax
from jax.experimental import pallas as pl
from jax.experimental.pallas import tpu as pltpu
from jax.sharding import PartitionSpec as P

MESH = pl.DeviceIdType.MESH
H = 64
KVH = 8
HD = 128
BLOCK = 128
PG = 4
NEG = -1e30
SCALE = HD**-0.5
LOG2E = 1.4426950408889634
SLOTS = 9
HALF = KVH // 2
GROUP = H // KVH
ROWS = 512
KT = 1024
WINDOW = 2048


def fused_kernel(
    lengths, serves, q_hbm, kv_hbm, raw_q, raw_kv, w_hbm, out_hbm, dec_hbm,
    qbuf, kvbuf, sbuf, sbuf1, peak0, peak1, eye, maskbuf, obuf, zbuf, wbuf, vq, vkv, tall, dq, qz, qb, qd, ds, dr, cs, dz, rs_s, rs_r, fz, fo,
    slot_sem, q_sem, own_sem, out_sem, fill_sem, send_sem, din, dout, dlocal
):
    role = lax.axis_index("role")
    seq = lax.axis_index("seq")
    core = seq % 2
    chip = seq // 2
    y = chip % 4
    x = chip // 4
    home = seq // 16
    prefilling = role < PG
    factor = SCALE * LOG2E

    def plane(other):
        return (role, other)

    def line(other):
        return (other, seq)

    def remote(src, dst, send, recv, device):
        return pltpu.make_async_remote_copy(
            src_ref=src, dst_ref=dst, send_sem=send, recv_sem=recv, device_id=device, device_id_type=MESH)

    def await_bytes(ref, sem):
        pltpu.make_async_copy(ref, ref, sem).wait()

    def q_columns(half, h):
        return q_hbm.at[:, pl.ds(pl.multiple_of((half * 32 + h) * HD, HD), HD)]

    def kv_columns(half, j):
        return kv_hbm.at[:, pl.ds(pl.multiple_of(half * HALF * 256 + j * 256, 256), 256)]

    def chunk(slot, j):
        return kvbuf.at[j, pl.ds(pl.multiple_of((8 - slot) * 256, 256), 256), :]

    def own_rows(j):
        return kvbuf.at[j, pl.ds(pl.multiple_of(2048 + core * 128, 128), 128), :]

    barrier = pltpu.get_barrier_semaphore()

    def greet(d, carry):
        pl.semaphore_signal(barrier, inc=1, device_id=plane((seq + d) % 32), device_id_type=MESH)
        return carry

    lax.fori_loop(1, 32, greet, 0)

    @pl.when(prefilling)
    def _():
        for g in range(PG):
            pl.semaphore_signal(barrier, inc=1, device_id=line(PG + g), device_id_type=MESH)
        for j in range(HALF):
            pltpu.make_async_copy(kv_columns(core, j), own_rows(j), own_sem.at[j]).start()

        def keep_q(h, carry):
            pltpu.make_async_copy(q_columns(core, h), qbuf.at[core, h], q_sem.at[1]).start()
            return carry

        lax.fori_loop(0, 32, keep_q, 0)
        pl.semaphore_wait(barrier, 35)

    @pl.when(role >= PG)
    def _():
        for d in range(1, 2 * PG):
            pl.semaphore_signal(barrier, inc=1, device_id=line((role + d) % (2 * PG)), device_id_type=MESH)
        pltpu.make_async_copy(raw_q, vq, own_sem.at[0]).start()
        kv_part = raw_kv.at[:, :, pl.ds(pl.multiple_of(seq // 4 * 256, 256), 256)]
        pltpu.make_async_copy(kv_part, vkv, own_sem.at[1]).start()
        pltpu.make_async_copy(w_hbm, wbuf, dlocal.at[0]).start()
        zbuf[...] = jnp.zeros_like(zbuf)
        for i in range(8):
            pltpu.make_async_copy(zbuf, out_hbm.at[:, i * 1024:(i + 1) * 1024], fill_sem.at[i]).start()
        pl.semaphore_wait(barrier, 38)

    mine = dec_hbm.at[chip, core]

    sibling = plane(seq + 1 - 2 * core)

    def finish_own():
        await_first = prefilling

        @pl.when(await_first)
        def _():
            await_bytes(fz.at[0:4], din.at[5])

        @pl.when(jnp.logical_not(await_first))
        def _():
            await_bytes(fz.at[0:3], din.at[5])

        to = lax.broadcasted_iota(jnp.int32, (64, 64), 0)
        at = lax.broadcasted_iota(jnp.int32, (64, 64), 1)
        order = (at == ((to // 4) % 4) * 16 + (to % 4) * 4 + to // 16).astype(jnp.bfloat16)
        slab = jnp.dot(order, fz[0:4].reshape(64, 256), preferred_element_type=jnp.float32)
        for i in range(16):
            fo[i // 4, i % 4] = slab[4 * i:4 * i + 4].astype(jnp.bfloat16)
        pltpu.make_async_copy(fo, mine, dlocal.at[1]).start()

        def spread(d, carry):
            other = ((chip + d) % 16) * 2 + core
            remote(fo, mine, dout.at[6], din.at[6], plane(other)).start()
            return carry

        lax.fori_loop(1, 16, spread, 0)

    def finish_pair():
        pltpu.make_async_copy(fo, mine, dlocal.at[1]).wait()
        await_bytes(dec_hbm.at[0:15, 0], din.at[6])
        remote(dec_hbm.at[:, core], dec_hbm.at[:, core], dout.at[7], din.at[7], sibling).start()

    def finish_wait():
        await_bytes(dec_hbm.at[0:15, 0], dout.at[6])
        await_bytes(dec_hbm.at[:, 0], dout.at[7])
        await_bytes(dec_hbm.at[:, 0], din.at[7])

    @pl.when(prefilling)
    def _():
        right, left = (y + 1) % 4, (y + 3) % 4

        def device(xx, yy):
            return plane((xx * 4 + yy) * 2 + core)

        for j in range(HALF):
            remote(kv_columns(1 - core, j), own_rows(j), send_sem.at[10], slot_sem.at[0, j], sibling).start()

        def wait_slot(slot, j):
            @pl.when(chip >= slot)
            def _():
                await_bytes(chunk(slot, j), slot_sem.at[slot, j])

        def send(kind, src, dst, j, xx, yy):
            remote(chunk(src, j), chunk(dst, j), send_sem.at[kind], slot_sem.at[dst, j], device(xx, yy)).start()

        def own_wait(j):
            pltpu.make_async_copy(kv_columns(core, j), own_rows(j), own_sem.at[j]).wait()
            await_bytes(own_rows(j), slot_sem.at[0, j])

        def own(j):
            @pl.when(x < 3)
            def _():
                send(0, 0, 4, j, (x + 1) % 4, y)

        def own_along_y(j):
            @pl.when(y < 3)
            def _():
                send(2, 0, 1, j, x, right)

            @pl.when(y == 0)
            def _():
                send(3, 0, 3, j, x, left)

        right_dst = jnp.where(y < 3, 5, 1)
        left_dst = jnp.where(y > 0, 3, 7)
        right_fwd = jnp.where(y < 3, 1, 5)
        left_fwd = jnp.where(y > 0, 7, 3)

        def inject(j):
            wait_slot(4, j)

            @pl.when(x >= 1)
            def _():
                send(4, 4, right_dst, j, x, right)
                send(5, 4, left_dst, j, x, left)

            @pl.when(jnp.logical_and(x >= 1, x < 3))
            def _():
                send(1, 4, 8, j, (x + 1) % 4, y)

        def inject_far(j):
            wait_slot(8, j)

            @pl.when(jnp.logical_and(x >= 2, y == 3))
            def _():
                send(6, 8, 5, j, x, right)

            @pl.when(jnp.logical_and(x >= 2, y > 0))
            def _():
                send(7, 8, 7, j, x, left)

        def forward(j):
            wait_slot(right_fwd, j)

            @pl.when(chip >= right_fwd)
            def _():
                send(8, right_fwd, 2, j, x, right)

            wait_slot(left_fwd, j)

            @pl.when(chip >= left_fwd)
            def _():
                send(9, left_fwd, 6, j, x, left)

        def rest(j):
            wait_slot(6 - right_fwd, j)
            wait_slot(10 - left_fwd, j)
            wait_slot(2, j)
            wait_slot(6, j)

        counts = [lengths[role, i] for i in range(4)]
        served = [serves[role, i] for i in range(4)]
        blocks = [(n + 127) // 128 for n in counts]
        starts = [0, blocks[0], blocks[0] + blocks[1], blocks[0] + blocks[1] + blocks[2]]

        def pick(block, values):
            chosen = values[0]
            for i in range(1, 4):
                chosen = jnp.where(block >= starts[i], values[i], chosen)
            return chosen

        firsts, lives = [], []
        for e in range(2):
            block = 2 * chip + e
            first = pick(block, starts)
            firsts.append(first - (2 * chip - 15 + e))
            lives.append(pick(block, counts) - (block - first) * 128)

        at_home = home == core

        def spread_queries():
            await_bytes(qz, din.at[0])
            qb[...] = qz[...].reshape(32, HD).astype(jnp.bfloat16)

            @pl.when(at_home)
            def _():
                qd[seq % 16] = qb[...]

            def one(d, carry):
                other = ((chip + d) % 16) * 2 + home

                @pl.when(other != seq)
                def _():
                    remote(qb, qd.at[seq % 16], dout.at[1], din.at[1], plane(other)).start()

                return carry

            lax.fori_loop(0, 16, one, 0)

        def await_many(buffer, sem):
            @pl.when(at_home)
            def _():
                await_bytes(buffer.at[0:15], sem)

            @pl.when(jnp.logical_not(at_home))
            def _():
                await_bytes(buffer, sem)

        lanes = lax.broadcasted_iota(jnp.int32, (32, HD), 1)

        def partial_terms():
            await_many(qd, din.at[1])
            stats = []
            for e in range(2):
                group = pick(2 * chip + e, served)
                live = lives[e]

                for j in range(HALF):
                    q = jnp.zeros((4, 8, HD), jnp.float32)
                    wide = qd[4 * j:4 * j + 4].astype(jnp.float32).reshape(4, PG, 8, HD)
                    for g in range(PG):
                        q = jnp.where(group == g, wide[:, g], q)
                    q = q.reshape(32, HD).astype(jnp.bfloat16)
                    keys = kvbuf[j, 2048 + 128 * e:2176 + 128 * e, 0:HD]
                    values = kvbuf[j, 2048 + 128 * e:2176 + 128 * e, HD:2 * HD]
                    s = lax.dot_general(q, keys, (((1,), (1,)), ((), ())), preferred_element_type=jnp.float32)
                    s = jnp.where(lanes < live, s, NEG)
                    m = jnp.max(s, axis=1, keepdims=True)
                    w = jnp.exp2((s - m) * factor)
                    total = jnp.sum(w, axis=1, keepdims=True)
                    o = jnp.dot(w.astype(jnp.bfloat16), values, preferred_element_type=jnp.float32)
                    ds[4 * j:4 * j + 4, e] = o.reshape(4, 8, HD)
                    stat = jnp.where(lanes < 64, m, total)
                    if e == 0:
                        stats.append(stat)
                    else:
                        stat = jnp.where(lanes % 64 < 32, stats[j], stat)
                        ds[4 * j:4 * j + 4, 2] = stat.reshape(4, 8, HD)

            @pl.when(at_home)
            def _():
                dr[chip] = ds[seq % 16]

            def out(d, carry):
                other = 16 * core + (chip + d) % 16

                @pl.when(other != seq)
                def _():
                    remote(ds.at[(chip + d) % 16], dr.at[chip], dout.at[2], din.at[2], plane(other)).start()

                return carry

            lax.fori_loop(0, 16, out, 0)

        which = lax.broadcasted_iota(jnp.int32, (PG, 8, HD), 0)

        def combine_terms():
            await_many(dr, din.at[2])

            terms = []
            top = jnp.full((PG, 8, HD), NEG, jnp.float32)
            for b in range(32):
                flag = which == pick(jnp.int32(b), served)
                m = jnp.broadcast_to(dr[b // 2, 2][:, 32 * (b % 2):32 * (b % 2) + 1], (8, HD))[None]
                top = jnp.maximum(top, jnp.where(flag, m, NEG))
                terms.append((flag, m))
            total = jnp.zeros((PG, 8, HD), jnp.float32)
            mixed = jnp.zeros((PG, 8, HD), jnp.float32)
            for b in range(32):
                flag, m = terms[b]
                part = jnp.broadcast_to(dr[b // 2, 2][:, 64 + 32 * (b % 2):65 + 32 * (b % 2)], (8, HD))[None]
                add = jnp.where(flag, jnp.exp2((jnp.minimum(m, top) - top) * factor), 0.0)
                total = total + add * part
                mixed = mixed + add * dr[b // 2, b % 2][None]
            lane3 = lax.broadcasted_iota(jnp.int32, (PG, 8, HD), 2)
            cs[:, 0] = mixed
            cs[:, 1] = jnp.where(lane3 < 64, top, total)
            for g in range(PG):
                remote(cs.at[g], dz.at[role], dout.at[3], din.at[3], line(PG + g)).start()

        own_wait(0)
        own(0)

        own_along_y(0)

        for slot in range(1, SLOTS):
            @pl.when(chip < slot)
            def _(slot=slot):
                for j in range(HALF):
                    kvbuf[j, (8 - slot) * 256:(9 - slot) * 256, :] = jnp.zeros((256, 256), jnp.bfloat16)

        at = lax.broadcasted_iota(jnp.int32, (128, 128), 0)
        to = lax.broadcasted_iota(jnp.int32, (128, 128), 1)
        for i in range(ROWS // 128):
            eye[i * 128:(i + 1) * 128, :] = (at == to).astype(jnp.bfloat16)
        for e in range(2):
            for w in range(15):
                level = jnp.where(firsts[e] <= w, 0.0, NEG)
                maskbuf[e, w * 128:(w + 1) * 128, :] = jnp.full((128, 128), level, jnp.float32).astype(jnp.bfloat16)
            maskbuf[e, 1920:2048, :] = jnp.where(at <= to, 0.0, NEG).astype(jnp.bfloat16)

        spread_queries()

        def start_q(h, carry):
            remote(q_columns(1 - core, h), qbuf.at[core, h], send_sem.at[11], q_sem.at[0], sibling).start()
            return carry

        lax.fori_loop(0, 32, start_q, 0)
        inject(0)
        for j in range(1, HALF):
            own_wait(j)
        own(1)
        own_along_y(1)
        partial_terms()
        inject_far(0)
        forward(0)
        inject(1)
        own(2)
        own_along_y(2)
        combine_terms()
        rest(0)

        await_bytes(qbuf.at[0], q_sem.at[0])
        await_bytes(qbuf.at[0], q_sem.at[1])

        row_in = lax.broadcasted_iota(jnp.int32, (ROWS, 128), 0) & 127
        ones = jnp.ones((KT, HD), jnp.bfloat16)

        def place(n):
            j, u = n // 4, n % 4
            return j, u // 2, j * GROUP + (u % 2) * 4

        def key_rows(j, e, kt):
            return j, pl.ds(pl.multiple_of(128 + e * 128 + kt * KT, 128), KT)

        def weave(current, following):
            if following is not None:
                n, scores, peaks = following
                j, e, base = place(n)
                q = jnp.concatenate([qbuf[e, pl.ds(base, 4)].reshape(ROWS, HD), eye[...]], axis=1)
                peak = None
            if current is not None:
                cn, cscores, cpeaks = current
                cj, ce, cbase = place(cn)
                total = None
            for kt in range(WINDOW // KT):
                if following is not None:
                    rows = key_rows(j, e, kt)
                    masked_keys = jnp.concatenate(
                        [kvbuf[rows[0], rows[1], 0:HD], maskbuf[e, kt * KT:(kt + 1) * KT, :]], axis=1)
                    s = lax.dot_general(
                        q, masked_keys, (((1,), (1,)), ((), ())), preferred_element_type=jnp.float32)
                if current is not None:
                    weights = [
                        jnp.exp2((cscores[:, kt * KT + i * 128:kt * KT + (i + 1) * 128] - cpeaks[...]) * factor)
                        for i in range(KT // 128)
                    ]
                    rows = key_rows(cj, ce, kt)
                    product = jnp.dot(
                        jnp.concatenate(weights, axis=1).astype(jnp.bfloat16),
                        jnp.concatenate([kvbuf[rows[0], rows[1], HD:2 * HD], ones], axis=1),
                        preferred_element_type=jnp.float32)
                    total = product if total is None else total + product
                if following is not None:
                    pieces = [s[:, i * 128:(i + 1) * 128] for i in range(KT // 128)]
                    for i, piece in enumerate(pieces):
                        scores[:, kt * KT + i * 128:kt * KT + (i + 1) * 128] = piece
                    while len(pieces) > 1:
                        pieces = [jnp.maximum(a, b) for a, b in zip(pieces[::2], pieces[1::2])]
                    peak = pieces[0] if peak is None else jnp.maximum(peak, pieces[0])
            if following is not None:
                peaks[...] = jnp.broadcast_to(jnp.max(peak, axis=1, keepdims=True), (ROWS, 128))
            if current is not None:
                live = jnp.where(ce == 0, lives[0], lives[1])
                mixed = total[:, :HD] / total[:, HD:]
                mixed = jnp.where(row_in < live, mixed, 0.0).astype(jnp.bfloat16)
                obuf[ce, pl.ds(cbase, 4)] = mixed.reshape(4, BLOCK, HD)
                for i in range(4):
                    columns = out_hbm.at[:, pl.ds(pl.multiple_of((core * 32 + cbase + i) * HD, HD), HD)]

                    @pl.when(ce == core)
                    def _(i=i, columns=columns):
                        pltpu.make_async_copy(obuf.at[ce, cbase + i], columns, out_sem.at[0]).start()

                    @pl.when(ce != core)
                    def _(i=i, columns=columns):
                        remote(obuf.at[ce, cbase + i], columns, send_sem.at[12], out_sem.at[1], sibling).start()

        weave(None, (jnp.int32(0), sbuf, peak0))

        def pair(i, carry):
            j = i // 2
            weave((2 * i, sbuf, peak0), (2 * i + 1, sbuf1, peak1))

            @pl.when(i == 0)
            def _():
                inject_far(1)
                inject(2)
                own(3)
                own_along_y(3)

            @pl.when(i == 1)
            def _():
                inject_far(2)
                inject(3)
                rest(1)

            @pl.when(i == 2)
            def _():
                inject_far(3)

            @pl.when(i == 3)
            def _():
                rest(2)

            @pl.when(i == 5)
            def _():
                rest(3)

            @pl.when(i == 6)
            def _():
                finish_own()

            weave((2 * i + 1, sbuf1, peak1), (2 * i + 2, sbuf, peak0))

            @pl.when(i < HALF - 1)
            def _():
                forward(i + 1)

            return carry

        lax.fori_loop(0, 7, pair, 0)
        weave((jnp.int32(14), sbuf, peak0), (jnp.int32(15), sbuf1, peak1))
        finish_pair()
        weave((jnp.int32(15), sbuf1, peak1), None)

        span = kvbuf.at[:, 0:256, :]

        def sent(kind, condition):
            @pl.when(condition)
            def _():
                await_bytes(span, send_sem.at[kind])

        sent(0, x < 3)
        sent(1, jnp.logical_and(x >= 1, x < 3))
        sent(2, y < 3)
        sent(3, y == 0)
        sent(4, x >= 1)
        sent(5, x >= 1)
        sent(6, jnp.logical_and(x >= 2, y == 3))
        sent(7, jnp.logical_and(x >= 2, y > 0))
        sent(8, chip >= right_fwd)
        sent(9, chip >= left_fwd)
        await_bytes(kvbuf.at[:, 0:128, :], send_sem.at[10])
        await_bytes(qbuf.at[0], send_sem.at[11])
        await_bytes(obuf.at[0], send_sem.at[12])
        await_bytes(obuf.at[0], out_sem.at[0])
        await_many(qd, dout.at[1])
        await_many(dr, dout.at[2])
        await_bytes(cs, dout.at[3])
        await_bytes(obuf.at[0], out_sem.at[1])
        finish_wait()

    @pl.when(role >= PG)
    def _():
        group = role - PG
        pltpu.make_async_copy(raw_q, vq, own_sem.at[0]).wait()
        pltpu.make_async_copy(vkv, vkv, own_sem.at[1]).wait()
        for t in range(4):
            tall[0, 4 * t:4 * t + 4, :] = vq[t].astype(jnp.float32)
            tall[1, 4 * t:4 * t + 4, :] = vkv[t].astype(jnp.float32)
        to = lax.broadcasted_iota(jnp.int32, (32, 16), 0)
        at = lax.broadcasted_iota(jnp.int32, (32, 16), 1)
        ordered = jnp.zeros((32, HD), jnp.float32)
        for h in range(2):
            chosen = jnp.logical_and((to & 7) // 4 == h, at == (to & 3) * 4 + to // 8).astype(jnp.bfloat16)
            ordered = ordered + jnp.dot(
                chosen, tall[0, :, h * HD:(h + 1) * HD].astype(jnp.bfloat16), preferred_element_type=jnp.float32)
        dq[...] = ordered.reshape(PG, 8, HD)
        for p in range(PG):
            remote(dq.at[p], qz.at[group], dout.at[0], din.at[0], line(p)).start()
        pltpu.make_async_copy(w_hbm, wbuf, dlocal.at[0]).wait()
        await_bytes(dz, din.at[3])
        step = lax.broadcasted_iota(jnp.int32, (8, HD), 0) & 3
        to = lax.broadcasted_iota(jnp.int32, (32, 16), 0)
        at = lax.broadcasted_iota(jnp.int32, (32, 16), 1)
        chosen = jnp.logical_and((to & 7) < 4, at == (to & 3) * 4 + to // 8).astype(jnp.bfloat16)
        new_rows = [
            jnp.dot(
                chosen, tall[1, :, i * HD:(i + 1) * HD].astype(jnp.bfloat16), preferred_element_type=jnp.float32
            ).reshape(PG, 8, HD)
            for i in range(2)
        ]
        tiles = []
        for p in range(PG):
            pair = dz[p, 1]
            m = jnp.broadcast_to(pair[:, 0:1], (8, HD))
            part = jnp.broadcast_to(pair[:, 64:65], (8, HD))
            q = dq[p]
            scores = []
            for t in range(4):
                s = jnp.sum(q * new_rows[0][p, t:t + 1, :], axis=1, keepdims=True)
                scores.append(jnp.where(step >= t, jnp.broadcast_to(s, (8, HD)), NEG))
            top = m
            for s in scores:
                top = jnp.maximum(top, s)
            old = jnp.exp2((m - top) * factor)
            total = part * old
            mixed = dz[p, 0] * old
            for t in range(4):
                w = jnp.exp2((scores[t] - top) * factor)
                total = total + w
                mixed = mixed + w * new_rows[1][p, t:t + 1, :]
            tiles.append(mixed / total)
        rows = jnp.concatenate(tiles, axis=0).astype(jnp.bfloat16)
        to = lax.broadcasted_iota(jnp.int32, (16, 32), 0)
        at = lax.broadcasted_iota(jnp.int32, (16, 32), 1)
        halves = []
        for h in range(2):
            chosen = (at == (to // 4) * 8 + h * 4 + to % 4).astype(jnp.bfloat16)
            halves.append(jnp.dot(chosen, rows, preferred_element_type=jnp.float32).astype(jnp.bfloat16))
        attended = jnp.concatenate(halves, axis=1)

        def project(i, carry):
            others = [(seq + 4 * i + d) % 32 for d in range(4)]
            for other in others:
                columns = pl.ds(pl.multiple_of(other * 256, 256), 256)
                rs_s[other] = jnp.dot(
                    attended, wbuf[:, columns], preferred_element_type=jnp.float32).astype(jnp.bfloat16)
            for other in others:
                @pl.when(other != seq)
                def _(other=other):
                    remote(rs_s.at[other], rs_r.at[seq], dout.at[4], din.at[4], plane(other)).start()

            return carry

        lax.fori_loop(0, 8, project, 0)
        rs_r[seq] = rs_s[seq]
        await_bytes(rs_r.at[0:31], din.at[4])

        def add(i, total):
            four = [rs_r[4 * i + d].astype(jnp.float32) for d in range(4)]
            return total + ((four[0] + four[1]) + (four[2] + four[3]))

        summed = lax.fori_loop(0, 8, add, jnp.zeros((16, 256), jnp.float32))
        fz[group] = summed.astype(jnp.bfloat16)
        for d in range(1, 2 * PG):
            remote(fz.at[group], fz.at[group], dout.at[5], din.at[5], line((role + d) % (2 * PG))).start()
        finish_own()
        finish_pair()
        await_bytes(qz, dout.at[0])
        await_bytes(rs_s.at[0:31], dout.at[4])
        await_bytes(fz.at[0:7], dout.at[5])
        for i in range(8):
            pltpu.make_async_copy(zbuf, out_hbm.at[:, i * 1024:(i + 1) * 1024], fill_sem.at[i]).wait()
        finish_wait()


def fused(prompt_lengths, decode_group, queries, kv, dq, fresh, out_weight):
    smem = pl.BlockSpec(memory_space=pltpu.SMEM)
    hbm = pl.BlockSpec(memory_space=pl.ANY)
    return pl.pallas_call(
        fused_kernel,
        out_shape=[
            jax.ShapeDtypeStruct((BLOCK, H * HD), jnp.bfloat16),
            jax.ShapeDtypeStruct((16, 2, 4, PG, PG, 256), jnp.bfloat16),
        ],
        in_specs=[smem, smem, hbm, hbm, hbm, hbm, hbm],
        out_specs=[hbm, hbm],
        scratch_shapes=[
            pltpu.VMEM((2, 32, BLOCK, HD), jnp.bfloat16),
            pltpu.VMEM((HALF, SLOTS * 256, 256), jnp.bfloat16),
            pltpu.VMEM((ROWS, WINDOW), jnp.float32),
            pltpu.VMEM((ROWS, WINDOW), jnp.float32),
            pltpu.VMEM((ROWS, 128), jnp.float32),
            pltpu.VMEM((ROWS, 128), jnp.float32),
            pltpu.VMEM((ROWS, 128), jnp.bfloat16),
            pltpu.VMEM((2, WINDOW, 128), jnp.bfloat16),
            pltpu.VMEM((2, 32, BLOCK, HD), jnp.bfloat16),
            pltpu.VMEM((BLOCK, 1024), jnp.bfloat16),
            pltpu.VMEM((256, 8192), jnp.bfloat16),
            pltpu.VMEM((4, PG, 256), jnp.bfloat16),
            pltpu.VMEM((4, PG, 256), jnp.bfloat16),
            pltpu.VMEM((2, 4 * PG, 256), jnp.float32),
            pltpu.VMEM((PG, 8, HD), jnp.float32),
            pltpu.VMEM((PG, 8, HD), jnp.float32),
            pltpu.VMEM((32, HD), jnp.bfloat16),
            pltpu.VMEM((16, 32, HD), jnp.bfloat16),
            pltpu.VMEM((16, 3, 8, HD), jnp.float32),
            pltpu.VMEM((16, 3, 8, HD), jnp.float32),
            pltpu.VMEM((PG, 2, 8, HD), jnp.float32),
            pltpu.VMEM((PG, 2, 8, HD), jnp.float32),
            pltpu.VMEM((32, 16, 256), jnp.bfloat16),
            pltpu.VMEM((32, 16, 256), jnp.bfloat16),
            pltpu.VMEM((8, 16, 256), jnp.bfloat16),
            pltpu.VMEM((4, PG, PG, 256), jnp.bfloat16),
            pltpu.SemaphoreType.DMA((SLOTS, HALF)),
            pltpu.SemaphoreType.DMA((2,)),
            pltpu.SemaphoreType.DMA((HALF,)),
            pltpu.SemaphoreType.DMA((2,)),
            pltpu.SemaphoreType.DMA((8,)),
            pltpu.SemaphoreType.DMA((13,)),
            pltpu.SemaphoreType.DMA((8,)),
            pltpu.SemaphoreType.DMA((8,)),
            pltpu.SemaphoreType.DMA((2,)),
        ],
        compiler_params=pltpu.CompilerParams(
            collective_id=0, has_side_effects=True, vmem_limit_bytes=62 * 1024 * 1024
        ),
        cost_estimate=pl.CostEstimate(flops=17_000_000_000, bytes_accessed=16_000_000, transcendentals=17_000_000),
    )(prompt_lengths, decode_group, queries, kv, dq, fresh, out_weight)


def on_device(prefill_queries, prefill_kv, prompt_lengths, decode_group, decode_queries, decode_kv, out_weight):
    prefill_out, decode_out = fused(
        prompt_lengths, decode_group, prefill_queries[0], prefill_kv[0], decode_queries[0], decode_kv[0], out_weight
    )
    decode_out = decode_out.reshape(32, 4, PG, PG, 256).transpose(1, 2, 3, 0, 4).reshape(4, PG, PG, -1)
    return prefill_out[None], decode_out


def solution(mesh):
    in_specs = (
        P("role", "seq", None),
        P("role", "seq", None),
        P(),
        P(),
        P("role", None, None, "seq"),
        P("role", None, None, None),
        P("seq", None),
    )
    out_specs = (P("role", "seq", None), P())
    return jax.shard_map(on_device, mesh=mesh, in_specs=in_specs, out_specs=out_specs, check_vma=False)
```

```python
import functools

import jax
import jax.numpy as jnp
from jax import lax
from jax.experimental import pallas as pl
from jax.experimental.pallas import tpu as pltpu
from jax.sharding import PartitionSpec as P

MESH = pl.DeviceIdType.MESH
H = 64
KVH = 8
HD = 128
BLOCK = 128
PG = 4
NEG = -1e30
SCALE = HD**-0.5
LOG2E = 1.4426950408889634
SLOTS = 9
HALF = KVH // 2
GROUP = H // KVH
ROWS = 512
KT = 1024
WINDOW = 2048


def fused_kernel(
    lengths, serves, q_hbm, kv_hbm, raw_q, raw_kv, w_hbm, out_hbm, dec_hbm,
    qbuf, kvbuf, sbuf, sbuf1, peak0, peak1, eye, maskbuf, obuf, zbuf, wbuf, vq, vkv, tall, dq, qz, qb, qd, ds, dr, cs, dz, rs_s, rs_r, fz, fo,
    slot_sem, q_sem, own_sem, out_sem, fill_sem, send_sem, din, dout, dlocal
):
    role = lax.axis_index("role")
    seq = lax.axis_index("seq")
    core = seq % 2
    chip = seq // 2
    y = chip % 4
    x = chip // 4
    home = seq // 16
    prefilling = role < PG
    factor = SCALE * LOG2E

    def plane(other):
        return (role, other)

    def line(other):
        return (other, seq)

    def remote(src, dst, send, recv, device):
        return pltpu.make_async_remote_copy(
            src_ref=src, dst_ref=dst, send_sem=send, recv_sem=recv, device_id=device, device_id_type=MESH)

    def await_bytes(ref, sem):
        pltpu.make_async_copy(ref, ref, sem).wait()

    def q_columns(half, h):
        return q_hbm.at[:, pl.ds(pl.multiple_of((half * 32 + h) * HD, HD), HD)]

    def kv_columns(half, j):
        return kv_hbm.at[:, pl.ds(pl.multiple_of(half * HALF * 256 + j * 256, 256), 256)]

    def chunk(slot, j):
        return kvbuf.at[j, pl.ds(pl.multiple_of((8 - slot) * 256, 256), 256), :]

    def own_rows(j):
        return kvbuf.at[j, pl.ds(pl.multiple_of(2048 + core * 128, 128), 128), :]

    barrier = pltpu.get_barrier_semaphore()

    def greet(d, carry):
        pl.semaphore_signal(barrier, inc=1, device_id=plane((seq + d) % 32), device_id_type=MESH)
        return carry

    lax.fori_loop(1, 32, greet, 0)

    @pl.when(prefilling)
    def _():
        for g in range(PG):
            pl.semaphore_signal(barrier, inc=1, device_id=line(PG + g), device_id_type=MESH)
        for j in range(HALF):
            pltpu.make_async_copy(kv_columns(core, j), own_rows(j), own_sem.at[j]).start()

        def keep_q(h, carry):
            pltpu.make_async_copy(q_columns(core, h), qbuf.at[core, h], q_sem.at[1]).start()
            return carry

        lax.fori_loop(0, 32, keep_q, 0)
        pl.semaphore_wait(barrier, 35)

    @pl.when(role >= PG)
    def _():
        for d in range(1, 2 * PG):
            pl.semaphore_signal(barrier, inc=1, device_id=line((role + d) % (2 * PG)), device_id_type=MESH)
        pltpu.make_async_copy(raw_q, vq, own_sem.at[0]).start()
        kv_part = raw_kv.at[:, :, pl.ds(pl.multiple_of(seq // 4 * 256, 256), 256)]
        pltpu.make_async_copy(kv_part, vkv, own_sem.at[1]).start()
        pltpu.make_async_copy(w_hbm, wbuf, dlocal.at[0]).start()
        zbuf[...] = jnp.zeros_like(zbuf)
        for i in range(8):
            pltpu.make_async_copy(zbuf, out_hbm.at[:, i * 1024:(i + 1) * 1024], fill_sem.at[i]).start()
        pl.semaphore_wait(barrier, 38)

    mine = dec_hbm.at[chip, core]

    sibling = plane(seq + 1 - 2 * core)

    def finish_own():
        await_first = prefilling

        @pl.when(await_first)
        def _():
            await_bytes(fz.at[0:4], din.at[5])

        @pl.when(jnp.logical_not(await_first))
        def _():
            await_bytes(fz.at[0:3], din.at[5])

        to = lax.broadcasted_iota(jnp.int32, (64, 64), 0)
        at = lax.broadcasted_iota(jnp.int32, (64, 64), 1)
        order = (at == ((to // 4) % 4) * 16 + (to % 4) * 4 + to // 16).astype(jnp.bfloat16)
        slab = jnp.dot(order, fz[0:4].reshape(64, 256), preferred_element_type=jnp.float32)
        for i in range(16):
            fo[i // 4, i % 4] = slab[4 * i:4 * i + 4].astype(jnp.bfloat16)
        pltpu.make_async_copy(fo, mine, dlocal.at[1]).start()

        def spread(d, carry):
            other = ((chip + d) % 16) * 2 + core
            remote(fo, mine, dout.at[6], din.at[6], plane(other)).start()
            return carry

        lax.fori_loop(1, 16, spread, 0)

    def finish_pair():
        pltpu.make_async_copy(fo, mine, dlocal.at[1]).wait()
        await_bytes(dec_hbm.at[0:15, 0], din.at[6])
        remote(dec_hbm.at[:, core], dec_hbm.at[:, core], dout.at[7], din.at[7], sibling).start()

    def finish_wait():
        await_bytes(dec_hbm.at[0:15, 0], dout.at[6])
        await_bytes(dec_hbm.at[:, 0], dout.at[7])
        await_bytes(dec_hbm.at[:, 0], din.at[7])

    @pl.when(prefilling)
    def _():
        right, left = (y + 1) % 4, (y + 3) % 4

        def device(xx, yy):
            return plane((xx * 4 + yy) * 2 + core)

        for j in range(HALF):
            remote(kv_columns(1 - core, j), own_rows(j), send_sem.at[10], slot_sem.at[0, j], sibling).start()

        def wait_slot(slot, j):
            @pl.when(chip >= slot)
            def _():
                await_bytes(chunk(slot, j), slot_sem.at[slot, j])

        def send(kind, src, dst, j, xx, yy):
            remote(chunk(src, j), chunk(dst, j), send_sem.at[kind], slot_sem.at[dst, j], device(xx, yy)).start()

        def own_wait(j):
            pltpu.make_async_copy(kv_columns(core, j), own_rows(j), own_sem.at[j]).wait()
            await_bytes(own_rows(j), slot_sem.at[0, j])

        def own(j):
            @pl.when(x < 3)
            def _():
                send(0, 0, 4, j, (x + 1) % 4, y)

        def own_along_y(j):
            @pl.when(y < 3)
            def _():
                send(2, 0, 1, j, x, right)

            @pl.when(y == 0)
            def _():
                send(3, 0, 3, j, x, left)

        right_dst = jnp.where(y < 3, 5, 1)
        left_dst = jnp.where(y > 0, 3, 7)
        right_fwd = jnp.where(y < 3, 1, 5)
        left_fwd = jnp.where(y > 0, 7, 3)

        def inject(j):
            wait_slot(4, j)

            @pl.when(x >= 1)
            def _():
                send(4, 4, right_dst, j, x, right)
                send(5, 4, left_dst, j, x, left)

            @pl.when(jnp.logical_and(x >= 1, x < 3))
            def _():
                send(1, 4, 8, j, (x + 1) % 4, y)

        def inject_far(j):
            wait_slot(8, j)

            @pl.when(jnp.logical_and(x >= 2, y == 3))
            def _():
                send(6, 8, 5, j, x, right)

            @pl.when(jnp.logical_and(x >= 2, y > 0))
            def _():
                send(7, 8, 7, j, x, left)

        def forward(j):
            wait_slot(right_fwd, j)

            @pl.when(chip >= right_fwd)
            def _():
                send(8, right_fwd, 2, j, x, right)

            wait_slot(left_fwd, j)

            @pl.when(chip >= left_fwd)
            def _():
                send(9, left_fwd, 6, j, x, left)

        def rest(j):
            wait_slot(6 - right_fwd, j)
            wait_slot(10 - left_fwd, j)
            wait_slot(2, j)
            wait_slot(6, j)

        counts = [lengths[role, i] for i in range(4)]
        served = [serves[role, i] for i in range(4)]
        blocks = [(n + 127) // 128 for n in counts]
        starts = [0, blocks[0], blocks[0] + blocks[1], blocks[0] + blocks[1] + blocks[2]]

        def pick(block, values):
            chosen = values[0]
            for i in range(1, 4):
                chosen = jnp.where(block >= starts[i], values[i], chosen)
            return chosen

        firsts, lives = [], []
        for e in range(2):
            block = 2 * chip + e
            first = pick(block, starts)
            firsts.append(first - (2 * chip - 15 + e))
            lives.append(pick(block, counts) - (block - first) * 128)

        at_home = home == core

        def spread_queries():
            await_bytes(qz, din.at[0])
            qb[...] = qz[...].reshape(32, HD).astype(jnp.bfloat16)

            @pl.when(at_home)
            def _():
                qd[seq % 16] = qb[...]

            def one(d, carry):
                other = ((chip + d) % 16) * 2 + home

                @pl.when(other != seq)
                def _():
                    remote(qb, qd.at[seq % 16], dout.at[1], din.at[1], plane(other)).start()

                return carry

            lax.fori_loop(0, 16, one, 0)

        def await_many(buffer, sem):
            @pl.when(at_home)
            def _():
                await_bytes(buffer.at[0:15], sem)

            @pl.when(jnp.logical_not(at_home))
            def _():
                await_bytes(buffer, sem)

        lanes = lax.broadcasted_iota(jnp.int32, (32, HD), 1)

        def partial_terms():
            await_many(qd, din.at[1])
            stats = []
            for e in range(2):
                group = pick(2 * chip + e, served)
                live = lives[e]

                for j in range(HALF):
                    q = jnp.zeros((4, 8, HD), jnp.float32)
                    wide = qd[4 * j:4 * j + 4].astype(jnp.float32).reshape(4, PG, 8, HD)
                    for g in range(PG):
                        q = jnp.where(group == g, wide[:, g], q)
                    q = q.reshape(32, HD).astype(jnp.bfloat16)
                    keys = kvbuf[j, 2048 + 128 * e:2176 + 128 * e, 0:HD]
                    values = kvbuf[j, 2048 + 128 * e:2176 + 128 * e, HD:2 * HD]
                    s = lax.dot_general(q, keys, (((1,), (1,)), ((), ())), preferred_element_type=jnp.float32)
                    s = jnp.where(lanes < live, s, NEG)
                    m = jnp.max(s, axis=1, keepdims=True)
                    w = jnp.exp2((s - m) * factor)
                    total = jnp.sum(w, axis=1, keepdims=True)
                    o = jnp.dot(w.astype(jnp.bfloat16), values, preferred_element_type=jnp.float32)
                    ds[4 * j:4 * j + 4, e] = o.reshape(4, 8, HD)
                    stat = jnp.where(lanes < 64, m, total)
                    if e == 0:
                        stats.append(stat)
                    else:
                        stat = jnp.where(lanes % 64 < 32, stats[j], stat)
                        ds[4 * j:4 * j + 4, 2] = stat.reshape(4, 8, HD)

            @pl.when(at_home)
            def _():
                dr[chip] = ds[seq % 16]

            def out(d, carry):
                other = 16 * core + (chip + d) % 16

                @pl.when(other != seq)
                def _():
                    remote(ds.at[(chip + d) % 16], dr.at[chip], dout.at[2], din.at[2], plane(other)).start()

                return carry

            lax.fori_loop(0, 16, out, 0)

        which = lax.broadcasted_iota(jnp.int32, (PG, 8, HD), 0)

        def combine_terms():
            await_many(dr, din.at[2])

            terms = []
            top = jnp.full((PG, 8, HD), NEG, jnp.float32)
            for b in range(32):
                flag = which == pick(jnp.int32(b), served)
                m = jnp.broadcast_to(dr[b // 2, 2][:, 32 * (b % 2):32 * (b % 2) + 1], (8, HD))[None]
                top = jnp.maximum(top, jnp.where(flag, m, NEG))
                terms.append((flag, m))
            total = jnp.zeros((PG, 8, HD), jnp.float32)
            mixed = jnp.zeros((PG, 8, HD), jnp.float32)
            for b in range(32):
                flag, m = terms[b]
                part = jnp.broadcast_to(dr[b // 2, 2][:, 64 + 32 * (b % 2):65 + 32 * (b % 2)], (8, HD))[None]
                add = jnp.where(flag, jnp.exp2((jnp.minimum(m, top) - top) * factor), 0.0)
                total = total + add * part
                mixed = mixed + add * dr[b // 2, b % 2][None]
            lane3 = lax.broadcasted_iota(jnp.int32, (PG, 8, HD), 2)
            cs[:, 0] = mixed
            cs[:, 1] = jnp.where(lane3 < 64, top, total)
            for g in range(PG):
                remote(cs.at[g], dz.at[role], dout.at[3], din.at[3], line(PG + g)).start()

        own_wait(0)
        own(0)

        own_along_y(0)

        for slot in range(1, SLOTS):
            @pl.when(chip < slot)
            def _(slot=slot):
                for j in range(HALF):
                    kvbuf[j, (8 - slot) * 256:(9 - slot) * 256, :] = jnp.zeros((256, 256), jnp.bfloat16)

        at = lax.broadcasted_iota(jnp.int32, (128, 128), 0)
        to = lax.broadcasted_iota(jnp.int32, (128, 128), 1)
        for i in range(ROWS // 128):
            eye[i * 128:(i + 1) * 128, :] = (at == to).astype(jnp.bfloat16)
        for e in range(2):
            for w in range(15):
                level = jnp.where(firsts[e] <= w, 0.0, NEG)
                maskbuf[e, w * 128:(w + 1) * 128, :] = jnp.full((128, 128), level, jnp.float32).astype(jnp.bfloat16)
            maskbuf[e, 1920:2048, :] = jnp.where(at <= to, 0.0, NEG).astype(jnp.bfloat16)

        spread_queries()

        def start_q(h, carry):
            remote(q_columns(1 - core, h), qbuf.at[core, h], send_sem.at[11], q_sem.at[0], sibling).start()
            return carry

        lax.fori_loop(0, 32, start_q, 0)
        inject(0)
        for j in range(1, HALF):
            own_wait(j)
        own(1)
        own_along_y(1)
        partial_terms()
        inject_far(0)
        forward(0)
        inject(1)
        own(2)
        own_along_y(2)
        combine_terms()
        rest(0)

        await_bytes(qbuf.at[0], q_sem.at[0])
        await_bytes(qbuf.at[0], q_sem.at[1])

        row_in = lax.broadcasted_iota(jnp.int32, (ROWS, 128), 0) & 127
        ones = jnp.ones((KT, HD), jnp.bfloat16)

        def place(n):
            j, u = n // 4, n % 4
            return j, u // 2, j * GROUP + (u % 2) * 4

        def key_rows(j, e, kt):
            return j, pl.ds(pl.multiple_of(128 + e * 128 + kt * KT, 128), KT)

        def weave(current, following):
            if following is not None:
                n, scores, peaks = following
                j, e, base = place(n)
                q = jnp.concatenate([qbuf[e, pl.ds(base, 4)].reshape(ROWS, HD), eye[...]], axis=1)
                peak = None
            if current is not None:
                cn, cscores, cpeaks = current
                cj, ce, cbase = place(cn)
                total = None
            for kt in range(WINDOW // KT):
                if following is not None:
                    rows = key_rows(j, e, kt)
                    masked_keys = jnp.concatenate(
                        [kvbuf[rows[0], rows[1], 0:HD], maskbuf[e, kt * KT:(kt + 1) * KT, :]], axis=1)
                    s = lax.dot_general(
                        q, masked_keys, (((1,), (1,)), ((), ())), preferred_element_type=jnp.float32)
                if current is not None:
                    weights = [
                        jnp.exp2(((cscores[:, kt * KT + i * 128:kt * KT + (i + 1) * 128] - cpeaks[...]) * factor).astype(
                            jnp.bfloat16))
                        for i in range(KT // 128)
                    ]
                    rows = key_rows(cj, ce, kt)
                    product = jnp.dot(
                        jnp.concatenate(weights, axis=1),
                        jnp.concatenate([kvbuf[rows[0], rows[1], HD:2 * HD], ones], axis=1),
                        preferred_element_type=jnp.float32)
                    total = product if total is None else total + product
                if following is not None:
                    pieces = [s[:, i * 128:(i + 1) * 128] for i in range(KT // 128)]
                    for i, piece in enumerate(pieces):
                        scores[:, kt * KT + i * 128:kt * KT + (i + 1) * 128] = piece
                    while len(pieces) > 1:
                        pieces = [jnp.maximum(a, b) for a, b in zip(pieces[::2], pieces[1::2])]
                    peak = pieces[0] if peak is None else jnp.maximum(peak, pieces[0])
            if following is not None:
                peaks[...] = jnp.broadcast_to(jnp.max(peak, axis=1, keepdims=True), (ROWS, 128))
            if current is not None:
                live = jnp.where(ce == 0, lives[0], lives[1])
                mixed = total[:, :HD] / total[:, HD:]
                mixed = jnp.where(row_in < live, mixed, 0.0).astype(jnp.bfloat16)
                obuf[ce, pl.ds(cbase, 4)] = mixed.reshape(4, BLOCK, HD)
                for i in range(4):
                    columns = out_hbm.at[:, pl.ds(pl.multiple_of((core * 32 + cbase + i) * HD, HD), HD)]

                    @pl.when(ce == core)
                    def _(i=i, columns=columns):
                        pltpu.make_async_copy(obuf.at[ce, cbase + i], columns, out_sem.at[0]).start()

                    @pl.when(ce != core)
                    def _(i=i, columns=columns):
                        remote(obuf.at[ce, cbase + i], columns, send_sem.at[12], out_sem.at[1], sibling).start()

        weave(None, (jnp.int32(0), sbuf, peak0))

        def pair(i, carry):
            j = i // 2
            weave((2 * i, sbuf, peak0), (2 * i + 1, sbuf1, peak1))

            @pl.when(i == 0)
            def _():
                inject_far(1)
                inject(2)
                own(3)
                own_along_y(3)

            @pl.when(i == 1)
            def _():
                inject_far(2)
                inject(3)
                rest(1)

            @pl.when(i == 2)
            def _():
                inject_far(3)

            @pl.when(i == 3)
            def _():
                rest(2)

            @pl.when(i == 5)
            def _():
                rest(3)

            @pl.when(i == 6)
            def _():
                finish_own()

            weave((2 * i + 1, sbuf1, peak1), (2 * i + 2, sbuf, peak0))

            @pl.when(i < HALF - 1)
            def _():
                forward(i + 1)

            return carry

        lax.fori_loop(0, 7, pair, 0)
        weave((jnp.int32(14), sbuf, peak0), (jnp.int32(15), sbuf1, peak1))
        finish_pair()
        weave((jnp.int32(15), sbuf1, peak1), None)

        span = kvbuf.at[:, 0:256, :]

        def sent(kind, condition):
            @pl.when(condition)
            def _():
                await_bytes(span, send_sem.at[kind])

        sent(0, x < 3)
        sent(1, jnp.logical_and(x >= 1, x < 3))
        sent(2, y < 3)
        sent(3, y == 0)
        sent(4, x >= 1)
        sent(5, x >= 1)
        sent(6, jnp.logical_and(x >= 2, y == 3))
        sent(7, jnp.logical_and(x >= 2, y > 0))
        sent(8, chip >= right_fwd)
        sent(9, chip >= left_fwd)
        await_bytes(kvbuf.at[:, 0:128, :], send_sem.at[10])
        await_bytes(qbuf.at[0], send_sem.at[11])
        await_bytes(obuf.at[0], send_sem.at[12])
        await_bytes(obuf.at[0], out_sem.at[0])
        await_many(qd, dout.at[1])
        await_many(dr, dout.at[2])
        await_bytes(cs, dout.at[3])
        await_bytes(obuf.at[0], out_sem.at[1])
        finish_wait()

    @pl.when(role >= PG)
    def _():
        group = role - PG
        pltpu.make_async_copy(raw_q, vq, own_sem.at[0]).wait()
        pltpu.make_async_copy(vkv, vkv, own_sem.at[1]).wait()
        for t in range(4):
            tall[0, 4 * t:4 * t + 4, :] = vq[t].astype(jnp.float32)
            tall[1, 4 * t:4 * t + 4, :] = vkv[t].astype(jnp.float32)
        to = lax.broadcasted_iota(jnp.int32, (32, 16), 0)
        at = lax.broadcasted_iota(jnp.int32, (32, 16), 1)
        ordered = jnp.zeros((32, HD), jnp.float32)
        for h in range(2):
            chosen = jnp.logical_and((to & 7) // 4 == h, at == (to & 3) * 4 + to // 8).astype(jnp.bfloat16)
            ordered = ordered + jnp.dot(
                chosen, tall[0, :, h * HD:(h + 1) * HD].astype(jnp.bfloat16), preferred_element_type=jnp.float32)
        dq[...] = ordered.reshape(PG, 8, HD)
        for p in range(PG):
            remote(dq.at[p], qz.at[group], dout.at[0], din.at[0], line(p)).start()
        pltpu.make_async_copy(w_hbm, wbuf, dlocal.at[0]).wait()
        await_bytes(dz, din.at[3])
        step = lax.broadcasted_iota(jnp.int32, (8, HD), 0) & 3
        to = lax.broadcasted_iota(jnp.int32, (32, 16), 0)
        at = lax.broadcasted_iota(jnp.int32, (32, 16), 1)
        chosen = jnp.logical_and((to & 7) < 4, at == (to & 3) * 4 + to // 8).astype(jnp.bfloat16)
        new_rows = [
            jnp.dot(
                chosen, tall[1, :, i * HD:(i + 1) * HD].astype(jnp.bfloat16), preferred_element_type=jnp.float32
            ).reshape(PG, 8, HD)
            for i in range(2)
        ]
        tiles = []
        for p in range(PG):
            pair = dz[p, 1]
            m = jnp.broadcast_to(pair[:, 0:1], (8, HD))
            part = jnp.broadcast_to(pair[:, 64:65], (8, HD))
            q = dq[p]
            scores = []
            for t in range(4):
                s = jnp.sum(q * new_rows[0][p, t:t + 1, :], axis=1, keepdims=True)
                scores.append(jnp.where(step >= t, jnp.broadcast_to(s, (8, HD)), NEG))
            top = m
            for s in scores:
                top = jnp.maximum(top, s)
            old = jnp.exp2((m - top) * factor)
            total = part * old
            mixed = dz[p, 0] * old
            for t in range(4):
                w = jnp.exp2((scores[t] - top) * factor)
                total = total + w
                mixed = mixed + w * new_rows[1][p, t:t + 1, :]
            tiles.append(mixed / total)
        rows = jnp.concatenate(tiles, axis=0).astype(jnp.bfloat16)
        to = lax.broadcasted_iota(jnp.int32, (16, 32), 0)
        at = lax.broadcasted_iota(jnp.int32, (16, 32), 1)
        halves = []
        for h in range(2):
            chosen = (at == (to // 4) * 8 + h * 4 + to % 4).astype(jnp.bfloat16)
            halves.append(jnp.dot(chosen, rows, preferred_element_type=jnp.float32).astype(jnp.bfloat16))
        attended = jnp.concatenate(halves, axis=1)

        def project(i, carry):
            others = [(seq + 4 * i + d) % 32 for d in range(4)]
            for other in others:
                columns = pl.ds(pl.multiple_of(other * 256, 256), 256)
                rs_s[other] = jnp.dot(
                    attended, wbuf[:, columns], preferred_element_type=jnp.float32).astype(jnp.bfloat16)
            for other in others:
                @pl.when(other != seq)
                def _(other=other):
                    remote(rs_s.at[other], rs_r.at[seq], dout.at[4], din.at[4], plane(other)).start()

            return carry

        lax.fori_loop(0, 8, project, 0)
        rs_r[seq] = rs_s[seq]
        await_bytes(rs_r.at[0:31], din.at[4])

        def add(i, total):
            four = [rs_r[4 * i + d].astype(jnp.float32) for d in range(4)]
            return total + ((four[0] + four[1]) + (four[2] + four[3]))

        summed = lax.fori_loop(0, 8, add, jnp.zeros((16, 256), jnp.float32))
        fz[group] = summed.astype(jnp.bfloat16)
        for d in range(1, 2 * PG):
            remote(fz.at[group], fz.at[group], dout.at[5], din.at[5], line((role + d) % (2 * PG))).start()
        finish_own()
        finish_pair()
        await_bytes(qz, dout.at[0])
        await_bytes(rs_s.at[0:31], dout.at[4])
        await_bytes(fz.at[0:7], dout.at[5])
        for i in range(8):
            pltpu.make_async_copy(zbuf, out_hbm.at[:, i * 1024:(i + 1) * 1024], fill_sem.at[i]).wait()
        finish_wait()


def fused(prompt_lengths, decode_group, queries, kv, dq, fresh, out_weight):
    smem = pl.BlockSpec(memory_space=pltpu.SMEM)
    hbm = pl.BlockSpec(memory_space=pl.ANY)
    return pl.pallas_call(
        fused_kernel,
        out_shape=[
            jax.ShapeDtypeStruct((BLOCK, H * HD), jnp.bfloat16),
            jax.ShapeDtypeStruct((16, 2, 4, PG, PG, 256), jnp.bfloat16),
        ],
        in_specs=[smem, smem, hbm, hbm, hbm, hbm, hbm],
        out_specs=[hbm, hbm],
        scratch_shapes=[
            pltpu.VMEM((2, 32, BLOCK, HD), jnp.bfloat16),
            pltpu.VMEM((HALF, SLOTS * 256, 256), jnp.bfloat16),
            pltpu.VMEM((ROWS, WINDOW), jnp.float32),
            pltpu.VMEM((ROWS, WINDOW), jnp.float32),
            pltpu.VMEM((ROWS, 128), jnp.float32),
            pltpu.VMEM((ROWS, 128), jnp.float32),
            pltpu.VMEM((ROWS, 128), jnp.bfloat16),
            pltpu.VMEM((2, WINDOW, 128), jnp.bfloat16),
            pltpu.VMEM((2, 32, BLOCK, HD), jnp.bfloat16),
            pltpu.VMEM((BLOCK, 1024), jnp.bfloat16),
            pltpu.VMEM((256, 8192), jnp.bfloat16),
            pltpu.VMEM((4, PG, 256), jnp.bfloat16),
            pltpu.VMEM((4, PG, 256), jnp.bfloat16),
            pltpu.VMEM((2, 4 * PG, 256), jnp.float32),
            pltpu.VMEM((PG, 8, HD), jnp.float32),
            pltpu.VMEM((PG, 8, HD), jnp.float32),
            pltpu.VMEM((32, HD), jnp.bfloat16),
            pltpu.VMEM((16, 32, HD), jnp.bfloat16),
            pltpu.VMEM((16, 3, 8, HD), jnp.float32),
            pltpu.VMEM((16, 3, 8, HD), jnp.float32),
            pltpu.VMEM((PG, 2, 8, HD), jnp.float32),
            pltpu.VMEM((PG, 2, 8, HD), jnp.float32),
            pltpu.VMEM((32, 16, 256), jnp.bfloat16),
            pltpu.VMEM((32, 16, 256), jnp.bfloat16),
            pltpu.VMEM((8, 16, 256), jnp.bfloat16),
            pltpu.VMEM((4, PG, PG, 256), jnp.bfloat16),
            pltpu.SemaphoreType.DMA((SLOTS, HALF)),
            pltpu.SemaphoreType.DMA((2,)),
            pltpu.SemaphoreType.DMA((HALF,)),
            pltpu.SemaphoreType.DMA((2,)),
            pltpu.SemaphoreType.DMA((8,)),
            pltpu.SemaphoreType.DMA((13,)),
            pltpu.SemaphoreType.DMA((8,)),
            pltpu.SemaphoreType.DMA((8,)),
            pltpu.SemaphoreType.DMA((2,)),
        ],
        compiler_params=pltpu.CompilerParams(
            collective_id=0, has_side_effects=True, vmem_limit_bytes=62 * 1024 * 1024
        ),
        cost_estimate=pl.CostEstimate(flops=17_000_000_000, bytes_accessed=16_000_000, transcendentals=17_000_000),
    )(prompt_lengths, decode_group, queries, kv, dq, fresh, out_weight)


def on_device(prefill_queries, prefill_kv, prompt_lengths, decode_group, decode_queries, decode_kv, out_weight):
    prefill_out, decode_out = fused(
        prompt_lengths, decode_group, prefill_queries[0], prefill_kv[0], decode_queries[0], decode_kv[0], out_weight
    )
    decode_out = decode_out.reshape(32, 4, PG, PG, 256).transpose(1, 2, 3, 0, 4).reshape(4, PG, PG, -1)
    return prefill_out[None], decode_out


def solution(mesh):
    in_specs = (
        P("role", "seq", None),
        P("role", "seq", None),
        P(),
        P(),
        P("role", None, None, "seq"),
        P("role", None, None, None),
        P("seq", None),
    )
    out_specs = (P("role", "seq", None), P())
    return jax.shard_map(on_device, mesh=mesh, in_specs=in_specs, out_specs=out_specs, check_vma=False)
```

```python
import functools

import jax
import jax.numpy as jnp
from jax import lax
from jax.experimental import pallas as pl
from jax.experimental.pallas import tpu as pltpu
from jax.sharding import PartitionSpec as P

MESH = pl.DeviceIdType.MESH
H = 64
KVH = 8
HD = 128
BLOCK = 128
PG = 4
NEG = -1e30
SCALE = HD**-0.5
LOG2E = 1.4426950408889634
SLOTS = 9
HALF = KVH // 2
GROUP = H // KVH
ROWS = 1024
KT = 512
WINDOW = 2048


def fused_kernel(
    lengths, serves, q_hbm, kv_hbm, raw_q, raw_kv, w_hbm, out_hbm, dec_hbm,
    qbuf, kvbuf, sbuf, sbuf1, peak0, peak1, eye, maskbuf, obuf, zbuf, wbuf, vq, vkv, tall, dq, qz, qb, qd, ds, dr, cs, dz, rs_s, rs_r, fz, fo,
    slot_sem, q_sem, own_sem, out_sem, fill_sem, send_sem, din, dout, dlocal
):
    role = lax.axis_index("role")
    seq = lax.axis_index("seq")
    core = seq % 2
    chip = seq // 2
    y = chip % 4
    x = chip // 4
    home = seq // 16
    prefilling = role < PG
    factor = SCALE * LOG2E

    def plane(other):
        return (role, other)

    def line(other):
        return (other, seq)

    def remote(src, dst, send, recv, device):
        return pltpu.make_async_remote_copy(
            src_ref=src, dst_ref=dst, send_sem=send, recv_sem=recv, device_id=device, device_id_type=MESH)

    def await_bytes(ref, sem):
        pltpu.make_async_copy(ref, ref, sem).wait()

    def q_columns(half, h):
        return q_hbm.at[:, pl.ds(pl.multiple_of((half * 32 + h) * HD, HD), HD)]

    def kv_columns(half, j):
        return kv_hbm.at[:, pl.ds(pl.multiple_of(half * HALF * 256 + j * 256, 256), 256)]

    def chunk(slot, j):
        return kvbuf.at[j, pl.ds(pl.multiple_of((8 - slot) * 256, 256), 256), :]

    def own_rows(j):
        return kvbuf.at[j, pl.ds(pl.multiple_of(2048 + core * 128, 128), 128), :]

    barrier = pltpu.get_barrier_semaphore()

    def greet(d, carry):
        pl.semaphore_signal(barrier, inc=1, device_id=plane((seq + d) % 32), device_id_type=MESH)
        return carry

    lax.fori_loop(1, 32, greet, 0)

    @pl.when(prefilling)
    def _():
        for g in range(PG):
            pl.semaphore_signal(barrier, inc=1, device_id=line(PG + g), device_id_type=MESH)
        for j in range(HALF):
            pltpu.make_async_copy(kv_columns(core, j), own_rows(j), own_sem.at[j]).start()

        def keep_q(h, carry):
            pltpu.make_async_copy(q_columns(core, h), qbuf.at[core, h], q_sem.at[1]).start()
            return carry

        lax.fori_loop(0, 32, keep_q, 0)
        pl.semaphore_wait(barrier, 35)

    @pl.when(role >= PG)
    def _():
        for d in range(1, 2 * PG):
            pl.semaphore_signal(barrier, inc=1, device_id=line((role + d) % (2 * PG)), device_id_type=MESH)
        pltpu.make_async_copy(raw_q, vq, own_sem.at[0]).start()
        kv_part = raw_kv.at[:, :, pl.ds(pl.multiple_of(seq // 4 * 256, 256), 256)]
        pltpu.make_async_copy(kv_part, vkv, own_sem.at[1]).start()
        pltpu.make_async_copy(w_hbm, wbuf, dlocal.at[0]).start()
        zbuf[...] = jnp.zeros_like(zbuf)
        for i in range(8):
            pltpu.make_async_copy(zbuf, out_hbm.at[:, i * 1024:(i + 1) * 1024], fill_sem.at[i]).start()
        pl.semaphore_wait(barrier, 38)

    mine = dec_hbm.at[chip, core]

    sibling = plane(seq + 1 - 2 * core)

    def finish_own():
        await_first = prefilling

        @pl.when(await_first)
        def _():
            await_bytes(fz.at[0:4], din.at[5])

        @pl.when(jnp.logical_not(await_first))
        def _():
            await_bytes(fz.at[0:3], din.at[5])

        to = lax.broadcasted_iota(jnp.int32, (64, 64), 0)
        at = lax.broadcasted_iota(jnp.int32, (64, 64), 1)
        order = (at == ((to // 4) % 4) * 16 + (to % 4) * 4 + to // 16).astype(jnp.bfloat16)
        slab = jnp.dot(order, fz[0:4].reshape(64, 256), preferred_element_type=jnp.float32)
        for i in range(16):
            fo[i // 4, i % 4] = slab[4 * i:4 * i + 4].astype(jnp.bfloat16)
        pltpu.make_async_copy(fo, mine, dlocal.at[1]).start()

        def spread(d, carry):
            other = ((chip + d) % 16) * 2 + core
            remote(fo, mine, dout.at[6], din.at[6], plane(other)).start()
            return carry

        lax.fori_loop(1, 16, spread, 0)

    def finish_pair():
        pltpu.make_async_copy(fo, mine, dlocal.at[1]).wait()
        await_bytes(dec_hbm.at[0:15, 0], din.at[6])
        remote(dec_hbm.at[:, core], dec_hbm.at[:, core], dout.at[7], din.at[7], sibling).start()

    def finish_wait():
        await_bytes(dec_hbm.at[0:15, 0], dout.at[6])
        await_bytes(dec_hbm.at[:, 0], dout.at[7])
        await_bytes(dec_hbm.at[:, 0], din.at[7])

    @pl.when(prefilling)
    def _():
        right, left = (y + 1) % 4, (y + 3) % 4

        def device(xx, yy):
            return plane((xx * 4 + yy) * 2 + core)

        for j in range(HALF):
            remote(kv_columns(1 - core, j), own_rows(j), send_sem.at[10], slot_sem.at[0, j], sibling).start()

        def wait_slot(slot, j):
            @pl.when(chip >= slot)
            def _():
                await_bytes(chunk(slot, j), slot_sem.at[slot, j])

        def send(kind, src, dst, j, xx, yy):
            remote(chunk(src, j), chunk(dst, j), send_sem.at[kind], slot_sem.at[dst, j], device(xx, yy)).start()

        def own_wait(j):
            pltpu.make_async_copy(kv_columns(core, j), own_rows(j), own_sem.at[j]).wait()
            await_bytes(own_rows(j), slot_sem.at[0, j])

        def own(j):
            @pl.when(x < 3)
            def _():
                send(0, 0, 4, j, (x + 1) % 4, y)

        def own_along_y(j):
            @pl.when(y < 3)
            def _():
                send(2, 0, 1, j, x, right)

            @pl.when(y == 0)
            def _():
                send(3, 0, 3, j, x, left)

        right_dst = jnp.where(y < 3, 5, 1)
        left_dst = jnp.where(y > 0, 3, 7)
        right_fwd = jnp.where(y < 3, 1, 5)
        left_fwd = jnp.where(y > 0, 7, 3)

        def inject(j):
            wait_slot(4, j)

            @pl.when(x >= 1)
            def _():
                send(4, 4, right_dst, j, x, right)
                send(5, 4, left_dst, j, x, left)

            @pl.when(jnp.logical_and(x >= 1, x < 3))
            def _():
                send(1, 4, 8, j, (x + 1) % 4, y)

        def inject_far(j):
            wait_slot(8, j)

            @pl.when(jnp.logical_and(x >= 2, y == 3))
            def _():
                send(6, 8, 5, j, x, right)

            @pl.when(jnp.logical_and(x >= 2, y > 0))
            def _():
                send(7, 8, 7, j, x, left)

        def forward(j):
            wait_slot(right_fwd, j)

            @pl.when(chip >= right_fwd)
            def _():
                send(8, right_fwd, 2, j, x, right)

            wait_slot(left_fwd, j)

            @pl.when(chip >= left_fwd)
            def _():
                send(9, left_fwd, 6, j, x, left)

        def rest(j):
            wait_slot(6 - right_fwd, j)
            wait_slot(10 - left_fwd, j)
            wait_slot(2, j)
            wait_slot(6, j)

        counts = [lengths[role, i] for i in range(4)]
        served = [serves[role, i] for i in range(4)]
        blocks = [(n + 127) // 128 for n in counts]
        starts = [0, blocks[0], blocks[0] + blocks[1], blocks[0] + blocks[1] + blocks[2]]

        def pick(block, values):
            chosen = values[0]
            for i in range(1, 4):
                chosen = jnp.where(block >= starts[i], values[i], chosen)
            return chosen

        firsts, lives = [], []
        for e in range(2):
            block = 2 * chip + e
            first = pick(block, starts)
            firsts.append(first - (2 * chip - 15 + e))
            lives.append(pick(block, counts) - (block - first) * 128)

        at_home = home == core

        def spread_queries():
            await_bytes(qz, din.at[0])
            qb[...] = qz[...].reshape(32, HD).astype(jnp.bfloat16)

            @pl.when(at_home)
            def _():
                qd[seq % 16] = qb[...]

            def one(d, carry):
                other = ((chip + d) % 16) * 2 + home

                @pl.when(other != seq)
                def _():
                    remote(qb, qd.at[seq % 16], dout.at[1], din.at[1], plane(other)).start()

                return carry

            lax.fori_loop(0, 16, one, 0)

        def await_many(buffer, sem):
            @pl.when(at_home)
            def _():
                await_bytes(buffer.at[0:15], sem)

            @pl.when(jnp.logical_not(at_home))
            def _():
                await_bytes(buffer, sem)

        lanes = lax.broadcasted_iota(jnp.int32, (32, HD), 1)

        def partial_terms():
            await_many(qd, din.at[1])
            stats = []
            for e in range(2):
                group = pick(2 * chip + e, served)
                live = lives[e]

                for j in range(HALF):
                    q = jnp.zeros((4, 8, HD), jnp.float32)
                    wide = qd[4 * j:4 * j + 4].astype(jnp.float32).reshape(4, PG, 8, HD)
                    for g in range(PG):
                        q = jnp.where(group == g, wide[:, g], q)
                    q = q.reshape(32, HD).astype(jnp.bfloat16)
                    keys = kvbuf[j, 2048 + 128 * e:2176 + 128 * e, 0:HD]
                    values = kvbuf[j, 2048 + 128 * e:2176 + 128 * e, HD:2 * HD]
                    s = lax.dot_general(q, keys, (((1,), (1,)), ((), ())), preferred_element_type=jnp.float32)
                    s = jnp.where(lanes < live, s, NEG)
                    m = jnp.max(s, axis=1, keepdims=True)
                    w = jnp.exp2((s - m) * factor)
                    total = jnp.sum(w, axis=1, keepdims=True)
                    o = jnp.dot(w.astype(jnp.bfloat16), values, preferred_element_type=jnp.float32)
                    ds[4 * j:4 * j + 4, e] = o.reshape(4, 8, HD)
                    stat = jnp.where(lanes < 64, m, total)
                    if e == 0:
                        stats.append(stat)
                    else:
                        stat = jnp.where(lanes % 64 < 32, stats[j], stat)
                        ds[4 * j:4 * j + 4, 2] = stat.reshape(4, 8, HD)

            @pl.when(at_home)
            def _():
                dr[chip] = ds[seq % 16]

            def out(d, carry):
                other = 16 * core + (chip + d) % 16

                @pl.when(other != seq)
                def _():
                    remote(ds.at[(chip + d) % 16], dr.at[chip], dout.at[2], din.at[2], plane(other)).start()

                return carry

            lax.fori_loop(0, 16, out, 0)

        which = lax.broadcasted_iota(jnp.int32, (PG, 8, HD), 0)

        def combine_terms():
            await_many(dr, din.at[2])

            terms = []
            top = jnp.full((PG, 8, HD), NEG, jnp.float32)
            for b in range(32):
                flag = which == pick(jnp.int32(b), served)
                m = jnp.broadcast_to(dr[b // 2, 2][:, 32 * (b % 2):32 * (b % 2) + 1], (8, HD))[None]
                top = jnp.maximum(top, jnp.where(flag, m, NEG))
                terms.append((flag, m))
            total = jnp.zeros((PG, 8, HD), jnp.float32)
            mixed = jnp.zeros((PG, 8, HD), jnp.float32)
            for b in range(32):
                flag, m = terms[b]
                part = jnp.broadcast_to(dr[b // 2, 2][:, 64 + 32 * (b % 2):65 + 32 * (b % 2)], (8, HD))[None]
                add = jnp.where(flag, jnp.exp2((jnp.minimum(m, top) - top) * factor), 0.0)
                total = total + add * part
                mixed = mixed + add * dr[b // 2, b % 2][None]
            lane3 = lax.broadcasted_iota(jnp.int32, (PG, 8, HD), 2)
            cs[:, 0] = mixed
            cs[:, 1] = jnp.where(lane3 < 64, top, total)
            for g in range(PG):
                remote(cs.at[g], dz.at[role], dout.at[3], din.at[3], line(PG + g)).start()

        own_wait(0)
        own(0)

        own_along_y(0)

        for slot in range(1, SLOTS):
            @pl.when(chip < slot)
            def _(slot=slot):
                for j in range(HALF):
                    kvbuf[j, (8 - slot) * 256:(9 - slot) * 256, :] = jnp.zeros((256, 256), jnp.bfloat16)

        at = lax.broadcasted_iota(jnp.int32, (128, 128), 0)
        to = lax.broadcasted_iota(jnp.int32, (128, 128), 1)
        for i in range(ROWS // 128):
            eye[i * 128:(i + 1) * 128, :] = (at == to).astype(jnp.bfloat16)
        for e in range(2):
            for w in range(15):
                level = jnp.where(firsts[e] <= w, 0.0, NEG)
                maskbuf[e, w * 128:(w + 1) * 128, :] = jnp.full((128, 128), level, jnp.float32).astype(jnp.bfloat16)
            maskbuf[e, 1920:2048, :] = jnp.where(at <= to, 0.0, NEG).astype(jnp.bfloat16)

        spread_queries()

        def start_q(h, carry):
            remote(q_columns(1 - core, h), qbuf.at[core, h], send_sem.at[11], q_sem.at[0], sibling).start()
            return carry

        lax.fori_loop(0, 32, start_q, 0)
        inject(0)
        for j in range(1, HALF):
            own_wait(j)
        own(1)
        own_along_y(1)
        partial_terms()
        inject_far(0)
        forward(0)
        inject(1)
        own(2)
        own_along_y(2)
        combine_terms()
        rest(0)

        await_bytes(qbuf.at[0], q_sem.at[0])
        await_bytes(qbuf.at[0], q_sem.at[1])

        row_in = lax.broadcasted_iota(jnp.int32, (ROWS, 128), 0) & 127
        ones = jnp.ones((KT, HD), jnp.bfloat16)

        def place(n):
            return n // 2, n % 2, n // 2 * GROUP

        def key_rows(j, e, kt):
            return j, pl.ds(pl.multiple_of(128 + e * 128 + kt * KT, 128), KT)

        def weave(current, following):
            if following is not None:
                n, scores, peaks = following
                j, e, base = place(n)
                q = jnp.concatenate([qbuf[e, pl.ds(base, GROUP)].reshape(ROWS, HD), eye[...]], axis=1)
                peak = None
            if current is not None:
                cn, cscores, cpeaks = current
                cj, ce, cbase = place(cn)
                total = None
            for kt in range(WINDOW // KT):
                if following is not None:
                    rows = key_rows(j, e, kt)
                    masked_keys = jnp.concatenate(
                        [kvbuf[rows[0], rows[1], 0:HD], maskbuf[e, kt * KT:(kt + 1) * KT, :]], axis=1)
                    s = lax.dot_general(
                        q, masked_keys, (((1,), (1,)), ((), ())), preferred_element_type=jnp.float32)
                if current is not None:
                    weights = [
                        jnp.exp2((cscores[:, kt * KT + i * 128:kt * KT + (i + 1) * 128] - cpeaks[...]) * factor)
                        for i in range(KT // 128)
                    ]
                    rows = key_rows(cj, ce, kt)
                    product = jnp.dot(
                        jnp.concatenate(weights, axis=1).astype(jnp.bfloat16),
                        jnp.concatenate([kvbuf[rows[0], rows[1], HD:2 * HD], ones], axis=1),
                        preferred_element_type=jnp.float32)
                    total = product if total is None else total + product
                if following is not None:
                    pieces = [s[:, i * 128:(i + 1) * 128] for i in range(KT // 128)]
                    for i, piece in enumerate(pieces):
                        scores[:, kt * KT + i * 128:kt * KT + (i + 1) * 128] = piece
                    while len(pieces) > 1:
                        pieces = [jnp.maximum(a, b) for a, b in zip(pieces[::2], pieces[1::2])]
                    peak = pieces[0] if peak is None else jnp.maximum(peak, pieces[0])
            if following is not None:
                peaks[...] = jnp.broadcast_to(jnp.max(peak, axis=1, keepdims=True), (ROWS, 128))
            if current is not None:
                live = jnp.where(ce == 0, lives[0], lives[1])
                mixed = total[:, :HD] / total[:, HD:]
                mixed = jnp.where(row_in < live, mixed, 0.0).astype(jnp.bfloat16)
                obuf[ce, pl.ds(cbase, GROUP)] = mixed.reshape(GROUP, BLOCK, HD)
                for i in range(GROUP):
                    columns = out_hbm.at[:, pl.ds(pl.multiple_of((core * 32 + cbase + i) * HD, HD), HD)]

                    @pl.when(ce == core)
                    def _(i=i, columns=columns):
                        pltpu.make_async_copy(obuf.at[ce, cbase + i], columns, out_sem.at[0]).start()

                    @pl.when(ce != core)
                    def _(i=i, columns=columns):
                        remote(obuf.at[ce, cbase + i], columns, send_sem.at[12], out_sem.at[1], sibling).start()

        weave(None, (jnp.int32(0), sbuf, peak0))
        inject_far(1)
        inject(2)
        own(3)
        own_along_y(3)
        forward(1)

        def pair(i, carry):
            weave((2 * i, sbuf, peak0), (2 * i + 1, sbuf1, peak1))

            @pl.when(i == 0)
            def _():
                inject_far(2)
                inject(3)

            rest(i + 1)
            weave((2 * i + 1, sbuf1, peak1), (2 * i + 2, sbuf, peak0))

            @pl.when(i == 0)
            def _():
                forward(2)
                inject_far(3)

            @pl.when(i == 1)
            def _():
                forward(3)

            return carry

        lax.fori_loop(0, 3, pair, 0)
        finish_own()
        weave((jnp.int32(6), sbuf, peak0), (jnp.int32(7), sbuf1, peak1))
        finish_pair()
        weave((jnp.int32(7), sbuf1, peak1), None)

        span = kvbuf.at[:, 0:256, :]

        def sent(kind, condition):
            @pl.when(condition)
            def _():
                await_bytes(span, send_sem.at[kind])

        sent(0, x < 3)
        sent(1, jnp.logical_and(x >= 1, x < 3))
        sent(2, y < 3)
        sent(3, y == 0)
        sent(4, x >= 1)
        sent(5, x >= 1)
        sent(6, jnp.logical_and(x >= 2, y == 3))
        sent(7, jnp.logical_and(x >= 2, y > 0))
        sent(8, chip >= right_fwd)
        sent(9, chip >= left_fwd)
        await_bytes(kvbuf.at[:, 0:128, :], send_sem.at[10])
        await_bytes(qbuf.at[0], send_sem.at[11])
        await_bytes(obuf.at[0], send_sem.at[12])
        await_bytes(obuf.at[0], out_sem.at[0])
        await_many(qd, dout.at[1])
        await_many(dr, dout.at[2])
        await_bytes(cs, dout.at[3])
        await_bytes(obuf.at[0], out_sem.at[1])
        finish_wait()

    @pl.when(role >= PG)
    def _():
        group = role - PG
        pltpu.make_async_copy(raw_q, vq, own_sem.at[0]).wait()
        pltpu.make_async_copy(vkv, vkv, own_sem.at[1]).wait()
        for t in range(4):
            tall[0, 4 * t:4 * t + 4, :] = vq[t].astype(jnp.float32)
            tall[1, 4 * t:4 * t + 4, :] = vkv[t].astype(jnp.float32)
        to = lax.broadcasted_iota(jnp.int32, (32, 16), 0)
        at = lax.broadcasted_iota(jnp.int32, (32, 16), 1)
        ordered = jnp.zeros((32, HD), jnp.float32)
        for h in range(2):
            chosen = jnp.logical_and((to & 7) // 4 == h, at == (to & 3) * 4 + to // 8).astype(jnp.bfloat16)
            ordered = ordered + jnp.dot(
                chosen, tall[0, :, h * HD:(h + 1) * HD].astype(jnp.bfloat16), preferred_element_type=jnp.float32)
        dq[...] = ordered.reshape(PG, 8, HD)
        for p in range(PG):
            remote(dq.at[p], qz.at[group], dout.at[0], din.at[0], line(p)).start()
        pltpu.make_async_copy(w_hbm, wbuf, dlocal.at[0]).wait()
        await_bytes(dz, din.at[3])
        step = lax.broadcasted_iota(jnp.int32, (8, HD), 0) & 3
        to = lax.broadcasted_iota(jnp.int32, (32, 16), 0)
        at = lax.broadcasted_iota(jnp.int32, (32, 16), 1)
        chosen = jnp.logical_and((to & 7) < 4, at == (to & 3) * 4 + to // 8).astype(jnp.bfloat16)
        new_rows = [
            jnp.dot(
                chosen, tall[1, :, i * HD:(i + 1) * HD].astype(jnp.bfloat16), preferred_element_type=jnp.float32
            ).reshape(PG, 8, HD)
            for i in range(2)
        ]
        tiles = []
        for p in range(PG):
            pair = dz[p, 1]
            m = jnp.broadcast_to(pair[:, 0:1], (8, HD))
            part = jnp.broadcast_to(pair[:, 64:65], (8, HD))
            q = dq[p]
            scores = []
            for t in range(4):
                s = jnp.sum(q * new_rows[0][p, t:t + 1, :], axis=1, keepdims=True)
                scores.append(jnp.where(step >= t, jnp.broadcast_to(s, (8, HD)), NEG))
            top = m
            for s in scores:
                top = jnp.maximum(top, s)
            old = jnp.exp2((m - top) * factor)
            total = part * old
            mixed = dz[p, 0] * old
            for t in range(4):
                w = jnp.exp2((scores[t] - top) * factor)
                total = total + w
                mixed = mixed + w * new_rows[1][p, t:t + 1, :]
            tiles.append(mixed / total)
        rows = jnp.concatenate(tiles, axis=0).astype(jnp.bfloat16)
        to = lax.broadcasted_iota(jnp.int32, (16, 32), 0)
        at = lax.broadcasted_iota(jnp.int32, (16, 32), 1)
        halves = []
        for h in range(2):
            chosen = (at == (to // 4) * 8 + h * 4 + to % 4).astype(jnp.bfloat16)
            halves.append(jnp.dot(chosen, rows, preferred_element_type=jnp.float32).astype(jnp.bfloat16))
        attended = jnp.concatenate(halves, axis=1)

        def project(i, carry):
            others = [(seq + 4 * i + d) % 32 for d in range(4)]
            for other in others:
                columns = pl.ds(pl.multiple_of(other * 256, 256), 256)
                rs_s[other] = jnp.dot(
                    attended, wbuf[:, columns], preferred_element_type=jnp.float32).astype(jnp.bfloat16)
            for other in others:
                @pl.when(other != seq)
                def _(other=other):
                    remote(rs_s.at[other], rs_r.at[seq], dout.at[4], din.at[4], plane(other)).start()

            return carry

        lax.fori_loop(0, 8, project, 0)
        rs_r[seq] = rs_s[seq]
        await_bytes(rs_r.at[0:31], din.at[4])

        def add(i, total):
            four = [rs_r[4 * i + d].astype(jnp.float32) for d in range(4)]
            return total + ((four[0] + four[1]) + (four[2] + four[3]))

        summed = lax.fori_loop(0, 8, add, jnp.zeros((16, 256), jnp.float32))
        fz[group] = summed.astype(jnp.bfloat16)
        for d in range(1, 2 * PG):
            remote(fz.at[group], fz.at[group], dout.at[5], din.at[5], line((role + d) % (2 * PG))).start()
        finish_own()
        finish_pair()
        await_bytes(qz, dout.at[0])
        await_bytes(rs_s.at[0:31], dout.at[4])
        await_bytes(fz.at[0:7], dout.at[5])
        for i in range(8):
            pltpu.make_async_copy(zbuf, out_hbm.at[:, i * 1024:(i + 1) * 1024], fill_sem.at[i]).wait()
        finish_wait()


def fused(prompt_lengths, decode_group, queries, kv, dq, fresh, out_weight):
    smem = pl.BlockSpec(memory_space=pltpu.SMEM)
    hbm = pl.BlockSpec(memory_space=pl.ANY)
    return pl.pallas_call(
        fused_kernel,
        out_shape=[
            jax.ShapeDtypeStruct((BLOCK, H * HD), jnp.bfloat16),
            jax.ShapeDtypeStruct((16, 2, 4, PG, PG, 256), jnp.bfloat16),
        ],
        in_specs=[smem, smem, hbm, hbm, hbm, hbm, hbm],
        out_specs=[hbm, hbm],
        scratch_shapes=[
            pltpu.VMEM((2, 32, BLOCK, HD), jnp.bfloat16),
            pltpu.VMEM((HALF, SLOTS * 256, 256), jnp.bfloat16),
            pltpu.VMEM((ROWS, WINDOW), jnp.float32),
            pltpu.VMEM((ROWS, WINDOW), jnp.float32),
            pltpu.VMEM((ROWS, 128), jnp.float32),
            pltpu.VMEM((ROWS, 128), jnp.float32),
            pltpu.VMEM((ROWS, 128), jnp.bfloat16),
            pltpu.VMEM((2, WINDOW, 128), jnp.bfloat16),
            pltpu.VMEM((2, 32, BLOCK, HD), jnp.bfloat16),
            pltpu.VMEM((BLOCK, 1024), jnp.bfloat16),
            pltpu.VMEM((256, 8192), jnp.bfloat16),
            pltpu.VMEM((4, PG, 256), jnp.bfloat16),
            pltpu.VMEM((4, PG, 256), jnp.bfloat16),
            pltpu.VMEM((2, 4 * PG, 256), jnp.float32),
            pltpu.VMEM((PG, 8, HD), jnp.float32),
            pltpu.VMEM((PG, 8, HD), jnp.float32),
            pltpu.VMEM((32, HD), jnp.bfloat16),
            pltpu.VMEM((16, 32, HD), jnp.bfloat16),
            pltpu.VMEM((16, 3, 8, HD), jnp.float32),
            pltpu.VMEM((16, 3, 8, HD), jnp.float32),
            pltpu.VMEM((PG, 2, 8, HD), jnp.float32),
            pltpu.VMEM((PG, 2, 8, HD), jnp.float32),
            pltpu.VMEM((32, 16, 256), jnp.bfloat16),
            pltpu.VMEM((32, 16, 256), jnp.bfloat16),
            pltpu.VMEM((8, 16, 256), jnp.bfloat16),
            pltpu.VMEM((4, PG, PG, 256), jnp.bfloat16),
            pltpu.SemaphoreType.DMA((SLOTS, HALF)),
            pltpu.SemaphoreType.DMA((2,)),
            pltpu.SemaphoreType.DMA((HALF,)),
            pltpu.SemaphoreType.DMA((2,)),
            pltpu.SemaphoreType.DMA((8,)),
            pltpu.SemaphoreType.DMA((13,)),
            pltpu.SemaphoreType.DMA((8,)),
            pltpu.SemaphoreType.DMA((8,)),
            pltpu.SemaphoreType.DMA((2,)),
        ],
        compiler_params=pltpu.CompilerParams(
            collective_id=0, has_side_effects=True, vmem_limit_bytes=62 * 1024 * 1024
        ),
        cost_estimate=pl.CostEstimate(flops=17_000_000_000, bytes_accessed=16_000_000, transcendentals=17_000_000),
    )(prompt_lengths, decode_group, queries, kv, dq, fresh, out_weight)


def on_device(prefill_queries, prefill_kv, prompt_lengths, decode_group, decode_queries, decode_kv, out_weight):
    prefill_out, decode_out = fused(
        prompt_lengths, decode_group, prefill_queries[0], prefill_kv[0], decode_queries[0], decode_kv[0], out_weight
    )
    decode_out = decode_out.reshape(32, 4, PG, PG, 256).transpose(1, 2, 3, 0, 4).reshape(4, PG, PG, -1)
    return prefill_out[None], decode_out


def solution(mesh):
    in_specs = (
        P("role", "seq", None),
        P("role", "seq", None),
        P(),
        P(),
        P("role", None, None, "seq"),
        P("role", None, None, None),
        P("seq", None),
    )
    out_specs = (P("role", "seq", None), P())
    return jax.shard_map(on_device, mesh=mesh, in_specs=in_specs, out_specs=out_specs, check_vma=False)
```

```python
import functools

import jax
import jax.numpy as jnp
from jax import lax
from jax.experimental import pallas as pl
from jax.experimental.pallas import tpu as pltpu
from jax.sharding import PartitionSpec as P

MESH = pl.DeviceIdType.MESH
H = 64
KVH = 8
HD = 128
BLOCK = 128
PG = 4
NEG = -1e30
SCALE = HD**-0.5
LOG2E = 1.4426950408889634
SLOTS = 9
HALF = KVH // 2
GROUP = H // KVH
ROWS = 512
KT = 1024
WINDOW = 2048


def fused_kernel(
    lengths, serves, q_hbm, kv_hbm, raw_q, raw_kv, w_hbm, out_hbm, dec_hbm,
    qbuf, kvbuf, sbuf, sbuf1, peak0, peak1, eye, maskbuf, obuf, zbuf, wbuf, vq, vkv, tall, dq, qz, qb, qd, ds, dr, cs, dz, rs_s, rs_r, fz, fo,
    slot_sem, q_sem, own_sem, out_sem, fill_sem, send_sem, din, dout, dlocal
):
    role = lax.axis_index("role")
    seq = lax.axis_index("seq")
    core = seq % 2
    chip = seq // 2
    y = chip % 4
    x = chip // 4
    home = seq // 16
    prefilling = role < PG
    factor = SCALE * LOG2E

    def plane(other):
        return (role, other)

    def line(other):
        return (other, seq)

    def remote(src, dst, send, recv, device):
        return pltpu.make_async_remote_copy(
            src_ref=src, dst_ref=dst, send_sem=send, recv_sem=recv, device_id=device, device_id_type=MESH)

    def await_bytes(ref, sem):
        pltpu.make_async_copy(ref, ref, sem).wait()

    def q_columns(half, h):
        return q_hbm.at[:, pl.ds(pl.multiple_of((half * 32 + h) * HD, HD), HD)]

    def kv_columns(half, j):
        return kv_hbm.at[:, pl.ds(pl.multiple_of(half * HALF * 256 + j * 256, 256), 256)]

    def chunk(slot, j):
        return kvbuf.at[j, pl.ds(pl.multiple_of((8 - slot) * 256, 256), 256), :]

    def own_rows(j):
        return kvbuf.at[j, pl.ds(pl.multiple_of(2048 + core * 128, 128), 128), :]

    barrier = pltpu.get_barrier_semaphore()

    def greet(d, carry):
        pl.semaphore_signal(barrier, inc=1, device_id=plane((seq + d) % 32), device_id_type=MESH)
        return carry

    lax.fori_loop(1, 32, greet, 0)

    @pl.when(prefilling)
    def _():
        for g in range(PG):
            pl.semaphore_signal(barrier, inc=1, device_id=line(PG + g), device_id_type=MESH)
        for j in range(HALF):
            pltpu.make_async_copy(kv_columns(core, j), own_rows(j), own_sem.at[j]).start()

        def keep_q(h, carry):
            pltpu.make_async_copy(q_columns(core, h), qbuf.at[core, h], q_sem.at[1, h // GROUP]).start()
            return carry

        lax.fori_loop(0, 32, keep_q, 0)
        pl.semaphore_wait(barrier, 35)

    @pl.when(role >= PG)
    def _():
        for d in range(1, 2 * PG):
            pl.semaphore_signal(barrier, inc=1, device_id=line((role + d) % (2 * PG)), device_id_type=MESH)
        pltpu.make_async_copy(raw_q, vq, own_sem.at[0]).start()
        kv_part = raw_kv.at[:, :, pl.ds(pl.multiple_of(seq // 4 * 256, 256), 256)]
        pltpu.make_async_copy(kv_part, vkv, own_sem.at[1]).start()
        pltpu.make_async_copy(w_hbm, wbuf, dlocal.at[0]).start()
        zbuf[...] = jnp.zeros_like(zbuf)
        for i in range(8):
            pltpu.make_async_copy(zbuf, out_hbm.at[:, i * 1024:(i + 1) * 1024], fill_sem.at[i]).start()
        pl.semaphore_wait(barrier, 38)

    mine = dec_hbm.at[chip, core]

    sibling = plane(seq + 1 - 2 * core)

    def finish_own():
        await_first = prefilling

        @pl.when(await_first)
        def _():
            await_bytes(fz.at[0:4], din.at[5])

        @pl.when(jnp.logical_not(await_first))
        def _():
            await_bytes(fz.at[0:3], din.at[5])

        to = lax.broadcasted_iota(jnp.int32, (64, 64), 0)
        at = lax.broadcasted_iota(jnp.int32, (64, 64), 1)
        order = (at == ((to // 4) % 4) * 16 + (to % 4) * 4 + to // 16).astype(jnp.bfloat16)
        slab = jnp.dot(order, fz[0:4].reshape(64, 256), preferred_element_type=jnp.float32)
        for i in range(16):
            fo[i // 4, i % 4] = slab[4 * i:4 * i + 4].astype(jnp.bfloat16)
        pltpu.make_async_copy(fo, mine, dlocal.at[1]).start()

        def spread(d, carry):
            other = ((chip + d) % 16) * 2 + core
            remote(fo, mine, dout.at[6], din.at[6], plane(other)).start()
            return carry

        lax.fori_loop(1, 16, spread, 0)

    def finish_pair():
        pltpu.make_async_copy(fo, mine, dlocal.at[1]).wait()
        await_bytes(dec_hbm.at[0:15, 0], din.at[6])
        remote(dec_hbm.at[:, core], dec_hbm.at[:, core], dout.at[7], din.at[7], sibling).start()

    def finish_wait():
        await_bytes(dec_hbm.at[0:15, 0], dout.at[6])
        await_bytes(dec_hbm.at[:, 0], dout.at[7])
        await_bytes(dec_hbm.at[:, 0], din.at[7])

    @pl.when(prefilling)
    def _():
        right, left = (y + 1) % 4, (y + 3) % 4

        def device(xx, yy):
            return plane((xx * 4 + yy) * 2 + core)

        for j in range(HALF):
            remote(kv_columns(1 - core, j), own_rows(j), send_sem.at[10], slot_sem.at[0, j], sibling).start()

        def wait_slot(slot, j):
            @pl.when(chip >= slot)
            def _():
                await_bytes(chunk(slot, j), slot_sem.at[slot, j])

        def send(kind, src, dst, j, xx, yy):
            remote(chunk(src, j), chunk(dst, j), send_sem.at[kind], slot_sem.at[dst, j], device(xx, yy)).start()

        def own_wait(j):
            pltpu.make_async_copy(kv_columns(core, j), own_rows(j), own_sem.at[j]).wait()
            await_bytes(own_rows(j), slot_sem.at[0, j])

        def own(j):
            @pl.when(x < 3)
            def _():
                send(0, 0, 4, j, (x + 1) % 4, y)

        def own_along_y(j):
            @pl.when(y < 3)
            def _():
                send(2, 0, 1, j, x, right)

            @pl.when(y == 0)
            def _():
                send(3, 0, 3, j, x, left)

        right_dst = jnp.where(y < 3, 5, 1)
        left_dst = jnp.where(y > 0, 3, 7)
        right_fwd = jnp.where(y < 3, 1, 5)
        left_fwd = jnp.where(y > 0, 7, 3)

        def inject(j):
            wait_slot(4, j)

            @pl.when(x >= 1)
            def _():
                send(4, 4, right_dst, j, x, right)
                send(5, 4, left_dst, j, x, left)

            @pl.when(jnp.logical_and(x >= 1, x < 3))
            def _():
                send(1, 4, 8, j, (x + 1) % 4, y)

        def inject_far(j):
            wait_slot(8, j)

            @pl.when(jnp.logical_and(x >= 2, y == 3))
            def _():
                send(6, 8, 5, j, x, right)

            @pl.when(jnp.logical_and(x >= 2, y > 0))
            def _():
                send(7, 8, 7, j, x, left)

        def forward(j):
            wait_slot(right_fwd, j)

            @pl.when(chip >= right_fwd)
            def _():
                send(8, right_fwd, 2, j, x, right)

            wait_slot(left_fwd, j)

            @pl.when(chip >= left_fwd)
            def _():
                send(9, left_fwd, 6, j, x, left)

        def rest(j):
            for side in range(2):
                await_bytes(qbuf.at[0, 0:GROUP], q_sem.at[side, j])
            wait_slot(6 - right_fwd, j)
            wait_slot(10 - left_fwd, j)
            wait_slot(2, j)
            wait_slot(6, j)

        counts = [lengths[role, i] for i in range(4)]
        served = [serves[role, i] for i in range(4)]
        blocks = [(n + 127) // 128 for n in counts]
        starts = [0, blocks[0], blocks[0] + blocks[1], blocks[0] + blocks[1] + blocks[2]]

        def pick(block, values):
            chosen = values[0]
            for i in range(1, 4):
                chosen = jnp.where(block >= starts[i], values[i], chosen)
            return chosen

        firsts, lives = [], []
        for e in range(2):
            block = 2 * chip + e
            first = pick(block, starts)
            firsts.append(first - (2 * chip - 15 + e))
            lives.append(pick(block, counts) - (block - first) * 128)

        at_home = home == core

        def spread_queries():
            await_bytes(qz, din.at[0])
            qb[...] = qz[...].reshape(32, HD).astype(jnp.bfloat16)

            @pl.when(at_home)
            def _():
                qd[seq % 16] = qb[...]

            def one(d, carry):
                other = ((chip + d) % 16) * 2 + home

                @pl.when(other != seq)
                def _():
                    remote(qb, qd.at[seq % 16], dout.at[1], din.at[1], plane(other)).start()

                return carry

            lax.fori_loop(0, 16, one, 0)

        def await_many(buffer, sem):
            @pl.when(at_home)
            def _():
                await_bytes(buffer.at[0:15], sem)

            @pl.when(jnp.logical_not(at_home))
            def _():
                await_bytes(buffer, sem)

        lanes = lax.broadcasted_iota(jnp.int32, (32, HD), 1)

        def partial_terms():
            await_many(qd, din.at[1])
            stats = []
            for e in range(2):
                group = pick(2 * chip + e, served)
                live = lives[e]

                for j in range(HALF):
                    q = jnp.zeros((4, 8, HD), jnp.float32)
                    wide = qd[4 * j:4 * j + 4].astype(jnp.float32).reshape(4, PG, 8, HD)
                    for g in range(PG):
                        q = jnp.where(group == g, wide[:, g], q)
                    q = q.reshape(32, HD).astype(jnp.bfloat16)
                    keys = kvbuf[j, 2048 + 128 * e:2176 + 128 * e, 0:HD]
                    values = kvbuf[j, 2048 + 128 * e:2176 + 128 * e, HD:2 * HD]
                    s = lax.dot_general(q, keys, (((1,), (1,)), ((), ())), preferred_element_type=jnp.float32)
                    s = jnp.where(lanes < live, s, NEG)
                    m = jnp.max(s, axis=1, keepdims=True)
                    w = jnp.exp2((s - m) * factor)
                    total = jnp.sum(w, axis=1, keepdims=True)
                    o = jnp.dot(w.astype(jnp.bfloat16), values, preferred_element_type=jnp.float32)
                    ds[4 * j:4 * j + 4, e] = o.reshape(4, 8, HD)
                    stat = jnp.where(lanes < 64, m, total)
                    if e == 0:
                        stats.append(stat)
                    else:
                        stat = jnp.where(lanes % 64 < 32, stats[j], stat)
                        ds[4 * j:4 * j + 4, 2] = stat.reshape(4, 8, HD)

            @pl.when(at_home)
            def _():
                dr[chip] = ds[seq % 16]

            def out(d, carry):
                other = 16 * core + (chip + d) % 16

                @pl.when(other != seq)
                def _():
                    remote(ds.at[(chip + d) % 16], dr.at[chip], dout.at[2], din.at[2], plane(other)).start()

                return carry

            lax.fori_loop(0, 16, out, 0)

        which = lax.broadcasted_iota(jnp.int32, (PG, 8, HD), 0)

        def combine_terms():
            await_many(dr, din.at[2])

            terms = []
            top = jnp.full((PG, 8, HD), NEG, jnp.float32)
            for b in range(32):
                flag = which == pick(jnp.int32(b), served)
                m = jnp.broadcast_to(dr[b // 2, 2][:, 32 * (b % 2):32 * (b % 2) + 1], (8, HD))[None]
                top = jnp.maximum(top, jnp.where(flag, m, NEG))
                terms.append((flag, m))
            total = jnp.zeros((PG, 8, HD), jnp.float32)
            mixed = jnp.zeros((PG, 8, HD), jnp.float32)
            for b in range(32):
                flag, m = terms[b]
                part = jnp.broadcast_to(dr[b // 2, 2][:, 64 + 32 * (b % 2):65 + 32 * (b % 2)], (8, HD))[None]
                add = jnp.where(flag, jnp.exp2((jnp.minimum(m, top) - top) * factor), 0.0)
                total = total + add * part
                mixed = mixed + add * dr[b // 2, b % 2][None]
            lane3 = lax.broadcasted_iota(jnp.int32, (PG, 8, HD), 2)
            cs[:, 0] = mixed
            cs[:, 1] = jnp.where(lane3 < 64, top, total)
            for g in range(PG):
                remote(cs.at[g], dz.at[role], dout.at[3], din.at[3], line(PG + g)).start()

        def start_q(h, carry):
            remote(q_columns(1 - core, h), qbuf.at[core, h], send_sem.at[11], q_sem.at[0, h // GROUP], sibling).start()
            return carry

        own_wait(0)
        own(0)

        own_along_y(0)
        lax.fori_loop(0, GROUP, start_q, 0)

        for slot in range(1, SLOTS):
            @pl.when(chip < slot)
            def _(slot=slot):
                for j in range(HALF):
                    kvbuf[j, (8 - slot) * 256:(9 - slot) * 256, :] = jnp.zeros((256, 256), jnp.bfloat16)

        at = lax.broadcasted_iota(jnp.int32, (128, 128), 0)
        to = lax.broadcasted_iota(jnp.int32, (128, 128), 1)
        for i in range(ROWS // 128):
            eye[i * 128:(i + 1) * 128, :] = (at == to).astype(jnp.bfloat16)
        for e in range(2):
            for w in range(15):
                level = jnp.where(firsts[e] <= w, 0.0, NEG)
                maskbuf[e, w * 128:(w + 1) * 128, :] = jnp.full((128, 128), level, jnp.float32).astype(jnp.bfloat16)
            maskbuf[e, 1920:2048, :] = jnp.where(at <= to, 0.0, NEG).astype(jnp.bfloat16)

        spread_queries()

        lax.fori_loop(GROUP, 32, start_q, 0)
        inject(0)
        for j in range(1, HALF):
            own_wait(j)
        own(1)
        own_along_y(1)
        partial_terms()
        inject_far(0)
        forward(0)
        inject(1)
        own(2)
        own_along_y(2)
        rest(0)

        row_in = lax.broadcasted_iota(jnp.int32, (ROWS, 128), 0) & 127
        ones = jnp.ones((KT, HD), jnp.bfloat16)

        def place(n):
            j, u = n // 4, n % 4
            return j, u // 2, j * GROUP + (u % 2) * 4

        def key_rows(j, e, kt):
            return j, pl.ds(pl.multiple_of(128 + e * 128 + kt * KT, 128), KT)

        def weave(current, following):
            if following is not None:
                n, scores, peaks = following
                j, e, base = place(n)
                q = jnp.concatenate([qbuf[e, pl.ds(base, 4)].reshape(ROWS, HD), eye[...]], axis=1)
                peak = None
            if current is not None:
                cn, cscores, cpeaks = current
                cj, ce, cbase = place(cn)
                total = None
            for kt in range(WINDOW // KT):
                if following is not None:
                    rows = key_rows(j, e, kt)
                    masked_keys = jnp.concatenate(
                        [kvbuf[rows[0], rows[1], 0:HD], maskbuf[e, kt * KT:(kt + 1) * KT, :]], axis=1)
                    s = lax.dot_general(
                        q, masked_keys, (((1,), (1,)), ((), ())), preferred_element_type=jnp.float32)
                if current is not None:
                    weights = [
                        jnp.exp2((cscores[:, kt * KT + i * 128:kt * KT + (i + 1) * 128] - cpeaks[...]) * factor)
                        for i in range(KT // 128)
                    ]
                    rows = key_rows(cj, ce, kt)
                    product = jnp.dot(
                        jnp.concatenate(weights, axis=1).astype(jnp.bfloat16),
                        jnp.concatenate([kvbuf[rows[0], rows[1], HD:2 * HD], ones], axis=1),
                        preferred_element_type=jnp.float32)
                    total = product if total is None else total + product
                if following is not None:
                    pieces = [s[:, i * 128:(i + 1) * 128] for i in range(KT // 128)]
                    for i, piece in enumerate(pieces):
                        scores[:, kt * KT + i * 128:kt * KT + (i + 1) * 128] = piece
                    while len(pieces) > 1:
                        pieces = [jnp.maximum(a, b) for a, b in zip(pieces[::2], pieces[1::2])]
                    peak = pieces[0] if peak is None else jnp.maximum(peak, pieces[0])
            if following is not None:
                peaks[...] = jnp.broadcast_to(jnp.max(peak, axis=1, keepdims=True), (ROWS, 128))
            if current is not None:
                live = jnp.where(ce == 0, lives[0], lives[1])
                mixed = total[:, :HD] / total[:, HD:]
                mixed = jnp.where(row_in < live, mixed, 0.0).astype(jnp.bfloat16)
                obuf[ce, pl.ds(cbase, 4)] = mixed.reshape(4, BLOCK, HD)
                for i in range(4):
                    columns = out_hbm.at[:, pl.ds(pl.multiple_of((core * 32 + cbase + i) * HD, HD), HD)]

                    @pl.when(ce == core)
                    def _(i=i, columns=columns):
                        pltpu.make_async_copy(obuf.at[ce, cbase + i], columns, out_sem.at[0]).start()

                    @pl.when(ce != core)
                    def _(i=i, columns=columns):
                        remote(obuf.at[ce, cbase + i], columns, send_sem.at[12], out_sem.at[1], sibling).start()

        weave(None, (jnp.int32(0), sbuf, peak0))
        combine_terms()

        def pair(i, carry):
            j = i // 2
            weave((2 * i, sbuf, peak0), (2 * i + 1, sbuf1, peak1))

            @pl.when(i == 0)
            def _():
                inject_far(1)
                inject(2)
                own(3)
                own_along_y(3)

            @pl.when(i == 1)
            def _():
                inject_far(2)
                inject(3)
                rest(1)

            @pl.when(i == 2)
            def _():
                inject_far(3)

            @pl.when(i == 3)
            def _():
                rest(2)

            @pl.when(i == 5)
            def _():
                rest(3)

            @pl.when(i == 6)
            def _():
                finish_own()

            weave((2 * i + 1, sbuf1, peak1), (2 * i + 2, sbuf, peak0))

            @pl.when(i < HALF - 1)
            def _():
                forward(i + 1)

            return carry

        lax.fori_loop(0, 7, pair, 0)
        weave((jnp.int32(14), sbuf, peak0), (jnp.int32(15), sbuf1, peak1))
        finish_pair()
        weave((jnp.int32(15), sbuf1, peak1), None)

        span = kvbuf.at[:, 0:256, :]

        def sent(kind, condition):
            @pl.when(condition)
            def _():
                await_bytes(span, send_sem.at[kind])

        sent(0, x < 3)
        sent(1, jnp.logical_and(x >= 1, x < 3))
        sent(2, y < 3)
        sent(3, y == 0)
        sent(4, x >= 1)
        sent(5, x >= 1)
        sent(6, jnp.logical_and(x >= 2, y == 3))
        sent(7, jnp.logical_and(x >= 2, y > 0))
        sent(8, chip >= right_fwd)
        sent(9, chip >= left_fwd)
        await_bytes(kvbuf.at[:, 0:128, :], send_sem.at[10])
        await_bytes(qbuf.at[0], send_sem.at[11])
        await_bytes(obuf.at[0], send_sem.at[12])
        await_bytes(obuf.at[0], out_sem.at[0])
        await_many(qd, dout.at[1])
        await_many(dr, dout.at[2])
        await_bytes(cs, dout.at[3])
        await_bytes(obuf.at[0], out_sem.at[1])
        finish_wait()

    @pl.when(role >= PG)
    def _():
        group = role - PG
        pltpu.make_async_copy(raw_q, vq, own_sem.at[0]).wait()
        pltpu.make_async_copy(vkv, vkv, own_sem.at[1]).wait()
        for t in range(4):
            tall[0, 4 * t:4 * t + 4, :] = vq[t].astype(jnp.float32)
            tall[1, 4 * t:4 * t + 4, :] = vkv[t].astype(jnp.float32)
        to = lax.broadcasted_iota(jnp.int32, (32, 16), 0)
        at = lax.broadcasted_iota(jnp.int32, (32, 16), 1)
        ordered = jnp.zeros((32, HD), jnp.float32)
        for h in range(2):
            chosen = jnp.logical_and((to & 7) // 4 == h, at == (to & 3) * 4 + to // 8).astype(jnp.bfloat16)
            ordered = ordered + jnp.dot(
                chosen, tall[0, :, h * HD:(h + 1) * HD].astype(jnp.bfloat16), preferred_element_type=jnp.float32)
        dq[...] = ordered.reshape(PG, 8, HD)
        for p in range(PG):
            remote(dq.at[p], qz.at[group], dout.at[0], din.at[0], line(p)).start()
        pltpu.make_async_copy(w_hbm, wbuf, dlocal.at[0]).wait()
        await_bytes(dz, din.at[3])
        step = lax.broadcasted_iota(jnp.int32, (8, HD), 0) & 3
        to = lax.broadcasted_iota(jnp.int32, (32, 16), 0)
        at = lax.broadcasted_iota(jnp.int32, (32, 16), 1)
        chosen = jnp.logical_and((to & 7) < 4, at == (to & 3) * 4 + to // 8).astype(jnp.bfloat16)
        new_rows = [
            jnp.dot(
                chosen, tall[1, :, i * HD:(i + 1) * HD].astype(jnp.bfloat16), preferred_element_type=jnp.float32
            ).reshape(PG, 8, HD)
            for i in range(2)
        ]
        tiles = []
        for p in range(PG):
            pair = dz[p, 1]
            m = jnp.broadcast_to(pair[:, 0:1], (8, HD))
            part = jnp.broadcast_to(pair[:, 64:65], (8, HD))
            q = dq[p]
            scores = []
            for t in range(4):
                s = jnp.sum(q * new_rows[0][p, t:t + 1, :], axis=1, keepdims=True)
                scores.append(jnp.where(step >= t, jnp.broadcast_to(s, (8, HD)), NEG))
            top = m
            for s in scores:
                top = jnp.maximum(top, s)
            old = jnp.exp2((m - top) * factor)
            total = part * old
            mixed = dz[p, 0] * old
            for t in range(4):
                w = jnp.exp2((scores[t] - top) * factor)
                total = total + w
                mixed = mixed + w * new_rows[1][p, t:t + 1, :]
            tiles.append(mixed / total)
        rows = jnp.concatenate(tiles, axis=0).astype(jnp.bfloat16)
        to = lax.broadcasted_iota(jnp.int32, (16, 32), 0)
        at = lax.broadcasted_iota(jnp.int32, (16, 32), 1)
        halves = []
        for h in range(2):
            chosen = (at == (to // 4) * 8 + h * 4 + to % 4).astype(jnp.bfloat16)
            halves.append(jnp.dot(chosen, rows, preferred_element_type=jnp.float32).astype(jnp.bfloat16))
        attended = jnp.concatenate(halves, axis=1)

        def project(i, carry):
            others = [(seq + 4 * i + d) % 32 for d in range(4)]
            for other in others:
                columns = pl.ds(pl.multiple_of(other * 256, 256), 256)
                rs_s[other] = jnp.dot(
                    attended, wbuf[:, columns], preferred_element_type=jnp.float32).astype(jnp.bfloat16)
            for other in others:
                @pl.when(other != seq)
                def _(other=other):
                    remote(rs_s.at[other], rs_r.at[seq], dout.at[4], din.at[4], plane(other)).start()

            return carry

        lax.fori_loop(0, 8, project, 0)
        rs_r[seq] = rs_s[seq]
        await_bytes(rs_r.at[0:31], din.at[4])

        def add(i, total):
            four = [rs_r[4 * i + d].astype(jnp.float32) for d in range(4)]
            return total + ((four[0] + four[1]) + (four[2] + four[3]))

        summed = lax.fori_loop(0, 8, add, jnp.zeros((16, 256), jnp.float32))
        fz[group] = summed.astype(jnp.bfloat16)
        for d in range(1, 2 * PG):
            remote(fz.at[group], fz.at[group], dout.at[5], din.at[5], line((role + d) % (2 * PG))).start()
        finish_own()
        finish_pair()
        await_bytes(qz, dout.at[0])
        await_bytes(rs_s.at[0:31], dout.at[4])
        await_bytes(fz.at[0:7], dout.at[5])
        for i in range(8):
            pltpu.make_async_copy(zbuf, out_hbm.at[:, i * 1024:(i + 1) * 1024], fill_sem.at[i]).wait()
        finish_wait()


def fused(prompt_lengths, decode_group, queries, kv, dq, fresh, out_weight):
    smem = pl.BlockSpec(memory_space=pltpu.SMEM)
    hbm = pl.BlockSpec(memory_space=pl.ANY)
    return pl.pallas_call(
        fused_kernel,
        out_shape=[
            jax.ShapeDtypeStruct((BLOCK, H * HD), jnp.bfloat16),
            jax.ShapeDtypeStruct((16, 2, 4, PG, PG, 256), jnp.bfloat16),
        ],
        in_specs=[smem, smem, hbm, hbm, hbm, hbm, hbm],
        out_specs=[hbm, hbm],
        scratch_shapes=[
            pltpu.VMEM((2, 32, BLOCK, HD), jnp.bfloat16),
            pltpu.VMEM((HALF, SLOTS * 256, 256), jnp.bfloat16),
            pltpu.VMEM((ROWS, WINDOW), jnp.float32),
            pltpu.VMEM((ROWS, WINDOW), jnp.float32),
            pltpu.VMEM((ROWS, 128), jnp.float32),
            pltpu.VMEM((ROWS, 128), jnp.float32),
            pltpu.VMEM((ROWS, 128), jnp.bfloat16),
            pltpu.VMEM((2, WINDOW, 128), jnp.bfloat16),
            pltpu.VMEM((2, 32, BLOCK, HD), jnp.bfloat16),
            pltpu.VMEM((BLOCK, 1024), jnp.bfloat16),
            pltpu.VMEM((256, 8192), jnp.bfloat16),
            pltpu.VMEM((4, PG, 256), jnp.bfloat16),
            pltpu.VMEM((4, PG, 256), jnp.bfloat16),
            pltpu.VMEM((2, 4 * PG, 256), jnp.float32),
            pltpu.VMEM((PG, 8, HD), jnp.float32),
            pltpu.VMEM((PG, 8, HD), jnp.float32),
            pltpu.VMEM((32, HD), jnp.bfloat16),
            pltpu.VMEM((16, 32, HD), jnp.bfloat16),
            pltpu.VMEM((16, 3, 8, HD), jnp.float32),
            pltpu.VMEM((16, 3, 8, HD), jnp.float32),
            pltpu.VMEM((PG, 2, 8, HD), jnp.float32),
            pltpu.VMEM((PG, 2, 8, HD), jnp.float32),
            pltpu.VMEM((32, 16, 256), jnp.bfloat16),
            pltpu.VMEM((32, 16, 256), jnp.bfloat16),
            pltpu.VMEM((8, 16, 256), jnp.bfloat16),
            pltpu.VMEM((4, PG, PG, 256), jnp.bfloat16),
            pltpu.SemaphoreType.DMA((SLOTS, HALF)),
            pltpu.SemaphoreType.DMA((2, HALF)),
            pltpu.SemaphoreType.DMA((HALF,)),
            pltpu.SemaphoreType.DMA((2,)),
            pltpu.SemaphoreType.DMA((8,)),
            pltpu.SemaphoreType.DMA((13,)),
            pltpu.SemaphoreType.DMA((8,)),
            pltpu.SemaphoreType.DMA((8,)),
            pltpu.SemaphoreType.DMA((2,)),
        ],
        compiler_params=pltpu.CompilerParams(
            collective_id=0, has_side_effects=True, vmem_limit_bytes=62 * 1024 * 1024
        ),
        cost_estimate=pl.CostEstimate(flops=17_000_000_000, bytes_accessed=16_000_000, transcendentals=17_000_000),
    )(prompt_lengths, decode_group, queries, kv, dq, fresh, out_weight)


def on_device(prefill_queries, prefill_kv, prompt_lengths, decode_group, decode_queries, decode_kv, out_weight):
    prefill_out, decode_out = fused(
        prompt_lengths, decode_group, prefill_queries[0], prefill_kv[0], decode_queries[0], decode_kv[0], out_weight
    )
    decode_out = decode_out.reshape(32, 4, PG, PG, 256).transpose(1, 2, 3, 0, 4).reshape(4, PG, PG, -1)
    return prefill_out[None], decode_out


def solution(mesh):
    in_specs = (
        P("role", "seq", None),
        P("role", "seq", None),
        P(),
        P(),
        P("role", None, None, "seq"),
        P("role", None, None, None),
        P("seq", None),
    )
    out_specs = (P("role", "seq", None), P())
    return jax.shard_map(on_device, mesh=mesh, in_specs=in_specs, out_specs=out_specs, check_vma=False)
```

```python
import functools

import jax
import jax.numpy as jnp
from jax import lax
from jax.experimental import pallas as pl
from jax.experimental.pallas import tpu as pltpu
from jax.sharding import PartitionSpec as P

MESH = pl.DeviceIdType.MESH
H = 64
KVH = 8
HD = 128
BLOCK = 128
PG = 4
NEG = -1e30
SCALE = HD**-0.5
LOG2E = 1.4426950408889634
SLOTS = 9
HALF = KVH // 2
GROUP = H // KVH
ROWS = 512
KT = 1024
WINDOW = 2048


def fused_kernel(
    lengths, serves, q_hbm, kv_hbm, raw_q, raw_kv, w_hbm, out_hbm, dec_hbm,
    qbuf, kvbuf, sbuf, sbuf1, peak0, peak1, eye, maskbuf, obuf, zbuf, wbuf, vq, vkv, tall, dq, qz, qb, qd, ds, dr, cs, dz, rs_s, rs_r, fz, fo,
    slot_sem, q_sem, own_sem, out_sem, fill_sem, send_sem, din, dout, dlocal
):
    role = lax.axis_index("role")
    seq = lax.axis_index("seq")
    core = seq % 2
    chip = seq // 2
    y = chip % 4
    x = chip // 4
    home = seq // 16
    prefilling = role < PG
    factor = SCALE * LOG2E

    def plane(other):
        return (role, other)

    def line(other):
        return (other, seq)

    def remote(src, dst, send, recv, device):
        return pltpu.make_async_remote_copy(
            src_ref=src, dst_ref=dst, send_sem=send, recv_sem=recv, device_id=device, device_id_type=MESH)

    def await_bytes(ref, sem):
        pltpu.make_async_copy(ref, ref, sem).wait()

    def q_columns(half, h):
        return q_hbm.at[:, pl.ds(pl.multiple_of((half * 32 + h) * HD, HD), HD)]

    def kv_columns(half, j):
        return kv_hbm.at[:, pl.ds(pl.multiple_of(half * HALF * 256 + j * 256, 256), 256)]

    def chunk(slot, j):
        return kvbuf.at[j, pl.ds(pl.multiple_of((8 - slot) * 256, 256), 256), :]

    def own_rows(j):
        return kvbuf.at[j, pl.ds(pl.multiple_of(2048 + core * 128, 128), 128), :]

    barrier = pltpu.get_barrier_semaphore()

    def greet(d, carry):
        pl.semaphore_signal(barrier, inc=1, device_id=plane((seq + d) % 32), device_id_type=MESH)
        return carry

    lax.fori_loop(1, 32, greet, 0)

    @pl.when(prefilling)
    def _():
        for g in range(PG):
            pl.semaphore_signal(barrier, inc=1, device_id=line(PG + g), device_id_type=MESH)
        for j in range(HALF):
            pltpu.make_async_copy(kv_columns(core, j), own_rows(j), own_sem.at[j]).start()

        def keep_q(h, carry):
            pltpu.make_async_copy(q_columns(core, h), qbuf.at[core, h], q_sem.at[1]).start()
            return carry

        lax.fori_loop(0, 32, keep_q, 0)
        pl.semaphore_wait(barrier, 35)

    @pl.when(role >= PG)
    def _():
        for d in range(1, 2 * PG):
            pl.semaphore_signal(barrier, inc=1, device_id=line((role + d) % (2 * PG)), device_id_type=MESH)
        pltpu.make_async_copy(raw_q, vq, own_sem.at[0]).start()
        kv_part = raw_kv.at[:, :, pl.ds(pl.multiple_of(seq // 4 * 256, 256), 256)]
        pltpu.make_async_copy(kv_part, vkv, own_sem.at[1]).start()
        pltpu.make_async_copy(w_hbm, wbuf, dlocal.at[0]).start()
        zbuf[...] = jnp.zeros_like(zbuf)
        for i in range(8):
            pltpu.make_async_copy(zbuf, out_hbm.at[:, i * 1024:(i + 1) * 1024], fill_sem.at[i]).start()
        pl.semaphore_wait(barrier, 38)

    mine = dec_hbm.at[chip, core]

    sibling = plane(seq + 1 - 2 * core)

    def finish_own():
        await_first = prefilling

        @pl.when(await_first)
        def _():
            await_bytes(fz.at[0:4], din.at[5])

        @pl.when(jnp.logical_not(await_first))
        def _():
            await_bytes(fz.at[0:3], din.at[5])

        to = lax.broadcasted_iota(jnp.int32, (64, 64), 0)
        at = lax.broadcasted_iota(jnp.int32, (64, 64), 1)
        order = (at == ((to // 4) % 4) * 16 + (to % 4) * 4 + to // 16).astype(jnp.bfloat16)
        slab = jnp.dot(order, fz[0:4].reshape(64, 256), preferred_element_type=jnp.float32)
        for i in range(16):
            fo[i // 4, i % 4] = slab[4 * i:4 * i + 4].astype(jnp.bfloat16)
        pltpu.make_async_copy(fo, mine, dlocal.at[1]).start()

        def spread(d, carry):
            other = ((chip + d) % 16) * 2 + core
            remote(fo, mine, dout.at[6], din.at[6], plane(other)).start()
            return carry

        lax.fori_loop(1, 16, spread, 0)

    def finish_pair():
        pltpu.make_async_copy(fo, mine, dlocal.at[1]).wait()
        await_bytes(dec_hbm.at[0:15, 0], din.at[6])
        remote(dec_hbm.at[:, core], dec_hbm.at[:, core], dout.at[7], din.at[7], sibling).start()

    def finish_wait():
        await_bytes(dec_hbm.at[0:15, 0], dout.at[6])
        await_bytes(dec_hbm.at[:, 0], dout.at[7])
        await_bytes(dec_hbm.at[:, 0], din.at[7])

    @pl.when(prefilling)
    def _():
        right, left = (y + 1) % 4, (y + 3) % 4

        def device(xx, yy):
            return plane((xx * 4 + yy) * 2 + core)

        for j in range(HALF):
            remote(kv_columns(1 - core, j), own_rows(j), send_sem.at[10], slot_sem.at[0, j], sibling).start()

        def wait_slot(slot, j):
            @pl.when(chip >= slot)
            def _():
                await_bytes(chunk(slot, j), slot_sem.at[slot, j])

        def send(kind, src, dst, j, xx, yy):
            remote(chunk(src, j), chunk(dst, j), send_sem.at[kind], slot_sem.at[dst, j], device(xx, yy)).start()

        def own_wait(j):
            pltpu.make_async_copy(kv_columns(core, j), own_rows(j), own_sem.at[j]).wait()
            await_bytes(own_rows(j), slot_sem.at[0, j])

        def own(j):
            @pl.when(x < 3)
            def _():
                send(0, 0, 4, j, (x + 1) % 4, y)

        def own_along_y(j):
            @pl.when(y < 3)
            def _():
                send(2, 0, 1, j, x, right)

            @pl.when(y == 0)
            def _():
                send(3, 0, 3, j, x, left)

        right_dst = jnp.where(y < 3, 5, 1)
        left_dst = jnp.where(y > 0, 3, 7)
        right_fwd = jnp.where(y < 3, 1, 5)
        left_fwd = jnp.where(y > 0, 7, 3)

        def inject(j):
            wait_slot(4, j)

            @pl.when(x >= 1)
            def _():
                send(4, 4, right_dst, j, x, right)
                send(5, 4, left_dst, j, x, left)

            @pl.when(jnp.logical_and(x >= 1, x < 3))
            def _():
                send(1, 4, 8, j, (x + 1) % 4, y)

        def inject_far(j):
            wait_slot(8, j)

            @pl.when(jnp.logical_and(x >= 2, y == 3))
            def _():
                send(6, 8, 5, j, x, right)

            @pl.when(jnp.logical_and(x >= 2, y > 0))
            def _():
                send(7, 8, 7, j, x, left)

        def forward(j):
            wait_slot(right_fwd, j)

            @pl.when(chip >= right_fwd)
            def _():
                send(8, right_fwd, 2, j, x, right)

            wait_slot(left_fwd, j)

            @pl.when(chip >= left_fwd)
            def _():
                send(9, left_fwd, 6, j, x, left)

        def rest(j):
            wait_slot(6 - right_fwd, j)
            wait_slot(10 - left_fwd, j)
            wait_slot(2, j)
            wait_slot(6, j)

        counts = [lengths[role, i] for i in range(4)]
        served = [serves[role, i] for i in range(4)]
        blocks = [(n + 127) // 128 for n in counts]
        starts = [0, blocks[0], blocks[0] + blocks[1], blocks[0] + blocks[1] + blocks[2]]

        def pick(block, values):
            chosen = values[0]
            for i in range(1, 4):
                chosen = jnp.where(block >= starts[i], values[i], chosen)
            return chosen

        firsts, lives = [], []
        for e in range(2):
            block = 2 * chip + e
            first = pick(block, starts)
            firsts.append(first - (2 * chip - 15 + e))
            lives.append(pick(block, counts) - (block - first) * 128)

        at_home = home == core

        def spread_queries():
            await_bytes(qz, din.at[0])
            qb[...] = qz[...].reshape(32, HD).astype(jnp.bfloat16)

            @pl.when(at_home)
            def _():
                qd[seq % 16] = qb[...]

            def one(d, carry):
                other = ((chip + d) % 16) * 2 + home

                @pl.when(other != seq)
                def _():
                    remote(qb, qd.at[seq % 16], dout.at[1], din.at[1], plane(other)).start()

                return carry

            lax.fori_loop(0, 16, one, 0)

        def await_many(buffer, sem):
            @pl.when(at_home)
            def _():
                await_bytes(buffer.at[0:15], sem)

            @pl.when(jnp.logical_not(at_home))
            def _():
                await_bytes(buffer, sem)

        lanes = lax.broadcasted_iota(jnp.int32, (32, HD), 1)

        def partial_terms():
            await_many(qd, din.at[1])
            stats = []
            for e in range(2):
                group = pick(2 * chip + e, served)
                live = lives[e]

                for j in range(HALF):
                    q = jnp.zeros((4, 8, HD), jnp.float32)
                    wide = qd[4 * j:4 * j + 4].astype(jnp.float32).reshape(4, PG, 8, HD)
                    for g in range(PG):
                        q = jnp.where(group == g, wide[:, g], q)
                    q = q.reshape(32, HD).astype(jnp.bfloat16)
                    keys = kvbuf[j, 2048 + 128 * e:2176 + 128 * e, 0:HD]
                    values = kvbuf[j, 2048 + 128 * e:2176 + 128 * e, HD:2 * HD]
                    s = lax.dot_general(q, keys, (((1,), (1,)), ((), ())), preferred_element_type=jnp.float32)
                    s = jnp.where(lanes < live, s, NEG)
                    m = jnp.max(s, axis=1, keepdims=True)
                    w = jnp.exp2((s - m) * factor)
                    total = jnp.sum(w, axis=1, keepdims=True)
                    o = jnp.dot(w.astype(jnp.bfloat16), values, preferred_element_type=jnp.float32)
                    ds[4 * j:4 * j + 4, e] = o.reshape(4, 8, HD)
                    stat = jnp.where(lanes < 64, m, total)
                    if e == 0:
                        stats.append(stat)
                    else:
                        stat = jnp.where(lanes % 64 < 32, stats[j], stat)
                        ds[4 * j:4 * j + 4, 2] = stat.reshape(4, 8, HD)

            @pl.when(at_home)
            def _():
                dr[chip] = ds[seq % 16]

            def out(d, carry):
                other = 16 * core + (chip + d) % 16

                @pl.when(other != seq)
                def _():
                    remote(ds.at[(chip + d) % 16], dr.at[chip], dout.at[2], din.at[2], plane(other)).start()

                return carry

            lax.fori_loop(0, 16, out, 0)

        which = lax.broadcasted_iota(jnp.int32, (PG, 8, HD), 0)

        def combine_terms():
            await_many(dr, din.at[2])

            terms = []
            top = jnp.full((PG, 8, HD), NEG, jnp.float32)
            for b in range(32):
                flag = which == pick(jnp.int32(b), served)
                m = jnp.broadcast_to(dr[b // 2, 2][:, 32 * (b % 2):32 * (b % 2) + 1], (8, HD))[None]
                top = jnp.maximum(top, jnp.where(flag, m, NEG))
                terms.append((flag, m))
            total = jnp.zeros((PG, 8, HD), jnp.float32)
            mixed = jnp.zeros((PG, 8, HD), jnp.float32)
            for b in range(32):
                flag, m = terms[b]
                part = jnp.broadcast_to(dr[b // 2, 2][:, 64 + 32 * (b % 2):65 + 32 * (b % 2)], (8, HD))[None]
                add = jnp.where(flag, jnp.exp2((jnp.minimum(m, top) - top) * factor), 0.0)
                total = total + add * part
                mixed = mixed + add * dr[b // 2, b % 2][None]
            lane3 = lax.broadcasted_iota(jnp.int32, (PG, 8, HD), 2)
            cs[:, 0] = mixed
            cs[:, 1] = jnp.where(lane3 < 64, top, total)
            for g in range(PG):
                remote(cs.at[g], dz.at[role], dout.at[3], din.at[3], line(PG + g)).start()

        own_wait(0)
        own(0)

        own_along_y(0)

        for slot in range(1, SLOTS):
            @pl.when(chip < slot)
            def _(slot=slot):
                for j in range(HALF):
                    kvbuf[j, (8 - slot) * 256:(9 - slot) * 256, :] = jnp.zeros((256, 256), jnp.bfloat16)

        at = lax.broadcasted_iota(jnp.int32, (128, 128), 0)
        to = lax.broadcasted_iota(jnp.int32, (128, 128), 1)
        for i in range(ROWS // 128):
            eye[i * 128:(i + 1) * 128, :] = (at == to).astype(jnp.bfloat16)
        for e in range(2):
            for w in range(15):
                level = jnp.where(firsts[e] <= w, 0.0, NEG)
                maskbuf[e, w * 128:(w + 1) * 128, :] = jnp.full((128, 128), level, jnp.float32).astype(jnp.bfloat16)
            maskbuf[e, 1920:2048, :] = jnp.where(at <= to, 0.0, NEG).astype(jnp.bfloat16)

        spread_queries()

        def start_q(h, carry):
            remote(q_columns(1 - core, h), qbuf.at[core, h], send_sem.at[11], q_sem.at[0], sibling).start()
            return carry

        lax.fori_loop(0, 32, start_q, 0)
        inject(0)
        for j in range(1, HALF):
            own_wait(j)
        own(1)
        own_along_y(1)
        partial_terms()
        inject_far(0)
        forward(0)
        inject(1)
        own(2)
        own_along_y(2)
        combine_terms()
        rest(0)

        await_bytes(qbuf.at[0], q_sem.at[0])
        await_bytes(qbuf.at[0], q_sem.at[1])

        row_in = lax.broadcasted_iota(jnp.int32, (ROWS, 128), 0) & 127
        ones = jnp.ones((KT, HD), jnp.bfloat16)

        def place(n):
            j, u = n // 4, n % 4
            return j, u // 2, j * GROUP + (u % 2) * 4

        def key_rows(j, e, kt):
            return j, pl.ds(pl.multiple_of(128 + e * 128 + kt * KT, 128), KT)

        def weave(current, following):
            if following is not None:
                n, scores, peaks = following
                j, e, base = place(n)
                q = jnp.concatenate([qbuf[e, pl.ds(base, 4)].reshape(ROWS, HD), eye[...]], axis=1)
                peak = None
            if current is not None:
                cn, cscores, cpeaks = current
                cj, ce, cbase = place(cn)
                total = None
            for kt in range(WINDOW // KT):
                if following is not None:
                    rows = key_rows(j, e, kt)
                    masked_keys = jnp.concatenate(
                        [kvbuf[rows[0], rows[1], 0:HD], maskbuf[e, kt * KT:(kt + 1) * KT, :]], axis=1)
                    s = lax.dot_general(
                        q, masked_keys, (((1,), (1,)), ((), ())), preferred_element_type=jnp.float32)
                if current is not None:
                    weights = [
                        jnp.exp2((cscores[:, kt * KT + i * 128:kt * KT + (i + 1) * 128] - cpeaks[...]) * factor)
                        for i in range(KT // 128)
                    ]
                    rows = key_rows(cj, ce, kt)
                    product = jnp.dot(
                        jnp.concatenate(weights, axis=1).astype(jnp.bfloat16),
                        jnp.concatenate([kvbuf[rows[0], rows[1], HD:2 * HD], ones], axis=1),
                        preferred_element_type=jnp.float32)
                    total = product if total is None else total + product
                if following is not None:
                    pieces = [s[:, i * 128:(i + 1) * 128] for i in range(KT // 128)]
                    for i, piece in enumerate(pieces):
                        scores[:, kt * KT + i * 128:kt * KT + (i + 1) * 128] = piece
                    while len(pieces) > 1:
                        pieces = [jnp.maximum(a, b) for a, b in zip(pieces[::2], pieces[1::2])]
                    peak = pieces[0] if peak is None else jnp.maximum(peak, pieces[0])
            if following is not None:
                peaks[...] = jnp.broadcast_to(jnp.max(peak, axis=1, keepdims=True), (ROWS, 128))
            if current is not None:
                live = jnp.where(ce == 0, lives[0], lives[1])
                mixed = total[:, :HD] / total[:, HD:]
                mixed = jnp.where(row_in < live, mixed, 0.0).astype(jnp.bfloat16)
                obuf[ce, pl.ds(cbase, 4)] = mixed.reshape(4, BLOCK, HD)
                for i in range(4):
                    columns = out_hbm.at[:, pl.ds(pl.multiple_of((core * 32 + cbase + i) * HD, HD), HD)]

                    @pl.when(ce == core)
                    def _(i=i, columns=columns):
                        pltpu.make_async_copy(obuf.at[ce, cbase + i], columns, out_sem.at[0]).start()

                    @pl.when(ce != core)
                    def _(i=i, columns=columns):
                        remote(obuf.at[ce, cbase + i], columns, send_sem.at[12], out_sem.at[1], sibling).start()

        weave(None, (jnp.int32(0), sbuf, peak0))

        def pair(i, carry):
            j = i // 2
            weave((2 * i, sbuf, peak0), (2 * i + 1, sbuf1, peak1))

            @pl.when(i == 0)
            def _():
                inject_far(1)
                inject(2)
                own(3)
                own_along_y(3)

            @pl.when(i == 1)
            def _():
                inject_far(2)
                inject(3)
                rest(1)

            @pl.when(i == 2)
            def _():
                inject_far(3)

            @pl.when(i == 3)
            def _():
                rest(2)

            @pl.when(i == 5)
            def _():
                rest(3)

            @pl.when(i == 4)
            def _():
                finish_own()

            @pl.when(i == 6)
            def _():
                finish_pair()

            weave((2 * i + 1, sbuf1, peak1), (2 * i + 2, sbuf, peak0))

            @pl.when(i < HALF - 1)
            def _():
                forward(i + 1)

            return carry

        lax.fori_loop(0, 7, pair, 0)
        weave((jnp.int32(14), sbuf, peak0), (jnp.int32(15), sbuf1, peak1))
        weave((jnp.int32(15), sbuf1, peak1), None)

        span = kvbuf.at[:, 0:256, :]

        def sent(kind, condition):
            @pl.when(condition)
            def _():
                await_bytes(span, send_sem.at[kind])

        sent(0, x < 3)
        sent(1, jnp.logical_and(x >= 1, x < 3))
        sent(2, y < 3)
        sent(3, y == 0)
        sent(4, x >= 1)
        sent(5, x >= 1)
        sent(6, jnp.logical_and(x >= 2, y == 3))
        sent(7, jnp.logical_and(x >= 2, y > 0))
        sent(8, chip >= right_fwd)
        sent(9, chip >= left_fwd)
        await_bytes(kvbuf.at[:, 0:128, :], send_sem.at[10])
        await_bytes(qbuf.at[0], send_sem.at[11])
        await_bytes(obuf.at[0], send_sem.at[12])
        await_bytes(obuf.at[0], out_sem.at[0])
        await_many(qd, dout.at[1])
        await_many(dr, dout.at[2])
        await_bytes(cs, dout.at[3])
        await_bytes(obuf.at[0], out_sem.at[1])
        finish_wait()

    @pl.when(role >= PG)
    def _():
        group = role - PG
        pltpu.make_async_copy(raw_q, vq, own_sem.at[0]).wait()
        pltpu.make_async_copy(vkv, vkv, own_sem.at[1]).wait()
        for t in range(4):
            tall[0, 4 * t:4 * t + 4, :] = vq[t].astype(jnp.float32)
            tall[1, 4 * t:4 * t + 4, :] = vkv[t].astype(jnp.float32)
        to = lax.broadcasted_iota(jnp.int32, (32, 16), 0)
        at = lax.broadcasted_iota(jnp.int32, (32, 16), 1)
        ordered = jnp.zeros((32, HD), jnp.float32)
        for h in range(2):
            chosen = jnp.logical_and((to & 7) // 4 == h, at == (to & 3) * 4 + to // 8).astype(jnp.bfloat16)
            ordered = ordered + jnp.dot(
                chosen, tall[0, :, h * HD:(h + 1) * HD].astype(jnp.bfloat16), preferred_element_type=jnp.float32)
        dq[...] = ordered.reshape(PG, 8, HD)
        for p in range(PG):
            remote(dq.at[p], qz.at[group], dout.at[0], din.at[0], line(p)).start()
        pltpu.make_async_copy(w_hbm, wbuf, dlocal.at[0]).wait()
        await_bytes(dz, din.at[3])
        step = lax.broadcasted_iota(jnp.int32, (8, HD), 0) & 3
        to = lax.broadcasted_iota(jnp.int32, (32, 16), 0)
        at = lax.broadcasted_iota(jnp.int32, (32, 16), 1)
        chosen = jnp.logical_and((to & 7) < 4, at == (to & 3) * 4 + to // 8).astype(jnp.bfloat16)
        new_rows = [
            jnp.dot(
                chosen, tall[1, :, i * HD:(i + 1) * HD].astype(jnp.bfloat16), preferred_element_type=jnp.float32
            ).reshape(PG, 8, HD)
            for i in range(2)
        ]
        tiles = []
        for p in range(PG):
            pair = dz[p, 1]
            m = jnp.broadcast_to(pair[:, 0:1], (8, HD))
            part = jnp.broadcast_to(pair[:, 64:65], (8, HD))
            q = dq[p]
            scores = []
            for t in range(4):
                s = jnp.sum(q * new_rows[0][p, t:t + 1, :], axis=1, keepdims=True)
                scores.append(jnp.where(step >= t, jnp.broadcast_to(s, (8, HD)), NEG))
            top = m
            for s in scores:
                top = jnp.maximum(top, s)
            old = jnp.exp2((m - top) * factor)
            total = part * old
            mixed = dz[p, 0] * old
            for t in range(4):
                w = jnp.exp2((scores[t] - top) * factor)
                total = total + w
                mixed = mixed + w * new_rows[1][p, t:t + 1, :]
            tiles.append(mixed / total)
        rows = jnp.concatenate(tiles, axis=0).astype(jnp.bfloat16)
        to = lax.broadcasted_iota(jnp.int32, (16, 32), 0)
        at = lax.broadcasted_iota(jnp.int32, (16, 32), 1)
        halves = []
        for h in range(2):
            chosen = (at == (to // 4) * 8 + h * 4 + to % 4).astype(jnp.bfloat16)
            halves.append(jnp.dot(chosen, rows, preferred_element_type=jnp.float32).astype(jnp.bfloat16))
        attended = jnp.concatenate(halves, axis=1)

        def project(i, carry):
            others = [(seq + 4 * i + d) % 32 for d in range(4)]
            for other in others:
                columns = pl.ds(pl.multiple_of(other * 256, 256), 256)
                rs_s[other] = jnp.dot(
                    attended, wbuf[:, columns], preferred_element_type=jnp.float32).astype(jnp.bfloat16)
            for other in others:
                @pl.when(other != seq)
                def _(other=other):
                    remote(rs_s.at[other], rs_r.at[seq], dout.at[4], din.at[4], plane(other)).start()

            return carry

        lax.fori_loop(0, 8, project, 0)
        rs_r[seq] = rs_s[seq]
        await_bytes(rs_r.at[0:31], din.at[4])

        def add(i, total):
            four = [rs_r[4 * i + d].astype(jnp.float32) for d in range(4)]
            return total + ((four[0] + four[1]) + (four[2] + four[3]))

        summed = lax.fori_loop(0, 8, add, jnp.zeros((16, 256), jnp.float32))
        fz[group] = summed.astype(jnp.bfloat16)
        for d in range(1, 2 * PG):
            remote(fz.at[group], fz.at[group], dout.at[5], din.at[5], line((role + d) % (2 * PG))).start()
        finish_own()
        finish_pair()
        await_bytes(qz, dout.at[0])
        await_bytes(rs_s.at[0:31], dout.at[4])
        await_bytes(fz.at[0:7], dout.at[5])
        for i in range(8):
            pltpu.make_async_copy(zbuf, out_hbm.at[:, i * 1024:(i + 1) * 1024], fill_sem.at[i]).wait()
        finish_wait()


def fused(prompt_lengths, decode_group, queries, kv, dq, fresh, out_weight):
    smem = pl.BlockSpec(memory_space=pltpu.SMEM)
    hbm = pl.BlockSpec(memory_space=pl.ANY)
    return pl.pallas_call(
        fused_kernel,
        out_shape=[
            jax.ShapeDtypeStruct((BLOCK, H * HD), jnp.bfloat16),
            jax.ShapeDtypeStruct((16, 2, 4, PG, PG, 256), jnp.bfloat16),
        ],
        in_specs=[smem, smem, hbm, hbm, hbm, hbm, hbm],
        out_specs=[hbm, hbm],
        scratch_shapes=[
            pltpu.VMEM((2, 32, BLOCK, HD), jnp.bfloat16),
            pltpu.VMEM((HALF, SLOTS * 256, 256), jnp.bfloat16),
            pltpu.VMEM((ROWS, WINDOW), jnp.float32),
            pltpu.VMEM((ROWS, WINDOW), jnp.float32),
            pltpu.VMEM((ROWS, 128), jnp.float32),
            pltpu.VMEM((ROWS, 128), jnp.float32),
            pltpu.VMEM((ROWS, 128), jnp.bfloat16),
            pltpu.VMEM((2, WINDOW, 128), jnp.bfloat16),
            pltpu.VMEM((2, 32, BLOCK, HD), jnp.bfloat16),
            pltpu.VMEM((BLOCK, 1024), jnp.bfloat16),
            pltpu.VMEM((256, 8192), jnp.bfloat16),
            pltpu.VMEM((4, PG, 256), jnp.bfloat16),
            pltpu.VMEM((4, PG, 256), jnp.bfloat16),
            pltpu.VMEM((2, 4 * PG, 256), jnp.float32),
            pltpu.VMEM((PG, 8, HD), jnp.float32),
            pltpu.VMEM((PG, 8, HD), jnp.float32),
            pltpu.VMEM((32, HD), jnp.bfloat16),
            pltpu.VMEM((16, 32, HD), jnp.bfloat16),
            pltpu.VMEM((16, 3, 8, HD), jnp.float32),
            pltpu.VMEM((16, 3, 8, HD), jnp.float32),
            pltpu.VMEM((PG, 2, 8, HD), jnp.float32),
            pltpu.VMEM((PG, 2, 8, HD), jnp.float32),
            pltpu.VMEM((32, 16, 256), jnp.bfloat16),
            pltpu.VMEM((32, 16, 256), jnp.bfloat16),
            pltpu.VMEM((8, 16, 256), jnp.bfloat16),
            pltpu.VMEM((4, PG, PG, 256), jnp.bfloat16),
            pltpu.SemaphoreType.DMA((SLOTS, HALF)),
            pltpu.SemaphoreType.DMA((2,)),
            pltpu.SemaphoreType.DMA((HALF,)),
            pltpu.SemaphoreType.DMA((2,)),
            pltpu.SemaphoreType.DMA((8,)),
            pltpu.SemaphoreType.DMA((13,)),
            pltpu.SemaphoreType.DMA((8,)),
            pltpu.SemaphoreType.DMA((8,)),
            pltpu.SemaphoreType.DMA((2,)),
        ],
        compiler_params=pltpu.CompilerParams(
            collective_id=0, has_side_effects=True, vmem_limit_bytes=62 * 1024 * 1024
        ),
        cost_estimate=pl.CostEstimate(flops=17_000_000_000, bytes_accessed=16_000_000, transcendentals=17_000_000),
    )(prompt_lengths, decode_group, queries, kv, dq, fresh, out_weight)


def on_device(prefill_queries, prefill_kv, prompt_lengths, decode_group, decode_queries, decode_kv, out_weight):
    prefill_out, decode_out = fused(
        prompt_lengths, decode_group, prefill_queries[0], prefill_kv[0], decode_queries[0], decode_kv[0], out_weight
    )
    decode_out = decode_out.reshape(32, 4, PG, PG, 256).transpose(1, 2, 3, 0, 4).reshape(4, PG, PG, -1)
    return prefill_out[None], decode_out


def solution(mesh):
    in_specs = (
        P("role", "seq", None),
        P("role", "seq", None),
        P(),
        P(),
        P("role", None, None, "seq"),
        P("role", None, None, None),
        P("seq", None),
    )
    out_specs = (P("role", "seq", None), P())
    return jax.shard_map(on_device, mesh=mesh, in_specs=in_specs, out_specs=out_specs, check_vma=False)
```

```python
import functools

import jax
import jax.numpy as jnp
from jax import lax
from jax.experimental import pallas as pl
from jax.experimental.pallas import tpu as pltpu
from jax.sharding import PartitionSpec as P

MESH = pl.DeviceIdType.MESH
H = 64
KVH = 8
HD = 128
BLOCK = 128
PG = 4
NEG = -1e30
SCALE = HD**-0.5
LOG2E = 1.4426950408889634
SLOTS = 9
HALF = KVH // 2
GROUP = H // KVH
ROWS = 512
KT = 1024
WINDOW = 2048


def fused_kernel(
    lengths, serves, q_hbm, kv_hbm, raw_q, raw_kv, w_hbm, out_hbm, dec_hbm,
    qbuf, kvbuf, sbuf, sbuf1, peak0, peak1, obuf, zbuf, wbuf, vq, vkv, tall, dq, qz, qb, qd, ds, dr, cs, dz, rs_s, rs_r, fz, fo,
    slot_sem, q_sem, own_sem, out_sem, fill_sem, send_sem, din, dout, dlocal
):
    role = lax.axis_index("role")
    seq = lax.axis_index("seq")
    core = seq % 2
    chip = seq // 2
    y = chip % 4
    x = chip // 4
    home = seq // 16
    prefilling = role < PG
    factor = SCALE * LOG2E

    def plane(other):
        return (role, other)

    def line(other):
        return (other, seq)

    def remote(src, dst, send, recv, device):
        return pltpu.make_async_remote_copy(
            src_ref=src, dst_ref=dst, send_sem=send, recv_sem=recv, device_id=device, device_id_type=MESH)

    def await_bytes(ref, sem):
        pltpu.make_async_copy(ref, ref, sem).wait()

    def q_columns(half, h):
        return q_hbm.at[:, pl.ds(pl.multiple_of((half * 32 + h) * HD, HD), HD)]

    def kv_columns(half, j):
        return kv_hbm.at[:, pl.ds(pl.multiple_of(half * HALF * 256 + j * 256, 256), 256)]

    def chunk(slot, j):
        return kvbuf.at[j, pl.ds(pl.multiple_of((8 - slot) * 256, 256), 256), :]

    def own_rows(j):
        return kvbuf.at[j, pl.ds(pl.multiple_of(2048 + core * 128, 128), 128), :]

    barrier = pltpu.get_barrier_semaphore()

    def greet(d, carry):
        pl.semaphore_signal(barrier, inc=1, device_id=plane((seq + d) % 32), device_id_type=MESH)
        return carry

    lax.fori_loop(1, 32, greet, 0)

    @pl.when(prefilling)
    def _():
        for g in range(PG):
            pl.semaphore_signal(barrier, inc=1, device_id=line(PG + g), device_id_type=MESH)
        for j in range(HALF):
            pltpu.make_async_copy(kv_columns(core, j), own_rows(j), own_sem.at[j]).start()

        def keep_q(h, carry):
            pltpu.make_async_copy(q_columns(core, h), qbuf.at[core, h], q_sem.at[1]).start()
            return carry

        lax.fori_loop(0, 32, keep_q, 0)
        pl.semaphore_wait(barrier, 35)

    @pl.when(role >= PG)
    def _():
        for d in range(1, 2 * PG):
            pl.semaphore_signal(barrier, inc=1, device_id=line((role + d) % (2 * PG)), device_id_type=MESH)
        pltpu.make_async_copy(raw_q, vq, own_sem.at[0]).start()
        kv_part = raw_kv.at[:, :, pl.ds(pl.multiple_of(seq // 4 * 256, 256), 256)]
        pltpu.make_async_copy(kv_part, vkv, own_sem.at[1]).start()
        pltpu.make_async_copy(w_hbm, wbuf, dlocal.at[0]).start()
        zbuf[...] = jnp.zeros_like(zbuf)
        for i in range(8):
            pltpu.make_async_copy(zbuf, out_hbm.at[:, i * 1024:(i + 1) * 1024], fill_sem.at[i]).start()
        pl.semaphore_wait(barrier, 38)

    mine = dec_hbm.at[chip, core]

    sibling = plane(seq + 1 - 2 * core)

    def finish_own():
        await_first = prefilling

        @pl.when(await_first)
        def _():
            await_bytes(fz.at[0:4], din.at[5])

        @pl.when(jnp.logical_not(await_first))
        def _():
            await_bytes(fz.at[0:3], din.at[5])

        to = lax.broadcasted_iota(jnp.int32, (64, 64), 0)
        at = lax.broadcasted_iota(jnp.int32, (64, 64), 1)
        order = (at == ((to // 4) % 4) * 16 + (to % 4) * 4 + to // 16).astype(jnp.bfloat16)
        slab = jnp.dot(order, fz[0:4].reshape(64, 256), preferred_element_type=jnp.float32)
        for i in range(16):
            fo[i // 4, i % 4] = slab[4 * i:4 * i + 4].astype(jnp.bfloat16)
        pltpu.make_async_copy(fo, mine, dlocal.at[1]).start()

        def spread(d, carry):
            other = ((chip + d) % 16) * 2 + core
            remote(fo, mine, dout.at[6], din.at[6], plane(other)).start()
            return carry

        lax.fori_loop(1, 16, spread, 0)

    def finish_pair():
        pltpu.make_async_copy(fo, mine, dlocal.at[1]).wait()
        await_bytes(dec_hbm.at[0:15, 0], din.at[6])
        remote(dec_hbm.at[:, core], dec_hbm.at[:, core], dout.at[7], din.at[7], sibling).start()

    def finish_wait():
        await_bytes(dec_hbm.at[0:15, 0], dout.at[6])
        await_bytes(dec_hbm.at[:, 0], dout.at[7])
        await_bytes(dec_hbm.at[:, 0], din.at[7])

    @pl.when(prefilling)
    def _():
        right, left = (y + 1) % 4, (y + 3) % 4

        def device(xx, yy):
            return plane((xx * 4 + yy) * 2 + core)

        for j in range(HALF):
            remote(kv_columns(1 - core, j), own_rows(j), send_sem.at[10], slot_sem.at[0, j], sibling).start()

        def wait_slot(slot, j):
            @pl.when(chip >= slot)
            def _():
                await_bytes(chunk(slot, j), slot_sem.at[slot, j])

        def send(kind, src, dst, j, xx, yy):
            remote(chunk(src, j), chunk(dst, j), send_sem.at[kind], slot_sem.at[dst, j], device(xx, yy)).start()

        def own_wait(j):
            pltpu.make_async_copy(kv_columns(core, j), own_rows(j), own_sem.at[j]).wait()
            await_bytes(own_rows(j), slot_sem.at[0, j])

        def own(j):
            @pl.when(x < 3)
            def _():
                send(0, 0, 4, j, (x + 1) % 4, y)

        def own_along_y(j):
            @pl.when(y < 3)
            def _():
                send(2, 0, 1, j, x, right)

            @pl.when(y == 0)
            def _():
                send(3, 0, 3, j, x, left)

        right_dst = jnp.where(y < 3, 5, 1)
        left_dst = jnp.where(y > 0, 3, 7)
        right_fwd = jnp.where(y < 3, 1, 5)
        left_fwd = jnp.where(y > 0, 7, 3)

        def inject(j):
            wait_slot(4, j)

            @pl.when(x >= 1)
            def _():
                send(4, 4, right_dst, j, x, right)
                send(5, 4, left_dst, j, x, left)

            @pl.when(jnp.logical_and(x >= 1, x < 3))
            def _():
                send(1, 4, 8, j, (x + 1) % 4, y)

        def inject_far(j):
            wait_slot(8, j)

            @pl.when(jnp.logical_and(x >= 2, y == 3))
            def _():
                send(6, 8, 5, j, x, right)

            @pl.when(jnp.logical_and(x >= 2, y > 0))
            def _():
                send(7, 8, 7, j, x, left)

        def forward(j):
            wait_slot(right_fwd, j)

            @pl.when(chip >= right_fwd)
            def _():
                send(8, right_fwd, 2, j, x, right)

            wait_slot(left_fwd, j)

            @pl.when(chip >= left_fwd)
            def _():
                send(9, left_fwd, 6, j, x, left)

        def rest(j):
            wait_slot(6 - right_fwd, j)
            wait_slot(10 - left_fwd, j)
            wait_slot(2, j)
            wait_slot(6, j)

        counts = [lengths[role, i] for i in range(4)]
        served = [serves[role, i] for i in range(4)]
        blocks = [(n + 127) // 128 for n in counts]
        starts = [0, blocks[0], blocks[0] + blocks[1], blocks[0] + blocks[1] + blocks[2]]

        def pick(block, values):
            chosen = values[0]
            for i in range(1, 4):
                chosen = jnp.where(block >= starts[i], values[i], chosen)
            return chosen

        firsts, lives = [], []
        for e in range(2):
            block = 2 * chip + e
            first = pick(block, starts)
            firsts.append(first - (2 * chip - 15 + e))
            lives.append(pick(block, counts) - (block - first) * 128)

        at_home = home == core

        def spread_queries():
            await_bytes(qz, din.at[0])
            qb[...] = qz[...].reshape(32, HD).astype(jnp.bfloat16)

            @pl.when(at_home)
            def _():
                qd[seq % 16] = qb[...]

            def one(d, carry):
                other = ((chip + d) % 16) * 2 + home

                @pl.when(other != seq)
                def _():
                    remote(qb, qd.at[seq % 16], dout.at[1], din.at[1], plane(other)).start()

                return carry

            lax.fori_loop(0, 16, one, 0)

        def await_many(buffer, sem):
            @pl.when(at_home)
            def _():
                await_bytes(buffer.at[0:15], sem)

            @pl.when(jnp.logical_not(at_home))
            def _():
                await_bytes(buffer, sem)

        lanes = lax.broadcasted_iota(jnp.int32, (32, HD), 1)

        def partial_terms():
            await_many(qd, din.at[1])
            stats = []
            for e in range(2):
                group = pick(2 * chip + e, served)
                live = lives[e]

                for j in range(HALF):
                    q = jnp.zeros((4, 8, HD), jnp.float32)
                    wide = qd[4 * j:4 * j + 4].astype(jnp.float32).reshape(4, PG, 8, HD)
                    for g in range(PG):
                        q = jnp.where(group == g, wide[:, g], q)
                    q = q.reshape(32, HD).astype(jnp.bfloat16)
                    keys = kvbuf[j, 2048 + 128 * e:2176 + 128 * e, 0:HD]
                    values = kvbuf[j, 2048 + 128 * e:2176 + 128 * e, HD:2 * HD]
                    s = lax.dot_general(q, keys, (((1,), (1,)), ((), ())), preferred_element_type=jnp.float32)
                    s = jnp.where(lanes < live, s, NEG)
                    m = jnp.max(s, axis=1, keepdims=True)
                    w = jnp.exp2((s - m) * factor)
                    total = jnp.sum(w, axis=1, keepdims=True)
                    o = jnp.dot(w.astype(jnp.bfloat16), values, preferred_element_type=jnp.float32)
                    ds[4 * j:4 * j + 4, e] = o.reshape(4, 8, HD)
                    stat = jnp.where(lanes < 64, m, total)
                    if e == 0:
                        stats.append(stat)
                    else:
                        stat = jnp.where(lanes % 64 < 32, stats[j], stat)
                        ds[4 * j:4 * j + 4, 2] = stat.reshape(4, 8, HD)

            @pl.when(at_home)
            def _():
                dr[chip] = ds[seq % 16]

            def out(d, carry):
                other = 16 * core + (chip + d) % 16

                @pl.when(other != seq)
                def _():
                    remote(ds.at[(chip + d) % 16], dr.at[chip], dout.at[2], din.at[2], plane(other)).start()

                return carry

            lax.fori_loop(0, 16, out, 0)

        which = lax.broadcasted_iota(jnp.int32, (PG, 8, HD), 0)

        def combine_terms():
            await_many(dr, din.at[2])

            terms = []
            top = jnp.full((PG, 8, HD), NEG, jnp.float32)
            for b in range(32):
                flag = which == pick(jnp.int32(b), served)
                m = jnp.broadcast_to(dr[b // 2, 2][:, 32 * (b % 2):32 * (b % 2) + 1], (8, HD))[None]
                top = jnp.maximum(top, jnp.where(flag, m, NEG))
                terms.append((flag, m))
            total = jnp.zeros((PG, 8, HD), jnp.float32)
            mixed = jnp.zeros((PG, 8, HD), jnp.float32)
            for b in range(32):
                flag, m = terms[b]
                part = jnp.broadcast_to(dr[b // 2, 2][:, 64 + 32 * (b % 2):65 + 32 * (b % 2)], (8, HD))[None]
                add = jnp.where(flag, jnp.exp2((jnp.minimum(m, top) - top) * factor), 0.0)
                total = total + add * part
                mixed = mixed + add * dr[b // 2, b % 2][None]
            lane3 = lax.broadcasted_iota(jnp.int32, (PG, 8, HD), 2)
            cs[:, 0] = mixed
            cs[:, 1] = jnp.where(lane3 < 64, top, total)
            for g in range(PG):
                remote(cs.at[g], dz.at[role], dout.at[3], din.at[3], line(PG + g)).start()

        own_wait(0)
        own(0)

        own_along_y(0)

        for slot in range(1, SLOTS):
            @pl.when(chip < slot)
            def _(slot=slot):
                for j in range(HALF):
                    kvbuf[j, (8 - slot) * 256:(9 - slot) * 256, :] = jnp.zeros((256, 256), jnp.bfloat16)

        spread_queries()

        def start_q(h, carry):
            remote(q_columns(1 - core, h), qbuf.at[core, h], send_sem.at[11], q_sem.at[0], sibling).start()
            return carry

        lax.fori_loop(0, 32, start_q, 0)
        inject(0)
        for j in range(1, HALF):
            own_wait(j)
        own(1)
        own_along_y(1)
        partial_terms()
        inject_far(0)
        forward(0)
        inject(1)
        own(2)
        own_along_y(2)
        combine_terms()
        rest(0)

        await_bytes(qbuf.at[0], q_sem.at[0])
        await_bytes(qbuf.at[0], q_sem.at[1])

        row_in = lax.broadcasted_iota(jnp.int32, (ROWS, 128), 0) & 127
        lane = lax.broadcasted_iota(jnp.int32, (1, KT), 1)
        tri = row_in >= lax.broadcasted_iota(jnp.int32, (ROWS, 128), 1)

        def place(n):
            j, u = n // 4, n % 4
            return j, u // 2, j * GROUP + (u % 2) * 4

        def key_rows(j, e, kt):
            return j, pl.ds(pl.multiple_of(128 + e * 128 + kt * KT, 128), KT)

        def weave(current, following):
            if following is not None:
                n, scores, peaks = following
                j, e, base = place(n)
                threshold = jnp.where(e == 0, firsts[0], firsts[1]) * 128
                q = qbuf[e, pl.ds(base, 4)].reshape(ROWS, HD)
                peak = None
            if current is not None:
                cn, cscores, cpeaks = current
                cj, ce, cbase = place(cn)
                total = None
                parts = None
            for kt in range(WINDOW // KT):
                if following is not None:
                    rows = key_rows(j, e, kt)
                    s = lax.dot_general(
                        q, kvbuf[rows[0], rows[1], 0:HD], (((1,), (1,)), ((), ())), preferred_element_type=jnp.float32)
                if current is not None:
                    weights = [
                        jnp.exp2((cscores[:, kt * KT + i * 128:kt * KT + (i + 1) * 128] - cpeaks[...]) * factor)
                        for i in range(KT // 128)
                    ]
                    rows = key_rows(cj, ce, kt)
                    product = jnp.dot(
                        jnp.concatenate(weights, axis=1).astype(jnp.bfloat16),
                        kvbuf[rows[0], rows[1], HD:2 * HD], preferred_element_type=jnp.float32)
                    total = product if total is None else total + product
                    while len(weights) > 1:
                        weights = [a + b for a, b in zip(weights[::2], weights[1::2])]
                    parts = weights[0] if parts is None else parts + weights[0]
                if following is not None:
                    s = s + jnp.where(lane + kt * KT >= threshold, 0.0, NEG)
                    pieces = [s[:, i * 128:(i + 1) * 128] for i in range(KT // 128)]
                    if kt == WINDOW // KT - 1:
                        pieces[-1] = jnp.where(tri, pieces[-1], NEG)
                    for i, piece in enumerate(pieces):
                        scores[:, kt * KT + i * 128:kt * KT + (i + 1) * 128] = piece
                    while len(pieces) > 1:
                        pieces = [jnp.maximum(a, b) for a, b in zip(pieces[::2], pieces[1::2])]
                    peak = pieces[0] if peak is None else jnp.maximum(peak, pieces[0])
            if following is not None:
                peaks[...] = jnp.broadcast_to(jnp.max(peak, axis=1, keepdims=True), (ROWS, 128))
            if current is not None:
                live = jnp.where(ce == 0, lives[0], lives[1])
                mixed = total / jnp.sum(parts, axis=1, keepdims=True)
                mixed = jnp.where(row_in < live, mixed, 0.0).astype(jnp.bfloat16)
                obuf[ce, pl.ds(cbase, 4)] = mixed.reshape(4, BLOCK, HD)
                for i in range(4):
                    columns = out_hbm.at[:, pl.ds(pl.multiple_of((core * 32 + cbase + i) * HD, HD), HD)]

                    @pl.when(ce == core)
                    def _(i=i, columns=columns):
                        pltpu.make_async_copy(obuf.at[ce, cbase + i], columns, out_sem.at[0]).start()

                    @pl.when(ce != core)
                    def _(i=i, columns=columns):
                        remote(obuf.at[ce, cbase + i], columns, send_sem.at[12], out_sem.at[1], sibling).start()

        weave(None, (jnp.int32(0), sbuf, peak0))

        def pair(i, carry):
            j = i // 2
            weave((2 * i, sbuf, peak0), (2 * i + 1, sbuf1, peak1))

            @pl.when(i == 0)
            def _():
                inject_far(1)
                inject(2)
                own(3)
                own_along_y(3)

            @pl.when(i == 1)
            def _():
                inject_far(2)
                inject(3)
                rest(1)

            @pl.when(i == 2)
            def _():
                inject_far(3)

            @pl.when(i == 3)
            def _():
                rest(2)

            @pl.when(i == 5)
            def _():
                rest(3)

            @pl.when(i == 6)
            def _():
                finish_own()

            weave((2 * i + 1, sbuf1, peak1), (2 * i + 2, sbuf, peak0))

            @pl.when(i < HALF - 1)
            def _():
                forward(i + 1)

            return carry

        lax.fori_loop(0, 7, pair, 0)
        weave((jnp.int32(14), sbuf, peak0), (jnp.int32(15), sbuf1, peak1))
        finish_pair()
        weave((jnp.int32(15), sbuf1, peak1), None)

        span = kvbuf.at[:, 0:256, :]

        def sent(kind, condition):
            @pl.when(condition)
            def _():
                await_bytes(span, send_sem.at[kind])

        sent(0, x < 3)
        sent(1, jnp.logical_and(x >= 1, x < 3))
        sent(2, y < 3)
        sent(3, y == 0)
        sent(4, x >= 1)
        sent(5, x >= 1)
        sent(6, jnp.logical_and(x >= 2, y == 3))
        sent(7, jnp.logical_and(x >= 2, y > 0))
        sent(8, chip >= right_fwd)
        sent(9, chip >= left_fwd)
        await_bytes(kvbuf.at[:, 0:128, :], send_sem.at[10])
        await_bytes(qbuf.at[0], send_sem.at[11])
        await_bytes(obuf.at[0], send_sem.at[12])
        await_bytes(obuf.at[0], out_sem.at[0])
        await_many(qd, dout.at[1])
        await_many(dr, dout.at[2])
        await_bytes(cs, dout.at[3])
        await_bytes(obuf.at[0], out_sem.at[1])
        finish_wait()

    @pl.when(role >= PG)
    def _():
        group = role - PG
        pltpu.make_async_copy(raw_q, vq, own_sem.at[0]).wait()
        pltpu.make_async_copy(vkv, vkv, own_sem.at[1]).wait()
        for t in range(4):
            tall[0, 4 * t:4 * t + 4, :] = vq[t].astype(jnp.float32)
            tall[1, 4 * t:4 * t + 4, :] = vkv[t].astype(jnp.float32)
        to = lax.broadcasted_iota(jnp.int32, (32, 16), 0)
        at = lax.broadcasted_iota(jnp.int32, (32, 16), 1)
        ordered = jnp.zeros((32, HD), jnp.float32)
        for h in range(2):
            chosen = jnp.logical_and((to & 7) // 4 == h, at == (to & 3) * 4 + to // 8).astype(jnp.bfloat16)
            ordered = ordered + jnp.dot(
                chosen, tall[0, :, h * HD:(h + 1) * HD].astype(jnp.bfloat16), preferred_element_type=jnp.float32)
        dq[...] = ordered.reshape(PG, 8, HD)
        for p in range(PG):
            remote(dq.at[p], qz.at[group], dout.at[0], din.at[0], line(p)).start()
        pltpu.make_async_copy(w_hbm, wbuf, dlocal.at[0]).wait()
        await_bytes(dz, din.at[3])
        step = lax.broadcasted_iota(jnp.int32, (8, HD), 0) & 3
        to = lax.broadcasted_iota(jnp.int32, (32, 16), 0)
        at = lax.broadcasted_iota(jnp.int32, (32, 16), 1)
        chosen = jnp.logical_and((to & 7) < 4, at == (to & 3) * 4 + to // 8).astype(jnp.bfloat16)
        new_rows = [
            jnp.dot(
                chosen, tall[1, :, i * HD:(i + 1) * HD].astype(jnp.bfloat16), preferred_element_type=jnp.float32
            ).reshape(PG, 8, HD)
            for i in range(2)
        ]
        tiles = []
        for p in range(PG):
            pair = dz[p, 1]
            m = jnp.broadcast_to(pair[:, 0:1], (8, HD))
            part = jnp.broadcast_to(pair[:, 64:65], (8, HD))
            q = dq[p]
            scores = []
            for t in range(4):
                s = jnp.sum(q * new_rows[0][p, t:t + 1, :], axis=1, keepdims=True)
                scores.append(jnp.where(step >= t, jnp.broadcast_to(s, (8, HD)), NEG))
            top = m
            for s in scores:
                top = jnp.maximum(top, s)
            old = jnp.exp2((m - top) * factor)
            total = part * old
            mixed = dz[p, 0] * old
            for t in range(4):
                w = jnp.exp2((scores[t] - top) * factor)
                total = total + w
                mixed = mixed + w * new_rows[1][p, t:t + 1, :]
            tiles.append(mixed / total)
        rows = jnp.concatenate(tiles, axis=0).astype(jnp.bfloat16)
        to = lax.broadcasted_iota(jnp.int32, (16, 32), 0)
        at = lax.broadcasted_iota(jnp.int32, (16, 32), 1)
        halves = []
        for h in range(2):
            chosen = (at == (to // 4) * 8 + h * 4 + to % 4).astype(jnp.bfloat16)
            halves.append(jnp.dot(chosen, rows, preferred_element_type=jnp.float32).astype(jnp.bfloat16))
        attended = jnp.concatenate(halves, axis=1)

        def project(i, carry):
            others = [(seq + 4 * i + d) % 32 for d in range(4)]
            for other in others:
                columns = pl.ds(pl.multiple_of(other * 256, 256), 256)
                rs_s[other] = jnp.dot(
                    attended, wbuf[:, columns], preferred_element_type=jnp.float32).astype(jnp.bfloat16)
            for other in others:
                @pl.when(other != seq)
                def _(other=other):
                    remote(rs_s.at[other], rs_r.at[seq], dout.at[4], din.at[4], plane(other)).start()

            return carry

        lax.fori_loop(0, 8, project, 0)
        rs_r[seq] = rs_s[seq]
        await_bytes(rs_r.at[0:31], din.at[4])

        def add(i, total):
            four = [rs_r[4 * i + d].astype(jnp.float32) for d in range(4)]
            return total + ((four[0] + four[1]) + (four[2] + four[3]))

        summed = lax.fori_loop(0, 8, add, jnp.zeros((16, 256), jnp.float32))
        fz[group] = summed.astype(jnp.bfloat16)
        for d in range(1, 2 * PG):
            remote(fz.at[group], fz.at[group], dout.at[5], din.at[5], line((role + d) % (2 * PG))).start()
        finish_own()
        finish_pair()
        await_bytes(qz, dout.at[0])
        await_bytes(rs_s.at[0:31], dout.at[4])
        await_bytes(fz.at[0:7], dout.at[5])
        for i in range(8):
            pltpu.make_async_copy(zbuf, out_hbm.at[:, i * 1024:(i + 1) * 1024], fill_sem.at[i]).wait()
        finish_wait()


def fused(prompt_lengths, decode_group, queries, kv, dq, fresh, out_weight):
    smem = pl.BlockSpec(memory_space=pltpu.SMEM)
    hbm = pl.BlockSpec(memory_space=pl.ANY)
    return pl.pallas_call(
        fused_kernel,
        out_shape=[
            jax.ShapeDtypeStruct((BLOCK, H * HD), jnp.bfloat16),
            jax.ShapeDtypeStruct((16, 2, 4, PG, PG, 256), jnp.bfloat16),
        ],
        in_specs=[smem, smem, hbm, hbm, hbm, hbm, hbm],
        out_specs=[hbm, hbm],
        scratch_shapes=[
            pltpu.VMEM((2, 32, BLOCK, HD), jnp.bfloat16),
            pltpu.VMEM((HALF, SLOTS * 256, 256), jnp.bfloat16),
            pltpu.VMEM((ROWS, WINDOW), jnp.float32),
            pltpu.VMEM((ROWS, WINDOW), jnp.float32),
            pltpu.VMEM((ROWS, 128), jnp.float32),
            pltpu.VMEM((ROWS, 128), jnp.float32),
            pltpu.VMEM((2, 32, BLOCK, HD), jnp.bfloat16),
            pltpu.VMEM((BLOCK, 1024), jnp.bfloat16),
            pltpu.VMEM((256, 8192), jnp.bfloat16),
            pltpu.VMEM((4, PG, 256), jnp.bfloat16),
            pltpu.VMEM((4, PG, 256), jnp.bfloat16),
            pltpu.VMEM((2, 4 * PG, 256), jnp.float32),
            pltpu.VMEM((PG, 8, HD), jnp.float32),
            pltpu.VMEM((PG, 8, HD), jnp.float32),
            pltpu.VMEM((32, HD), jnp.bfloat16),
            pltpu.VMEM((16, 32, HD), jnp.bfloat16),
            pltpu.VMEM((16, 3, 8, HD), jnp.float32),
            pltpu.VMEM((16, 3, 8, HD), jnp.float32),
            pltpu.VMEM((PG, 2, 8, HD), jnp.float32),
            pltpu.VMEM((PG, 2, 8, HD), jnp.float32),
            pltpu.VMEM((32, 16, 256), jnp.bfloat16),
            pltpu.VMEM((32, 16, 256), jnp.bfloat16),
            pltpu.VMEM((8, 16, 256), jnp.bfloat16),
            pltpu.VMEM((4, PG, PG, 256), jnp.bfloat16),
            pltpu.SemaphoreType.DMA((SLOTS, HALF)),
            pltpu.SemaphoreType.DMA((2,)),
            pltpu.SemaphoreType.DMA((HALF,)),
            pltpu.SemaphoreType.DMA((2,)),
            pltpu.SemaphoreType.DMA((8,)),
            pltpu.SemaphoreType.DMA((13,)),
            pltpu.SemaphoreType.DMA((8,)),
            pltpu.SemaphoreType.DMA((8,)),
            pltpu.SemaphoreType.DMA((2,)),
        ],
        compiler_params=pltpu.CompilerParams(
            collective_id=0, has_side_effects=True, vmem_limit_bytes=62 * 1024 * 1024
        ),
        cost_estimate=pl.CostEstimate(flops=17_000_000_000, bytes_accessed=16_000_000, transcendentals=17_000_000),
    )(prompt_lengths, decode_group, queries, kv, dq, fresh, out_weight)


def on_device(prefill_queries, prefill_kv, prompt_lengths, decode_group, decode_queries, decode_kv, out_weight):
    prefill_out, decode_out = fused(
        prompt_lengths, decode_group, prefill_queries[0], prefill_kv[0], decode_queries[0], decode_kv[0], out_weight
    )
    decode_out = decode_out.reshape(32, 4, PG, PG, 256).transpose(1, 2, 3, 0, 4).reshape(4, PG, PG, -1)
    return prefill_out[None], decode_out


def solution(mesh):
    in_specs = (
        P("role", "seq", None),
        P("role", "seq", None),
        P(),
        P(),
        P("role", None, None, "seq"),
        P("role", None, None, None),
        P("seq", None),
    )
    out_specs = (P("role", "seq", None), P())
    return jax.shard_map(on_device, mesh=mesh, in_specs=in_specs, out_specs=out_specs, check_vma=False)
```
